32 devices in a mesh: row: 8 (over z, core), col: 4 (over y, x).
Axes of the slice: x: 2, y: 2, z: 4, core: 2. Of those that a mesh axis runs over, the one named last changes fastest.
Arguments:
- patches: bfloat16 [256, 256, 256], P('row', 'col'), may hold values from -6 to 6
- norm_gain: float32 [256], replicated, may hold values from 0.1 to 1.9
- w_first: bfloat16 [2, 4, 64, 64], replicated, may hold values from -0.5 to 0.5
- w_second: bfloat16 [2, 4, 64, 64], replicated, may hold values from -0.5 to 0.5
- depth_kernel: float32 [3, 3, 256], replicated, may hold values from -2 to 2
Outputs:
- mixed: bfloat16 [256, 256, 256], P('row', 'col')
The draws below stay inside these ranges and needn't reach their ends.
All inputs are finite; a program needn't handle non-finite values.
Results may differ from the reference program's by a relative error of at most 0.008.
Values may be sent and summed in bfloat16 or wider, within the bound.
A program may use at most 64 MiB of HBM per device.

```python
import math
import jax
import jax.numpy as jnp
from jax import lax

BLOCK = 64
BLOCKS = 4
CH = 256
GRID_H = 256
GRID_W = 256


def level_of(rng, extent, split, low, top_value):
    level, own = 1.0, jax.random.fold_in(rng, 6)
    for position, shards_of in split:
        draws = jnp.exp(jax.random.uniform(jax.random.fold_in(own, position), (shards_of,), jnp.float32, low / len(split), top_value / len(split)))
        level = level * jnp.repeat(draws, extent[position] // shards_of).reshape([-1 if axis == position else 1 for axis in range(len(extent))])
    return level


def noise(stream_key, extent, scale, reach, pieces=(), kind=jnp.bfloat16):
    gain = level_of(stream_key, extent, pieces, -0.22, 0.18) if pieces else 1.0
    entries = jax.random.normal(stream_key, extent, jnp.float32) * scale * gain
    return jnp.minimum(jnp.maximum(entries, -reach), reach).astype(kind)


def setup_inputs(seed: int = 0) -> dict:
    key_of = jax.random.split(jax.random.key(seed), 6)
    return {
        "patches": noise(key_of[0], (GRID_H, GRID_W, CH), 1.0, 6.0, ((0, 8), (1, 4))),
        "norm_gain": jnp.clip(1.0 + 0.18 * jax.random.normal(key_of[1], (CH,), jnp.float32), 0.1, 1.9),
        "w_first": noise(key_of[2], (2, BLOCKS, BLOCK, BLOCK), (2 * BLOCK) ** -0.5, 0.5),
        "w_second": noise(key_of[3], (2, BLOCKS, BLOCK, BLOCK), (2 * BLOCK) ** -0.5, 0.5),
        "depth_kernel": noise(key_of[4], (3, 3, CH), 9 ** -0.5, 2.0, (), jnp.float32),
    }


def phase_table(first_idx, second_idx, length):
    product = first_idx[:, None] * second_idx[None, :] % length
    phase = product.astype(jnp.float32) * (2.0 * math.pi / length)
    return (jnp.cos(phase).astype(jnp.bfloat16), jnp.sin(phase).astype(jnp.bfloat16))

def shrink(values):
    level = 0.25
    return jnp.where(values > level, values - level, jnp.where(values < -level, values + level, 0.0 * values))

def reference(patches, norm_gain, w_first, w_second, depth_kernel):
    patch_grid_height, grid_w, chans = patches.shape
    half = grid_w // 2
    xf = patches.astype(jnp.float32)
    mean = lax.optimization_barrier(jnp.mean(xf, axis=-1, keepdims=True))
    var = lax.optimization_barrier(jnp.mean((xf - mean) ** 2, axis=-1, keepdims=True))
    normed = ((xf - mean) * lax.rsqrt(var + 1e-05) * norm_gain).astype(jnp.bfloat16)
    cos_w, sin_w = phase_table(jnp.arange(grid_w, dtype=jnp.int32), jnp.arange(half, dtype=jnp.int32), grid_w)
    cos_h, sin_h = phase_table(jnp.arange(patch_grid_height, dtype=jnp.int32), jnp.arange(patch_grid_height, dtype=jnp.int32), patch_grid_height)
    cosine_width_factor, sine_width_factor = (cos_w.astype(jnp.float32), sin_w.astype(jnp.float32))
    cosine_height_factor, sine_height_factor = (cos_h.astype(jnp.float32), sin_h.astype(jnp.float32))
    filter_coefficient = jnp.where(jnp.arange(half) == 0, 1.0, 2.0).astype(jnp.float32)
    width_factors = 1.0 / math.sqrt(grid_w)
    height_factors = 1.0 / math.sqrt(patch_grid_height)
    blocks = w_first.shape[1]
    width = w_first.shape[2]
    normed_blocks = normed.reshape(patch_grid_height, grid_w, blocks, width).transpose(2, 0, 1, 3)
    first_b = w_first.transpose(1, 0, 2, 3)
    second_b = w_second.transpose(1, 0, 2, 3)

    def one_block(packed):
        block, wa, wb = packed
        nb = block.astype(jnp.float32)
        wre = (jnp.einsum('hwc,wk->hkc', nb, cosine_width_factor) * width_factors).astype(jnp.bfloat16).astype(jnp.float32)
        wim = (-jnp.einsum('hwc,wk->hkc', nb, sine_width_factor) * width_factors).astype(jnp.bfloat16).astype(jnp.float32)
        zre = (height_factors * (jnp.einsum('qh,hkc->qkc', cosine_height_factor, wre) + jnp.einsum('qh,hkc->qkc', sine_height_factor, wim))).astype(jnp.bfloat16).astype(jnp.float32)
        zim = (height_factors * (jnp.einsum('qh,hkc->qkc', cosine_height_factor, wim) - jnp.einsum('qh,hkc->qkc', sine_height_factor, wre))).astype(jnp.bfloat16).astype(jnp.float32)
        a0, a1 = (wa[0].astype(jnp.float32), wa[1].astype(jnp.float32))
        b0, b1 = (wb[0].astype(jnp.float32), wb[1].astype(jnp.float32))
        hre = jnp.tanh(jnp.einsum('qkc,cd->qkd', zre, a0) - jnp.einsum('qkc,cd->qkd', zim, a1)).astype(jnp.bfloat16).astype(jnp.float32)
        him = jnp.tanh(jnp.einsum('qkc,cd->qkd', zre, a1) + jnp.einsum('qkc,cd->qkd', zim, a0)).astype(jnp.bfloat16).astype(jnp.float32)
        spectrum_real = shrink(jnp.einsum('qkc,cd->qkd', hre, b0) - jnp.einsum('qkc,cd->qkd', him, b1)).astype(jnp.bfloat16).astype(jnp.float32)
        spectrum_imaginary = shrink(jnp.einsum('qkc,cd->qkd', hre, b1) + jnp.einsum('qkc,cd->qkd', him, b0)).astype(jnp.bfloat16).astype(jnp.float32)
        value_real = (height_factors * (jnp.einsum('eu,ear->uar', cosine_height_factor, spectrum_real) - jnp.einsum('eu,ear->uar', sine_height_factor, spectrum_imaginary))).astype(jnp.bfloat16).astype(jnp.float32)
        value_imaginary = (height_factors * (jnp.einsum('eu,ear->uar', cosine_height_factor, spectrum_imaginary) + jnp.einsum('eu,ear->uar', sine_height_factor, spectrum_real))).astype(jnp.bfloat16).astype(jnp.float32)
        spectrum_values = width_factors * (jnp.einsum('osl,xs->oxl', value_real, cosine_width_factor * filter_coefficient) - jnp.einsum('osl,xs->oxl', value_imaginary, sine_width_factor * filter_coefficient))
        return spectrum_values.astype(jnp.bfloat16)
    spectral = lax.map(one_block, (normed_blocks, first_b, second_b))
    spectral = spectral.transpose(1, 2, 0, 3).reshape(patch_grid_height, grid_w, chans)
    nf = normed.astype(jnp.float32)
    conv = jnp.zeros((patch_grid_height, grid_w, chans), jnp.float32)
    for i in range(3):
        for j in range(3):
            conv = conv + jnp.roll(nf, (1 - i, 1 - j), axis=(0, 1)) * depth_kernel[i, j]
    return (xf + spectral.astype(jnp.float32) + conv).astype(jnp.bfloat16)
```

```python
import functools
import math

import jax
import jax.numpy as jnp
import ml_dtypes
import numpy as np
from jax import lax
from jax.experimental import pallas as pl
from jax.experimental.pallas import tpu as pltpu
from jax.sharding import PartitionSpec as P


def with_halo(shard, sides, width):
    for axis, dim in sides:
        devices, length = (lax.axis_size(axis), shard.shape[dim])
        up = [(i, (i + 1) % devices) for i in range(devices)]
        down = [(j, i) for i, j in up]
        last = lax.slice_in_dim(shard, length - width, length, axis=dim)
        leading = lax.slice_in_dim(shard, 0, width, axis=dim)
        before = lax.ppermute(last, axis, up)
        after = lax.ppermute(leading, axis, down)
        shard = jnp.concatenate([before, shard, after], axis=dim)
    return shard


def phase_table(first_idx, second_idx, length):
    product = first_idx[:, None] * second_idx[None, :] % length
    phase = product.astype(jnp.float32) * (2.0 * math.pi / length)
    return (jnp.cos(phase).astype(jnp.bfloat16), jnp.sin(phase).astype(jnp.bfloat16))


def shrink(values):
    level = 0.25
    return jnp.where(
        values > level, values - level, jnp.where(values < -level, values + level, 0.0 * values)
    )


def block_product(left, weight):
    return jnp.einsum("qmbc,bcd->qmbd", left, weight, preferred_element_type=jnp.float32)


def general(patches, norm_gain, w_first, w_second, depth_kernel):
    n_row = lax.axis_size("row")
    n_col = lax.axis_size("col")
    rows_dev, cols_dev, chans = patches.shape
    patch_grid_height = rows_dev * n_row
    grid_w = cols_dev * n_col
    half = grid_w // 2
    blocks = w_first.shape[1]
    width = w_first.shape[2]
    width_factors = 1.0 / math.sqrt(grid_w)
    height_factors = 1.0 / math.sqrt(patch_grid_height)
    xf = patches.astype(jnp.float32)
    mean = jnp.mean(xf, axis=-1, keepdims=True)
    var = jnp.mean((xf - mean) ** 2, axis=-1, keepdims=True)
    normed = ((xf - mean) * lax.rsqrt(var + 1e-05) * norm_gain).astype(jnp.bfloat16)
    padded = with_halo(normed, (("row", 0), ("col", 1)), 1)
    conv = jnp.zeros((rows_dev, cols_dev, chans), jnp.float32)
    for i in range(3):
        for j in range(3):
            conv = conv + padded[i : i + rows_dev, j : j + cols_dev] * depth_kernel[i, j]
    strips = lax.all_to_all(normed, "col", split_axis=0, concat_axis=1, tiled=True)
    cos_w, sin_w = phase_table(
        jnp.arange(grid_w, dtype=jnp.int32), jnp.arange(half, dtype=jnp.int32), grid_w
    )
    forward_w = jnp.concatenate([cos_w, -sin_w], axis=1)
    spectrum_values = jnp.einsum(
        "hwc,wk->hkc", strips, forward_w, preferred_element_type=jnp.float32
    )
    spectrum_values = (spectrum_values * width_factors).astype(jnp.bfloat16)
    wre = spectrum_values[:, :half]
    wim = spectrum_values[:, half:]
    positions = jnp.arange(patch_grid_height, dtype=jnp.int32)
    across_re, across_im = (
        lax.all_to_all(wre, "col", split_axis=1, concat_axis=0, tiled=True),
        lax.all_to_all(wim, "col", split_axis=1, concat_axis=0, tiled=True),
    )
    full_re, full_im = (
        lax.all_to_all(across_re, "row", split_axis=1, concat_axis=0, tiled=True),
        lax.all_to_all(across_im, "row", split_axis=1, concat_axis=0, tiled=True),
    )
    cos_h, sin_h = phase_table(positions, positions, patch_grid_height)
    big_table = jnp.concatenate(
        [jnp.concatenate([cos_h, sin_h], axis=1), jnp.concatenate([-sin_h, cos_h], axis=1)], axis=0
    )
    stacked = jnp.concatenate([full_re, full_im], axis=0)
    spectrum = jnp.einsum("qp,pmc->qmc", big_table, stacked, preferred_element_type=jnp.float32)
    spectrum = (spectrum * height_factors).astype(jnp.bfloat16)
    modes = spectrum.shape[1]
    zre = spectrum[:patch_grid_height].reshape(patch_grid_height, modes, blocks, width)
    zim = spectrum[patch_grid_height:].reshape(patch_grid_height, modes, blocks, width)
    hre = jnp.tanh(block_product(zre, w_first[0]) - block_product(zim, w_first[1])).astype(
        jnp.bfloat16
    )
    him = jnp.tanh(block_product(zre, w_first[1]) + block_product(zim, w_first[0])).astype(
        jnp.bfloat16
    )
    spectrum_real = shrink(
        block_product(hre, w_second[0]) - block_product(him, w_second[1])
    ).astype(jnp.bfloat16)
    spectrum_imaginary = shrink(
        block_product(hre, w_second[1]) + block_product(him, w_second[0])
    ).astype(jnp.bfloat16)
    filtered = jnp.concatenate(
        [
            spectrum_real.reshape(patch_grid_height, modes, chans),
            spectrum_imaginary.reshape(patch_grid_height, modes, chans),
        ],
        axis=0,
    )
    inverse_transform = jnp.einsum(
        "qp,qmc->pmc", big_table, filtered, preferred_element_type=jnp.float32
    )
    inverse_transform = (inverse_transform * height_factors).astype(jnp.bfloat16)
    value_real = inverse_transform[:patch_grid_height]
    value_imaginary = inverse_transform[patch_grid_height:]
    part_re, part_im = (
        lax.all_to_all(value_real, "row", split_axis=0, concat_axis=1, tiled=True),
        lax.all_to_all(value_imaginary, "row", split_axis=0, concat_axis=1, tiled=True),
    )
    line_re, line_im = (
        lax.all_to_all(part_re, "col", split_axis=0, concat_axis=1, tiled=True),
        lax.all_to_all(part_im, "col", split_axis=0, concat_axis=1, tiled=True),
    )
    filter_coefficient = jnp.where(jnp.arange(half) == 0, 1.0, 2.0).astype(jnp.float32)
    inverse_w = jnp.concatenate(
        [
            (cos_w.astype(jnp.float32) * filter_coefficient).T,
            -(sin_w.astype(jnp.float32) * filter_coefficient).T,
        ],
        axis=0,
    ).astype(jnp.bfloat16)
    lines = jnp.concatenate([line_re, line_im], axis=1)
    spectral = jnp.einsum("hkc,kw->hwc", lines, inverse_w, preferred_element_type=jnp.float32)
    spectral = (spectral * width_factors).astype(jnp.bfloat16)
    home = lax.all_to_all(spectral, "col", split_axis=1, concat_axis=0, tiled=True)
    return (xf + home.astype(jnp.float32) + conv).astype(jnp.bfloat16)


LANES = 128
PAIR = 64
TILE = 16
COL_CHUNKS = 4
KGROUPS = 2


def row_order(n_row, rows_dev):
    pairs = rows_dev // 2
    zc = rows_dev // TILE
    per = pairs // zc
    order = []
    for z in range(zc):
        for s in range(n_row):
            for slot in range(TILE):
                order.append(s * rows_dev + (slot // per) * pairs + z * per + slot % per)
    return np.array(order)


def host_tables(grid_h, grid_w, n_row, rows_dev):
    half = grid_w // 2

    def table(a, b, n):
        phase = (np.outer(a, b) % n).astype(np.float32) * np.float32(2.0 * math.pi / n)
        bf16 = ml_dtypes.bfloat16
        cos, sin = (np.cos(phase).astype(bf16), np.sin(phase).astype(bf16))
        return cos.astype(np.float32), sin.astype(np.float32)

    cos_w, sin_w = table(np.arange(half), np.arange(grid_w), grid_w)
    weight = np.where(np.arange(half) == 0, 1.0, 2.0).astype(np.float32)[:, None]
    forward = np.concatenate([cos_w, -sin_w], axis=0)
    inverse = np.concatenate([cos_w * weight, -sin_w * weight], axis=0).T
    order = row_order(n_row, rows_dev)
    cos_h, sin_h = table(order, order, grid_h)
    swap = np.zeros((TILE, TILE, TILE, TILE), np.float32)
    for a in range(TILE):
        for b in range(TILE):
            swap[a, b, b, a] = 1.0
    cast = lambda v: v.astype(ml_dtypes.bfloat16)
    return (
        cast(forward),
        cast(inverse),
        cast(np.concatenate([cos_h, sin_h], axis=0)),
        cast(swap.reshape(TILE * TILE, TILE * TILE)),
    )


def half_turn(x):
    return pltpu.roll(x, PAIR, x.ndim - 1)


def low_lanes(shape):
    return lax.broadcasted_iota(jnp.int32, shape, len(shape) - 1) < PAIR


def swap_halves(a, b):
    low = low_lanes(a.shape)
    return jnp.where(low, a, half_turn(b)), jnp.where(low, half_turn(a), b)


def mixing_kernel(
    n_row,
    n_col,
    scale_w,
    scale_h,
    patches,
    gain,
    w_first,
    w_second,
    depth,
    forward_ref,
    inverse_ref,
    height_ref,
    swap_ref,
    out,
    send1,
    recv1,
    turned,
    send2,
    recv2,
    send3,
    recv3,
    send4,
    recv4,
    conv,
    rim_send,
    rim_recv,
    rim,
    s1,
    r1,
    s2,
    r2,
    s3,
    r3,
    s4,
    r4,
    sh,
    rh,
):
    f32, bf16 = jnp.float32, jnp.bfloat16
    row, col = lax.axis_index("row"), lax.axis_index("col")
    rows_dev, cols_dev, chans = patches.shape
    pairs = rows_dev // 2
    per_col = pairs // COL_CHUNKS
    zc = rows_dev // TILE
    per_z = pairs // zc
    col_per_z = COL_CHUNKS // zc
    grid_w = cols_dev * n_col
    half = grid_w // 2
    kl = half // n_row
    per_k = kl // KGROUPS
    groups = chans // LANES

    def col_peer(d):
        return lax.rem(col + d, n_col)

    def row_peer(d):
        return lax.rem(row + d, n_row)

    def to_col(d):
        return {"col": col_peer(d)}

    def to_row(d):
        return {"row": row_peer(d)}

    def dot(a, b):
        return jnp.dot(a, b, preferred_element_type=f32)

    barrier = pltpu.get_barrier_semaphore()
    for d in range(1, n_col):
        pl.semaphore_signal(barrier, inc=1, device_id=to_col(d), device_id_type=pl.DeviceIdType.MESH)
    for d in range(1, n_row):
        pl.semaphore_signal(barrier, inc=1, device_id=to_row(d), device_id_type=pl.DeviceIdType.MESH)

    def copy1(ch, d):
        return pltpu.make_async_remote_copy(
            src_ref=send1.at[ch, col_peer(d)],
            dst_ref=recv1.at[ch, col],
            send_sem=s1.at[ch, d - 1],
            recv_sem=r1.at[ch, d - 1],
            device_id=to_col(d),
            device_id_type=pl.DeviceIdType.MESH,
        )

    def copy2(z, g, d):
        ks = pl.ds(g * per_k, per_k)
        return pltpu.make_async_remote_copy(
            src_ref=send2.at[z, row_peer(d), ks],
            dst_ref=recv2.at[z, row, ks],
            send_sem=s2.at[z, g, d - 1],
            recv_sem=r2.at[z, g, d - 1],
            device_id=to_row(d),
            device_id_type=pl.DeviceIdType.MESH,
        )

    def copy3(z, g, d):
        ks = pl.ds(g * per_k, per_k)
        return pltpu.make_async_remote_copy(
            src_ref=send3.at[z, row_peer(d), ks],
            dst_ref=recv3.at[z, row, ks],
            send_sem=s3.at[z, g, d - 1],
            recv_sem=r3.at[z, g, d - 1],
            device_id=to_row(d),
            device_id_type=pl.DeviceIdType.MESH,
        )

    def copy4(ch, d):
        return pltpu.make_async_remote_copy(
            src_ref=send4.at[ch, col_peer(d)],
            dst_ref=recv4.at[ch, col],
            send_sem=s4.at[ch, d - 1],
            recv_sem=r4.at[ch, d - 1],
            device_id=to_col(d),
            device_id_type=pl.DeviceIdType.MESH,
        )

    def copy_rim(side):
        return pltpu.make_async_remote_copy(
            src_ref=rim_send.at[side],
            dst_ref=rim_recv.at[side],
            send_sem=sh.at[side],
            recv_sem=rh.at[side],
            device_id=to_row(1 if side == 0 else n_row - 1),
            device_id_type=pl.DeviceIdType.MESH,
        )

    def normed_row(h):
        x = patches[h].astype(f32)
        mean = jnp.mean(x, axis=-1, keepdims=True)
        centred = x - mean
        var = jnp.mean(centred * centred, axis=-1, keepdims=True)
        return centred * lax.rsqrt(var + 1e-05) * gain[...]

    for ch in range(COL_CHUNKS):

        def norm_pair(i, carry, ch=ch):
            hp = ch * per_col + i
            lower, upper = normed_row(hp), normed_row(hp + pairs)
            for j in range(groups):
                lanes = slice(j * LANES, (j + 1) * LANES)
                even, odd = swap_halves(lower[:, lanes], upper[:, lanes])
                send1[ch, 2 * j, i] = even.astype(bf16)
                send1[ch, 2 * j + 1, i] = odd.astype(bf16)
            return carry

        lax.fori_loop(0, per_col, norm_pair, 0)
        if ch == 0:
            pl.semaphore_wait(barrier, n_col + n_row - 2)
        for d in range(1, n_col):
            copy1(ch, d).start()
        recv1[ch, col] = send1[ch, col]

    def line(ch, i):
        return recv1[ch, :, i].reshape(grid_w, LANES)

    for z in range(zc):
        for ch in range(z * col_per_z, (z + 1) * col_per_z):
            for d in range(1, n_col):
                copy1(ch, d).wait_recv()

            def width_pair(i, carry, ch=ch, z=z):
                y = dot(forward_ref[...], line(ch, i)) * scale_w
                lower, upper = swap_halves(y[:half], y[half:])
                slot = (ch - z * col_per_z) * per_col + i
                turned[slot] = lower.astype(bf16)
                turned[per_z + slot] = upper.astype(bf16)
                return carry

            lax.fori_loop(0, per_col, width_pair, 0)

        def turn_out(r, carry, z=z):
            ks = pl.ds(pl.multiple_of(r * kl, kl), kl)
            tile = turned[:, ks, :].reshape(TILE * kl, LANES)
            send2[z, r] = dot(swap_ref[...], tile).astype(bf16).reshape(kl, TILE, LANES)
            return carry

        lax.fori_loop(0, n_row, turn_out, 0)
        for g in range(KGROUPS):
            for d in range(1, n_row):
                copy2(z, g, d).start()
        recv2[z, row] = send2[z, row]

    first = line(0, 0).astype(f32)
    final = line(COL_CHUNKS - 1, per_col - 1).astype(f32)
    rim_send[0] = swap_halves(final[:half], final[half:])[1].astype(bf16)
    rim_send[1] = swap_halves(first[:half], first[half:])[0].astype(bf16)
    for side in range(2):
        copy_rim(side).start()

    def complex_weight(ref):
        re, im = ref[0, col].astype(f32), ref[1, col].astype(f32)
        return jnp.concatenate(
            [jnp.concatenate([re, im], axis=1), jnp.concatenate([-im, re], axis=1)], axis=0
        ).astype(bf16)

    weight_a, weight_b = complex_weight(w_first), complex_weight(w_second)

    lane_group = pl.multiple_of((col // 2) * LANES, LANES)
    own = depth[:, pl.ds(lane_group, LANES)]
    low = low_lanes(own.shape)
    other = half_turn(own)
    taps = jnp.where((col % 2) == 0, jnp.where(low, own, other), jnp.where(low, other, own))
    for side in range(2):
        copy_rim(side).wait_recv()
    before = rim_recv[0].astype(f32)
    after = rim_recv[1].astype(f32)
    before = jnp.concatenate([before, half_turn(before)], axis=0)
    after = jnp.concatenate([half_turn(after), after], axis=0)
    low = low_lanes(before.shape)
    rim[0] = jnp.where(low, before, half_turn(final)).astype(bf16)
    rim[1] = jnp.where(low, half_turn(first), after).astype(bf16)

    def conv_pair(hp, above, here, below):
        total = None
        for j in range(3):
            part = None
            for i, rows in enumerate((above, here, below)):
                term = rows * taps[3 * i + j : 3 * i + j + 1]
                part = term if part is None else part + term
            if j == 0:
                part = pltpu.roll(part, 1, 0)
            if j == 2:
                part = pltpu.roll(part, grid_w - 1, 0)
            total = part if total is None else total + part
        conv[hp] = total

    def at(hp):
        return line(hp // per_col, hp % per_col).astype(f32)

    conv_pair(0, rim[0].astype(f32), at(0), at(1))

    def conv_inner(hp, carry):
        conv_pair(hp, at(hp - 1), at(hp), at(hp + 1))
        return carry

    lax.fori_loop(1, pairs - 1, conv_inner, 0)
    conv_pair(pairs - 1, at(pairs - 2), at(pairs - 1), rim[1].astype(f32))

    def height(u):
        both = dot(height_ref[...], u)
        n = both.shape[0] // 2
        turned_part = half_turn(both[n:])
        return both[:n], jnp.where(low_lanes(turned_part.shape), turned_part, -turned_part)

    grid_h = rows_dev * n_row

    def filter_mode(k, carry):
        u = recv2[:, :, k].reshape(grid_h, LANES)
        a, b = height(u)
        zed = ((a + b) * scale_h).astype(bf16)
        hidden = jnp.tanh(dot(zed, weight_a)).astype(bf16)
        s = dot(hidden, weight_b)
        s = (s - jnp.clip(s, -0.25, 0.25)).astype(bf16)
        a, b = height(s)
        v = ((a - b) * scale_h).astype(bf16)
        send3[:, :, k] = v.reshape(zc, n_row, TILE, LANES)
        return carry

    for g in range(KGROUPS):
        for z in range(zc):
            for d in range(1, n_row):
                copy2(z, g, d).wait_recv()
        lax.fori_loop(g * per_k, (g + 1) * per_k, filter_mode, 0)
        for d in range(1, n_row):
            copy3(0, g, d).start()
    for z in range(1, zc):
        for g in range(KGROUPS):
            for d in range(1, n_row):
                copy3(z, g, d).start()
    for z in range(zc):
        recv3[z, row] = send3[z, row]

    for z in range(zc):
        for g in range(KGROUPS):
            for d in range(1, n_row):
                copy3(z, g, d).wait_recv()

        def turn_back(r, carry, z=z):
            tile = recv3[z, r].reshape(kl * TILE, LANES)
            ks = pl.ds(pl.multiple_of(r * kl, kl), kl)
            turned[:, ks, :] = dot(swap_ref[...], tile).astype(bf16).reshape(TILE, kl, LANES)
            return carry

        lax.fori_loop(0, n_row, turn_back, 0)
        for ch in range(z * col_per_z, (z + 1) * col_per_z):

            def inverse_pair(i, carry, ch=ch, z=z):
                slot = (ch - z * col_per_z) * per_col + i
                re, im = swap_halves(turned[slot].astype(f32), turned[per_z + slot].astype(f32))
                x = jnp.concatenate([re.astype(bf16), im.astype(bf16)], axis=0)
                cells = dot(inverse_ref[...], x) * scale_w + conv[ch * per_col + i]
                send4[ch, :, i] = cells.astype(bf16).reshape(n_col, cols_dev, LANES)
                return carry

            lax.fori_loop(0, per_col, inverse_pair, 0)
            for d in range(1, n_col):
                copy4(ch, d).start()
            recv4[ch, col] = send4[ch, col]

    for ch in range(COL_CHUNKS):
        for d in range(1, n_col):
            copy4(ch, d).wait_recv()

        def finish_pair(i, carry, ch=ch):
            hp = ch * per_col + i
            for j in range(groups):
                lanes = slice(j * LANES, (j + 1) * LANES)
                lower, upper = swap_halves(
                    recv4[ch, 2 * j, i].astype(f32), recv4[ch, 2 * j + 1, i].astype(f32)
                )
                out[hp, :, lanes] = (patches[hp, :, lanes].astype(f32) + lower).astype(bf16)
                out[hp + pairs, :, lanes] = (
                    patches[hp + pairs, :, lanes].astype(f32) + upper
                ).astype(bf16)
            return carry

        lax.fori_loop(0, per_col, finish_pair, 0)

    for ch in range(COL_CHUNKS):
        for d in range(1, n_col):
            copy1(ch, d).wait_send()
            copy4(ch, d).wait_send()
    for z in range(zc):
        for g in range(KGROUPS):
            for d in range(1, n_row):
                copy2(z, g, d).wait_send()
                copy3(z, g, d).wait_send()
    for side in range(2):
        copy_rim(side).wait_send()


def fused(patches, norm_gain, w_first, w_second, depth_kernel):
    n_row = lax.axis_size("row")
    n_col = lax.axis_size("col")
    rows_dev, cols_dev, chans = patches.shape
    grid_h, grid_w = rows_dev * n_row, cols_dev * n_col
    pairs, zc = rows_dev // 2, rows_dev // TILE
    per_col = pairs // COL_CHUNKS
    half = grid_w // 2
    kl = half // n_row
    tables = host_tables(grid_h, grid_w, n_row, rows_dev)
    bf16, f32 = jnp.bfloat16, jnp.float32
    vmem = pl.BlockSpec(memory_space=pltpu.VMEM)
    col_buffer = pltpu.VMEM((COL_CHUNKS, n_col, per_col, cols_dev, LANES), bf16)
    row_buffer = pltpu.VMEM((zc, n_row, kl, TILE, LANES), bf16)
    col_sems = pltpu.SemaphoreType.DMA((COL_CHUNKS, n_col - 1))
    row_sems = pltpu.SemaphoreType.DMA((zc, KGROUPS, n_row - 1))
    rim_sems = pltpu.SemaphoreType.DMA((2,))
    return pl.pallas_call(
        functools.partial(
            mixing_kernel, n_row, n_col, 1.0 / math.sqrt(grid_w), 1.0 / math.sqrt(grid_h)
        ),
        out_shape=jax.ShapeDtypeStruct(patches.shape, bf16),
        in_specs=[vmem] * 9,
        out_specs=vmem,
        scratch_shapes=[
            col_buffer,
            col_buffer,
            pltpu.VMEM((TILE, half, LANES), bf16),
            row_buffer,
            row_buffer,
            row_buffer,
            row_buffer,
            col_buffer,
            col_buffer,
            pltpu.VMEM((pairs, grid_w, LANES), f32),
            pltpu.VMEM((2, half, LANES), bf16),
            pltpu.VMEM((2, half, LANES), bf16),
            pltpu.VMEM((2, grid_w, LANES), bf16),
            col_sems,
            col_sems,
            row_sems,
            row_sems,
            row_sems,
            row_sems,
            col_sems,
            col_sems,
            rim_sems,
            rim_sems,
        ],
        compiler_params=pltpu.CompilerParams(
            collective_id=0, has_side_effects=True, vmem_limit_bytes=40 * 1024 * 1024
        ),
        cost_estimate=pl.CostEstimate(flops=2_000_000_000, bytes_accessed=3_000_000, transcendentals=600_000),
    )(
        patches,
        norm_gain.reshape(1, chans),
        w_first,
        w_second,
        depth_kernel.reshape(9, chans),
        *[jnp.asarray(t) for t in tables],
    )


def fits(patches, w_first):
    n_row, n_col = lax.axis_size("row"), lax.axis_size("col")
    rows_dev, cols_dev, chans = patches.shape
    blocks, width = w_first.shape[1:3]
    half = cols_dev * n_col // 2
    return (
        blocks == n_col
        and width == PAIR
        and chans % LANES == 0
        and rows_dev == 2 * TILE
        and cols_dev % TILE == 0
        and half == n_row * TILE
    )


def local(patches, norm_gain, w_first, w_second, depth_kernel):
    plan = fused if fits(patches, w_first) else general
    return plan(patches, norm_gain, w_first, w_second, depth_kernel)


def solution(mesh):
    return jax.shard_map(
        local,
        mesh=mesh,
        in_specs=(P("row", "col", None), P(), P(), P(), P()),
        out_specs=P("row", "col", None),
        check_vma=False,
    )
```

```python
import functools
import math

import jax
import jax.numpy as jnp
import ml_dtypes
import numpy as np
from jax import lax
from jax.experimental import pallas as pl
from jax.experimental.pallas import tpu as pltpu
from jax.sharding import PartitionSpec as P


def with_halo(shard, sides, width):
    for axis, dim in sides:
        devices, length = (lax.axis_size(axis), shard.shape[dim])
        up = [(i, (i + 1) % devices) for i in range(devices)]
        down = [(j, i) for i, j in up]
        last = lax.slice_in_dim(shard, length - width, length, axis=dim)
        leading = lax.slice_in_dim(shard, 0, width, axis=dim)
        before = lax.ppermute(last, axis, up)
        after = lax.ppermute(leading, axis, down)
        shard = jnp.concatenate([before, shard, after], axis=dim)
    return shard


def phase_table(first_idx, second_idx, length):
    product = first_idx[:, None] * second_idx[None, :] % length
    phase = product.astype(jnp.float32) * (2.0 * math.pi / length)
    return (jnp.cos(phase).astype(jnp.bfloat16), jnp.sin(phase).astype(jnp.bfloat16))


def shrink(values):
    level = 0.25
    return jnp.where(
        values > level, values - level, jnp.where(values < -level, values + level, 0.0 * values)
    )


def block_product(left, weight):
    return jnp.einsum("qmbc,bcd->qmbd", left, weight, preferred_element_type=jnp.float32)


def general(patches, norm_gain, w_first, w_second, depth_kernel):
    n_row = lax.axis_size("row")
    n_col = lax.axis_size("col")
    rows_dev, cols_dev, chans = patches.shape
    patch_grid_height = rows_dev * n_row
    grid_w = cols_dev * n_col
    half = grid_w // 2
    blocks = w_first.shape[1]
    width = w_first.shape[2]
    width_factors = 1.0 / math.sqrt(grid_w)
    height_factors = 1.0 / math.sqrt(patch_grid_height)
    xf = patches.astype(jnp.float32)
    mean = jnp.mean(xf, axis=-1, keepdims=True)
    var = jnp.mean((xf - mean) ** 2, axis=-1, keepdims=True)
    normed = ((xf - mean) * lax.rsqrt(var + 1e-05) * norm_gain).astype(jnp.bfloat16)
    padded = with_halo(normed, (("row", 0), ("col", 1)), 1)
    conv = jnp.zeros((rows_dev, cols_dev, chans), jnp.float32)
    for i in range(3):
        for j in range(3):
            conv = conv + padded[i : i + rows_dev, j : j + cols_dev] * depth_kernel[i, j]
    strips = lax.all_to_all(normed, "col", split_axis=0, concat_axis=1, tiled=True)
    cos_w, sin_w = phase_table(
        jnp.arange(grid_w, dtype=jnp.int32), jnp.arange(half, dtype=jnp.int32), grid_w
    )
    forward_w = jnp.concatenate([cos_w, -sin_w], axis=1)
    spectrum_values = jnp.einsum(
        "hwc,wk->hkc", strips, forward_w, preferred_element_type=jnp.float32
    )
    spectrum_values = (spectrum_values * width_factors).astype(jnp.bfloat16)
    wre = spectrum_values[:, :half]
    wim = spectrum_values[:, half:]
    positions = jnp.arange(patch_grid_height, dtype=jnp.int32)
    across_re, across_im = (
        lax.all_to_all(wre, "col", split_axis=1, concat_axis=0, tiled=True),
        lax.all_to_all(wim, "col", split_axis=1, concat_axis=0, tiled=True),
    )
    full_re, full_im = (
        lax.all_to_all(across_re, "row", split_axis=1, concat_axis=0, tiled=True),
        lax.all_to_all(across_im, "row", split_axis=1, concat_axis=0, tiled=True),
    )
    cos_h, sin_h = phase_table(positions, positions, patch_grid_height)
    big_table = jnp.concatenate(
        [jnp.concatenate([cos_h, sin_h], axis=1), jnp.concatenate([-sin_h, cos_h], axis=1)], axis=0
    )
    stacked = jnp.concatenate([full_re, full_im], axis=0)
    spectrum = jnp.einsum("qp,pmc->qmc", big_table, stacked, preferred_element_type=jnp.float32)
    spectrum = (spectrum * height_factors).astype(jnp.bfloat16)
    modes = spectrum.shape[1]
    zre = spectrum[:patch_grid_height].reshape(patch_grid_height, modes, blocks, width)
    zim = spectrum[patch_grid_height:].reshape(patch_grid_height, modes, blocks, width)
    hre = jnp.tanh(block_product(zre, w_first[0]) - block_product(zim, w_first[1])).astype(
        jnp.bfloat16
    )
    him = jnp.tanh(block_product(zre, w_first[1]) + block_product(zim, w_first[0])).astype(
        jnp.bfloat16
    )
    spectrum_real = shrink(
        block_product(hre, w_second[0]) - block_product(him, w_second[1])
    ).astype(jnp.bfloat16)
    spectrum_imaginary = shrink(
        block_product(hre, w_second[1]) + block_product(him, w_second[0])
    ).astype(jnp.bfloat16)
    filtered = jnp.concatenate(
        [
            spectrum_real.reshape(patch_grid_height, modes, chans),
            spectrum_imaginary.reshape(patch_grid_height, modes, chans),
        ],
        axis=0,
    )
    inverse_transform = jnp.einsum(
        "qp,qmc->pmc", big_table, filtered, preferred_element_type=jnp.float32
    )
    inverse_transform = (inverse_transform * height_factors).astype(jnp.bfloat16)
    value_real = inverse_transform[:patch_grid_height]
    value_imaginary = inverse_transform[patch_grid_height:]
    part_re, part_im = (
        lax.all_to_all(value_real, "row", split_axis=0, concat_axis=1, tiled=True),
        lax.all_to_all(value_imaginary, "row", split_axis=0, concat_axis=1, tiled=True),
    )
    line_re, line_im = (
        lax.all_to_all(part_re, "col", split_axis=0, concat_axis=1, tiled=True),
        lax.all_to_all(part_im, "col", split_axis=0, concat_axis=1, tiled=True),
    )
    filter_coefficient = jnp.where(jnp.arange(half) == 0, 1.0, 2.0).astype(jnp.float32)
    inverse_w = jnp.concatenate(
        [
            (cos_w.astype(jnp.float32) * filter_coefficient).T,
            -(sin_w.astype(jnp.float32) * filter_coefficient).T,
        ],
        axis=0,
    ).astype(jnp.bfloat16)
    lines = jnp.concatenate([line_re, line_im], axis=1)
    spectral = jnp.einsum("hkc,kw->hwc", lines, inverse_w, preferred_element_type=jnp.float32)
    spectral = (spectral * width_factors).astype(jnp.bfloat16)
    home = lax.all_to_all(spectral, "col", split_axis=1, concat_axis=0, tiled=True)
    return (xf + home.astype(jnp.float32) + conv).astype(jnp.bfloat16)


LANES = 128
PAIR = 64
TILE = 16
COL_CHUNKS = 4
KGROUPS = 2
BATCH = 4


def row_order(n_row, rows_dev):
    pairs = rows_dev // 2
    zc = rows_dev // TILE
    per = pairs // zc
    order = []
    for z in range(zc):
        for s in range(n_row):
            for slot in range(TILE):
                order.append(s * rows_dev + (slot // per) * pairs + z * per + slot % per)
    return np.array(order)


def exact_scale(length):
    scale = 1.0 / math.sqrt(length)
    return (scale, 1.0) if math.frexp(scale)[0] == 0.5 else (1.0, scale)


def host_tables(grid_h, grid_w, n_row, rows_dev):
    half = grid_w // 2

    def table(a, b, n):
        phase = (np.outer(a, b) % n).astype(np.float32) * np.float32(2.0 * math.pi / n)
        bf16 = ml_dtypes.bfloat16
        cos, sin = (np.cos(phase).astype(bf16), np.sin(phase).astype(bf16))
        return cos.astype(np.float32), sin.astype(np.float32)

    cos_w, sin_w = table(np.arange(half), np.arange(grid_w), grid_w)
    weight = np.where(np.arange(half) == 0, 1.0, 2.0).astype(np.float32)[:, None]
    forward = np.concatenate([cos_w, -sin_w], axis=0)
    inverse = np.concatenate([cos_w * weight, -sin_w * weight], axis=0).T
    order = row_order(n_row, rows_dev)
    cos_h, sin_h = table(order, order, grid_h)
    swap = np.zeros((TILE, TILE, TILE, TILE), np.float32)
    for a in range(TILE):
        for b in range(TILE):
            swap[a, b, b, a] = 1.0
    cast = lambda v: v.astype(ml_dtypes.bfloat16)
    fold_w, fold_h = exact_scale(grid_w)[0], exact_scale(grid_h)[0]
    return (
        cast(forward * fold_w),
        cast(inverse * fold_w),
        cast(np.concatenate([cos_h, sin_h], axis=0) * fold_h),
        cast(swap.reshape(TILE * TILE, TILE * TILE)),
    )


def half_turn(x):
    parts = [pltpu.roll(part, PAIR, 1) for part in lane_groups(x)]
    return parts[0] if len(parts) == 1 else jnp.concatenate(parts, axis=1)


def lane_groups(x):
    return [x[:, i : i + LANES] for i in range(0, x.shape[1], LANES)]


def low_lanes(shape):
    return lax.broadcasted_iota(jnp.int32, shape, len(shape) - 1) % LANES < PAIR


def scaled(x, factor):
    return x if factor == 1.0 else x * factor


def swap_halves(a, b):
    low = low_lanes(a.shape)
    return jnp.where(low, a, half_turn(b)), jnp.where(low, half_turn(a), b)


def mixing_kernel(
    n_row,
    n_col,
    scale_w,
    scale_h,
    patches_hbm,
    gain_hbm,
    w_first_hbm,
    w_second_hbm,
    depth_hbm,
    forward_hbm,
    inverse_hbm,
    height_hbm,
    swap_hbm,
    out_hbm,
    patches,
    gain,
    w_first,
    w_second,
    depth,
    forward_ref,
    inverse_ref,
    height_ref,
    swap_ref,
    send1,
    recv1,
    turned,
    send2,
    recv2,
    send3,
    recv3,
    send4,
    recv4,
    conv,
    rim_send,
    rim_recv,
    rim,
    s1,
    r1,
    s2,
    r2,
    s3,
    r3,
    s4,
    r4,
    sh,
    rh,
    fetch_sem,
    patch_sem,
    out_sem,
):
    f32, bf16 = jnp.float32, jnp.bfloat16
    row, col = lax.axis_index("row"), lax.axis_index("col")
    rows_dev, cols_dev, chans = patches.shape
    pairs = rows_dev // 2
    per_col = pairs // COL_CHUNKS
    zc = rows_dev // TILE
    per_z = pairs // zc
    col_per_z = COL_CHUNKS // zc
    grid_w = cols_dev * n_col
    half = grid_w // 2
    kl = half // n_row
    per_k = kl // KGROUPS
    groups = chans // LANES

    def col_peer(d):
        return lax.rem(col + d, n_col)

    def row_peer(d):
        return lax.rem(row + d, n_row)

    def to_col(d):
        return {"col": col_peer(d)}

    def to_row(d):
        return {"row": row_peer(d)}

    def dot(a, b):
        return jnp.dot(a, b, preferred_element_type=f32)

    barrier = pltpu.get_barrier_semaphore()
    for d in range(1, n_col):
        pl.semaphore_signal(barrier, inc=1, device_id=to_col(d), device_id_type=pl.DeviceIdType.MESH)
    for d in range(1, n_row):
        pl.semaphore_signal(barrier, inc=1, device_id=to_row(d), device_id_type=pl.DeviceIdType.MESH)

    def chunk_rows(ch, side):
        return pl.ds(side * pairs + ch * per_col, per_col)

    def fetch_patches(ch, side):
        rows = chunk_rows(ch, side)
        return pltpu.make_async_copy(patches_hbm.at[rows], patches.at[rows], patch_sem.at[ch, side])

    def leave(ch, side):
        rows = chunk_rows(ch, side)
        return pltpu.make_async_copy(patches.at[rows], out_hbm.at[rows], out_sem.at[ch, side])

    operands = (
        (gain_hbm, gain),
        (forward_hbm, forward_ref),
        (swap_hbm, swap_ref),
        (w_first_hbm, w_first),
        (w_second_hbm, w_second),
        (depth_hbm, depth),
        (height_hbm, height_ref),
        (inverse_hbm, inverse_ref),
    )
    fetches = [
        pltpu.make_async_copy(src, dst, fetch_sem.at[i]) for i, (src, dst) in enumerate(operands)
    ]
    for side in range(2):
        fetch_patches(0, side).start()
    fetches[0].start()
    for ch in range(1, COL_CHUNKS):
        for side in range(2):
            fetch_patches(ch, side).start()
    for fetch in fetches[1:]:
        fetch.start()
    fetches[0].wait()

    def copy1(ch, d):
        return pltpu.make_async_remote_copy(
            src_ref=send1.at[ch, col_peer(d)],
            dst_ref=recv1.at[ch, col],
            send_sem=s1.at[ch, d - 1],
            recv_sem=r1.at[ch, d - 1],
            device_id=to_col(d),
            device_id_type=pl.DeviceIdType.MESH,
        )

    def copy2(z, g, d):
        ks = pl.ds(g * per_k, per_k)
        return pltpu.make_async_remote_copy(
            src_ref=send2.at[z, row_peer(d), ks],
            dst_ref=recv2.at[z, row, ks],
            send_sem=s2.at[z, g, d - 1],
            recv_sem=r2.at[z, g, d - 1],
            device_id=to_row(d),
            device_id_type=pl.DeviceIdType.MESH,
        )

    def copy3(z, g, d):
        ks = pl.ds(g * per_k, per_k)
        return pltpu.make_async_remote_copy(
            src_ref=send3.at[z, row_peer(d), ks],
            dst_ref=recv3.at[z, row, ks],
            send_sem=s3.at[z, g, d - 1],
            recv_sem=r3.at[z, g, d - 1],
            device_id=to_row(d),
            device_id_type=pl.DeviceIdType.MESH,
        )

    def copy4(ch, d):
        return pltpu.make_async_remote_copy(
            src_ref=send4.at[ch, col_peer(d)],
            dst_ref=recv4.at[ch, col],
            send_sem=s4.at[ch, d - 1],
            recv_sem=r4.at[ch, d - 1],
            device_id=to_col(d),
            device_id_type=pl.DeviceIdType.MESH,
        )

    def copy_rim(side):
        return pltpu.make_async_remote_copy(
            src_ref=rim_send.at[side],
            dst_ref=rim_recv.at[side],
            send_sem=sh.at[side],
            recv_sem=rh.at[side],
            device_id=to_row(1 if side == 0 else n_row - 1),
            device_id_type=pl.DeviceIdType.MESH,
        )

    def normed_row(h):
        x = patches[h].astype(f32)
        mean = jnp.mean(x, axis=-1, keepdims=True)
        centred = x - mean
        var = jnp.mean(centred * centred, axis=-1, keepdims=True)
        return centred * lax.rsqrt(var + 1e-05) * gain[...]

    for ch in range(COL_CHUNKS):
        for side in range(2):
            fetch_patches(ch, side).wait()

        def norm_pair(i, carry, ch=ch):
            hp = ch * per_col + i
            lower, upper = normed_row(hp), normed_row(hp + pairs)
            for j in range(groups):
                lanes = slice(j * LANES, (j + 1) * LANES)
                even, odd = swap_halves(lower[:, lanes], upper[:, lanes])
                send1[ch, 2 * j, i] = even.astype(bf16)
                send1[ch, 2 * j + 1, i] = odd.astype(bf16)
            return carry

        lax.fori_loop(0, per_col, norm_pair, 0)
        if ch == 0:
            pl.semaphore_wait(barrier, n_col + n_row - 2)
        for d in range(1, n_col):
            copy1(ch, d).start()
        recv1[ch, col] = send1[ch, col]

    def line(ch, i):
        return recv1[ch, :, i].reshape(grid_w, LANES)

    for fetch in fetches[1:]:
        fetch.wait()
    for z in range(zc):
        for ch in range(z * col_per_z, (z + 1) * col_per_z):
            for d in range(1, n_col):
                copy1(ch, d).wait_recv()

            x = jnp.concatenate([line(ch, i) for i in range(per_col)], axis=1)
            y = scaled(dot(forward_ref[...], x), scale_w)
            lower, upper = swap_halves(y[:half], y[half:])
            for i in range(per_col):
                slot = (ch - z * col_per_z) * per_col + i
                turned[slot] = lane_groups(lower)[i].astype(bf16)
                turned[per_z + slot] = lane_groups(upper)[i].astype(bf16)

        def turn_out(step, carry, z=z):
            rs = [step * BATCH + i for i in range(BATCH)]
            tiles = [
                turned[:, pl.ds(pl.multiple_of(r * kl, kl), kl), :].reshape(TILE * kl, LANES)
                for r in rs
            ]
            swapped = dot(swap_ref[...], jnp.concatenate(tiles, axis=1)).astype(bf16)
            for r, part in zip(rs, lane_groups(swapped)):
                send2[z, r] = part.reshape(kl, TILE, LANES)
            return carry

        lax.fori_loop(0, n_row // BATCH, turn_out, 0)
        for g in range(KGROUPS):
            for d in range(1, n_row):
                copy2(z, g, d).start()
        recv2[z, row] = send2[z, row]

    first = line(0, 0).astype(f32)
    final = line(COL_CHUNKS - 1, per_col - 1).astype(f32)
    rim_send[0] = swap_halves(final[:half], final[half:])[1].astype(bf16)
    rim_send[1] = swap_halves(first[:half], first[half:])[0].astype(bf16)
    for side in range(2):
        copy_rim(side).start()

    def complex_weight(ref):
        re, im = ref[0, col].astype(f32), ref[1, col].astype(f32)
        one = jnp.concatenate(
            [jnp.concatenate([re, im], axis=1), jnp.concatenate([-im, re], axis=1)], axis=0
        ).astype(bf16)
        none = jnp.zeros_like(one)
        return jnp.concatenate(
            [jnp.concatenate([one, none], axis=1), jnp.concatenate([none, one], axis=1)], axis=0
        )

    weight_a, weight_b = complex_weight(w_first), complex_weight(w_second)

    lane_group = pl.multiple_of((col // 2) * LANES, LANES)
    taps = []
    for i in range(3):
        own = depth[i, :, pl.ds(lane_group, LANES)]
        low = low_lanes(own.shape)
        other = half_turn(own)
        taps.append(
            jnp.where((col % 2) == 0, jnp.where(low, own, other), jnp.where(low, other, own))
        )
    for side in range(2):
        copy_rim(side).wait_recv()
    before = rim_recv[0].astype(f32)
    after = rim_recv[1].astype(f32)
    before = jnp.concatenate([before, half_turn(before)], axis=0)
    after = jnp.concatenate([half_turn(after), after], axis=0)
    low = low_lanes(before.shape)
    rim[0] = jnp.where(low, before, half_turn(final)).astype(bf16)
    rim[1] = jnp.where(low, half_turn(first), after).astype(bf16)

    def conv_pair(hp, above, here, below):
        total = None
        for j in range(3):
            part = None
            for i, rows in enumerate((above, here, below)):
                term = rows * taps[i][j : j + 1]
                part = term if part is None else part + term
            if j == 0:
                part = pltpu.roll(part, 1, 0)
            if j == 2:
                part = pltpu.roll(part, grid_w - 1, 0)
            total = part if total is None else total + part
        conv[hp] = total

    def at(hp):
        return line(hp // per_col, hp % per_col).astype(f32)

    conv_pair(0, rim[0].astype(f32), at(0), at(1))

    def conv_inner(hp, carry):
        conv_pair(hp, at(hp - 1), at(hp), at(hp + 1))
        return carry

    lax.fori_loop(1, pairs - 1, conv_inner, 0)
    conv_pair(pairs - 1, at(pairs - 2), at(pairs - 1), rim[1].astype(f32))

    grid_h = rows_dev * n_row
    sign = jnp.where(low_lanes((1, 2 * LANES)), 1.0, -1.0)

    def height(u):
        both = dot(height_ref[...], u)
        return both[:grid_h], half_turn(both[grid_h:]) * sign

    def filter_pair(k):
        u = jnp.concatenate(
            [recv2[:, :, k + i].reshape(grid_h, LANES) for i in range(2)], axis=1
        )
        a, b = height(u)
        zed = scaled(a + b, scale_h).astype(bf16)
        hidden = jnp.tanh(dot(zed, weight_a)).astype(bf16)
        s = dot(hidden, weight_b)
        s = (s - jnp.clip(s, -0.25, 0.25)).astype(bf16)
        a, b = height(s)
        v = scaled(a - b, scale_h).astype(bf16)
        for i, part in enumerate(lane_groups(v)):
            send3[:, :, k + i] = part.reshape(zc, n_row, TILE, LANES)

    def filter_modes(step, carry):
        for i in range(0, BATCH, 2):
            filter_pair(step * BATCH + i)
        return carry

    for g in range(KGROUPS):
        for z in range(zc):
            for d in range(1, n_row):
                copy2(z, g, d).wait_recv()
        lax.fori_loop(g * per_k // BATCH, (g + 1) * per_k // BATCH, filter_modes, 0)
        for d in range(1, n_row):
            copy3(0, g, d).start()
    for z in range(1, zc):
        for g in range(KGROUPS):
            for d in range(1, n_row):
                copy3(z, g, d).start()
    for z in range(zc):
        recv3[z, row] = send3[z, row]

    for z in range(zc):
        for g in range(KGROUPS):
            for d in range(1, n_row):
                copy3(z, g, d).wait_recv()

        def turn_back(step, carry, z=z):
            rs = [step * BATCH + i for i in range(BATCH)]
            tiles = [recv3[z, r].reshape(kl * TILE, LANES) for r in rs]
            swapped = dot(swap_ref[...], jnp.concatenate(tiles, axis=1)).astype(bf16)
            for r, part in zip(rs, lane_groups(swapped)):
                ks = pl.ds(pl.multiple_of(r * kl, kl), kl)
                turned[:, ks, :] = part.reshape(TILE, kl, LANES)
            return carry

        lax.fori_loop(0, n_row // BATCH, turn_back, 0)
        for ch in range(z * col_per_z, (z + 1) * col_per_z):
            columns = []
            for i in range(per_col):
                slot = (ch - z * col_per_z) * per_col + i
                re, im = swap_halves(turned[slot].astype(f32), turned[per_z + slot].astype(f32))
                columns.append(jnp.concatenate([re.astype(bf16), im.astype(bf16)], axis=0))
            cells = scaled(dot(inverse_ref[...], jnp.concatenate(columns, axis=1)), scale_w)
            for i, part in enumerate(lane_groups(cells)):
                part = (part + conv[ch * per_col + i]).astype(bf16)
                send4[ch, :, i] = part.reshape(n_col, cols_dev, LANES)
            for d in range(1, n_col):
                copy4(ch, d).start()
            recv4[ch, col] = send4[ch, col]

    for ch in range(COL_CHUNKS):
        for d in range(1, n_col):
            copy4(ch, d).wait_recv()

        def finish_pair(i, carry, ch=ch):
            hp = ch * per_col + i
            for j in range(groups):
                lanes = slice(j * LANES, (j + 1) * LANES)
                lower, upper = swap_halves(
                    recv4[ch, 2 * j, i].astype(f32), recv4[ch, 2 * j + 1, i].astype(f32)
                )
                patches[hp, :, lanes] = (patches[hp, :, lanes].astype(f32) + lower).astype(bf16)
                patches[hp + pairs, :, lanes] = (
                    patches[hp + pairs, :, lanes].astype(f32) + upper
                ).astype(bf16)
            return carry

        lax.fori_loop(0, per_col, finish_pair, 0)
        for side in range(2):
            leave(ch, side).start()

    for ch in range(COL_CHUNKS):
        for d in range(1, n_col):
            copy1(ch, d).wait_send()
            copy4(ch, d).wait_send()
    for z in range(zc):
        for g in range(KGROUPS):
            for d in range(1, n_row):
                copy2(z, g, d).wait_send()
                copy3(z, g, d).wait_send()
    for side in range(2):
        copy_rim(side).wait_send()
    for ch in range(COL_CHUNKS):
        for side in range(2):
            leave(ch, side).wait()


def fused(patches, norm_gain, w_first, w_second, depth_kernel):
    n_row = lax.axis_size("row")
    n_col = lax.axis_size("col")
    rows_dev, cols_dev, chans = patches.shape
    grid_h, grid_w = rows_dev * n_row, cols_dev * n_col
    pairs, zc = rows_dev // 2, rows_dev // TILE
    per_col = pairs // COL_CHUNKS
    half = grid_w // 2
    kl = half // n_row
    tables = host_tables(grid_h, grid_w, n_row, rows_dev)
    bf16, f32 = jnp.bfloat16, jnp.float32
    anywhere = pl.BlockSpec(memory_space=pl.ANY)
    col_buffer = pltpu.VMEM((COL_CHUNKS, n_col, per_col, cols_dev, LANES), bf16)
    row_buffer = pltpu.VMEM((zc, n_row, kl, TILE, LANES), bf16)
    col_sems = pltpu.SemaphoreType.DMA((COL_CHUNKS, n_col - 1))
    row_sems = pltpu.SemaphoreType.DMA((zc, KGROUPS, n_row - 1))
    rim_sems = pltpu.SemaphoreType.DMA((2,))
    operands = (
        patches,
        norm_gain.reshape(1, chans),
        w_first,
        w_second,
        depth_kernel,
        *[jnp.asarray(t) for t in tables],
    )
    return pl.pallas_call(
        functools.partial(
            mixing_kernel, n_row, n_col, exact_scale(grid_w)[1], exact_scale(grid_h)[1]
        ),
        out_shape=jax.ShapeDtypeStruct(patches.shape, bf16),
        in_specs=[anywhere] * 9,
        out_specs=anywhere,
        scratch_shapes=[
            *[pltpu.VMEM(v.shape, v.dtype) for v in operands],
            col_buffer,
            col_buffer,
            pltpu.VMEM((TILE, half, LANES), bf16),
            row_buffer,
            row_buffer,
            row_buffer,
            row_buffer,
            col_buffer,
            col_buffer,
            pltpu.VMEM((pairs, grid_w, LANES), f32),
            pltpu.VMEM((2, half, LANES), bf16),
            pltpu.VMEM((2, half, LANES), bf16),
            pltpu.VMEM((2, grid_w, LANES), bf16),
            col_sems,
            col_sems,
            row_sems,
            row_sems,
            row_sems,
            row_sems,
            col_sems,
            col_sems,
            rim_sems,
            rim_sems,
            pltpu.SemaphoreType.DMA((8,)),
            pltpu.SemaphoreType.DMA((COL_CHUNKS, 2)),
            pltpu.SemaphoreType.DMA((COL_CHUNKS, 2)),
        ],
        compiler_params=pltpu.CompilerParams(
            collective_id=0, has_side_effects=True, vmem_limit_bytes=40 * 1024 * 1024
        ),
        cost_estimate=pl.CostEstimate(flops=2_000_000_000, bytes_accessed=3_000_000, transcendentals=600_000),
    )(*operands)


def fits(patches, w_first):
    n_row, n_col = lax.axis_size("row"), lax.axis_size("col")
    rows_dev, cols_dev, chans = patches.shape
    blocks, width = w_first.shape[1:3]
    half = cols_dev * n_col // 2
    return (
        blocks == n_col
        and width == PAIR
        and chans % LANES == 0
        and rows_dev == 2 * TILE
        and cols_dev % TILE == 0
        and half == n_row * TILE
        and n_row % BATCH == 0
    )


def local(patches, norm_gain, w_first, w_second, depth_kernel):
    plan = fused if fits(patches, w_first) else general
    return plan(patches, norm_gain, w_first, w_second, depth_kernel)


def solution(mesh):
    return jax.shard_map(
        local,
        mesh=mesh,
        in_specs=(P("row", "col", None), P(), P(), P(), P()),
        out_specs=P("row", "col", None),
        check_vma=False,
    )
```

```python
import functools
import math

import jax
import jax.numpy as jnp
import ml_dtypes
import numpy as np
from jax import lax
from jax.experimental import pallas as pl
from jax.experimental.pallas import tpu as pltpu
from jax.sharding import PartitionSpec as P


def with_halo(shard, sides, width):
    for axis, dim in sides:
        devices, length = (lax.axis_size(axis), shard.shape[dim])
        up = [(i, (i + 1) % devices) for i in range(devices)]
        down = [(j, i) for i, j in up]
        last = lax.slice_in_dim(shard, length - width, length, axis=dim)
        leading = lax.slice_in_dim(shard, 0, width, axis=dim)
        before = lax.ppermute(last, axis, up)
        after = lax.ppermute(leading, axis, down)
        shard = jnp.concatenate([before, shard, after], axis=dim)
    return shard


def phase_table(first_idx, second_idx, length):
    product = first_idx[:, None] * second_idx[None, :] % length
    phase = product.astype(jnp.float32) * (2.0 * math.pi / length)
    return (jnp.cos(phase).astype(jnp.bfloat16), jnp.sin(phase).astype(jnp.bfloat16))


def shrink(values):
    level = 0.25
    return jnp.where(
        values > level, values - level, jnp.where(values < -level, values + level, 0.0 * values)
    )


def block_product(left, weight):
    return jnp.einsum("qmbc,bcd->qmbd", left, weight, preferred_element_type=jnp.float32)


def general(patches, norm_gain, w_first, w_second, depth_kernel):
    n_row = lax.axis_size("row")
    n_col = lax.axis_size("col")
    rows_dev, cols_dev, chans = patches.shape
    patch_grid_height = rows_dev * n_row
    grid_w = cols_dev * n_col
    half = grid_w // 2
    blocks = w_first.shape[1]
    width = w_first.shape[2]
    width_factors = 1.0 / math.sqrt(grid_w)
    height_factors = 1.0 / math.sqrt(patch_grid_height)
    xf = patches.astype(jnp.float32)
    mean = jnp.mean(xf, axis=-1, keepdims=True)
    var = jnp.mean((xf - mean) ** 2, axis=-1, keepdims=True)
    normed = ((xf - mean) * lax.rsqrt(var + 1e-05) * norm_gain).astype(jnp.bfloat16)
    padded = with_halo(normed, (("row", 0), ("col", 1)), 1)
    conv = jnp.zeros((rows_dev, cols_dev, chans), jnp.float32)
    for i in range(3):
        for j in range(3):
            conv = conv + padded[i : i + rows_dev, j : j + cols_dev] * depth_kernel[i, j]
    strips = lax.all_to_all(normed, "col", split_axis=0, concat_axis=1, tiled=True)
    cos_w, sin_w = phase_table(
        jnp.arange(grid_w, dtype=jnp.int32), jnp.arange(half, dtype=jnp.int32), grid_w
    )
    forward_w = jnp.concatenate([cos_w, -sin_w], axis=1)
    spectrum_values = jnp.einsum(
        "hwc,wk->hkc", strips, forward_w, preferred_element_type=jnp.float32
    )
    spectrum_values = (spectrum_values * width_factors).astype(jnp.bfloat16)
    wre = spectrum_values[:, :half]
    wim = spectrum_values[:, half:]
    positions = jnp.arange(patch_grid_height, dtype=jnp.int32)
    across_re, across_im = (
        lax.all_to_all(wre, "col", split_axis=1, concat_axis=0, tiled=True),
        lax.all_to_all(wim, "col", split_axis=1, concat_axis=0, tiled=True),
    )
    full_re, full_im = (
        lax.all_to_all(across_re, "row", split_axis=1, concat_axis=0, tiled=True),
        lax.all_to_all(across_im, "row", split_axis=1, concat_axis=0, tiled=True),
    )
    cos_h, sin_h = phase_table(positions, positions, patch_grid_height)
    big_table = jnp.concatenate(
        [jnp.concatenate([cos_h, sin_h], axis=1), jnp.concatenate([-sin_h, cos_h], axis=1)], axis=0
    )
    stacked = jnp.concatenate([full_re, full_im], axis=0)
    spectrum = jnp.einsum("qp,pmc->qmc", big_table, stacked, preferred_element_type=jnp.float32)
    spectrum = (spectrum * height_factors).astype(jnp.bfloat16)
    modes = spectrum.shape[1]
    zre = spectrum[:patch_grid_height].reshape(patch_grid_height, modes, blocks, width)
    zim = spectrum[patch_grid_height:].reshape(patch_grid_height, modes, blocks, width)
    hre = jnp.tanh(block_product(zre, w_first[0]) - block_product(zim, w_first[1])).astype(
        jnp.bfloat16
    )
    him = jnp.tanh(block_product(zre, w_first[1]) + block_product(zim, w_first[0])).astype(
        jnp.bfloat16
    )
    spectrum_real = shrink(
        block_product(hre, w_second[0]) - block_product(him, w_second[1])
    ).astype(jnp.bfloat16)
    spectrum_imaginary = shrink(
        block_product(hre, w_second[1]) + block_product(him, w_second[0])
    ).astype(jnp.bfloat16)
    filtered = jnp.concatenate(
        [
            spectrum_real.reshape(patch_grid_height, modes, chans),
            spectrum_imaginary.reshape(patch_grid_height, modes, chans),
        ],
        axis=0,
    )
    inverse_transform = jnp.einsum(
        "qp,qmc->pmc", big_table, filtered, preferred_element_type=jnp.float32
    )
    inverse_transform = (inverse_transform * height_factors).astype(jnp.bfloat16)
    value_real = inverse_transform[:patch_grid_height]
    value_imaginary = inverse_transform[patch_grid_height:]
    part_re, part_im = (
        lax.all_to_all(value_real, "row", split_axis=0, concat_axis=1, tiled=True),
        lax.all_to_all(value_imaginary, "row", split_axis=0, concat_axis=1, tiled=True),
    )
    line_re, line_im = (
        lax.all_to_all(part_re, "col", split_axis=0, concat_axis=1, tiled=True),
        lax.all_to_all(part_im, "col", split_axis=0, concat_axis=1, tiled=True),
    )
    filter_coefficient = jnp.where(jnp.arange(half) == 0, 1.0, 2.0).astype(jnp.float32)
    inverse_w = jnp.concatenate(
        [
            (cos_w.astype(jnp.float32) * filter_coefficient).T,
            -(sin_w.astype(jnp.float32) * filter_coefficient).T,
        ],
        axis=0,
    ).astype(jnp.bfloat16)
    lines = jnp.concatenate([line_re, line_im], axis=1)
    spectral = jnp.einsum("hkc,kw->hwc", lines, inverse_w, preferred_element_type=jnp.float32)
    spectral = (spectral * width_factors).astype(jnp.bfloat16)
    home = lax.all_to_all(spectral, "col", split_axis=1, concat_axis=0, tiled=True)
    return (xf + home.astype(jnp.float32) + conv).astype(jnp.bfloat16)


LANES = 128
PAIR = 64
TILE = 16
SLOTS = 8
TURN = 32
COL_CHUNKS = 4
KGROUPS = 2
BATCH = 2


def row_order(n_row, rows_dev):
    pairs = rows_dev // 2
    zc = rows_dev // SLOTS
    per = pairs // zc
    order = []
    for z in range(zc):
        for s in range(n_row):
            for slot in range(SLOTS):
                order.append(s * rows_dev + (slot // per) * pairs + z * per + slot % per)
    return np.array(order)


def exact_scale(length):
    scale = 1.0 / math.sqrt(length)
    return (scale, 1.0) if math.frexp(scale)[0] == 0.5 else (1.0, scale)


def host_tables(grid_h, grid_w, n_row, rows_dev):
    half = grid_w // 2

    def table(a, b, n):
        phase = (np.outer(a, b) % n).astype(np.float32) * np.float32(2.0 * math.pi / n)
        bf16 = ml_dtypes.bfloat16
        cos, sin = (np.cos(phase).astype(bf16), np.sin(phase).astype(bf16))
        return cos.astype(np.float32), sin.astype(np.float32)

    cos_w, sin_w = table(np.arange(half), np.arange(grid_w), grid_w)
    weight = np.where(np.arange(half) == 0, 1.0, 2.0).astype(np.float32)[:, None]
    forward = np.concatenate([cos_w, -sin_w], axis=0)
    inverse = np.concatenate([cos_w * weight, -sin_w * weight], axis=0).T
    order = row_order(n_row, rows_dev)
    cos_h, sin_h = table(order, order, grid_h)
    swap = np.zeros((TURN, SLOTS, SLOTS, TURN), np.float32)
    for a in range(TURN):
        for b in range(SLOTS):
            swap[a, b, b, a] = 1.0
    swap = swap.reshape(TURN * SLOTS, TURN * SLOTS)
    cast = lambda v: v.astype(ml_dtypes.bfloat16)
    fold_w, fold_h = exact_scale(grid_w)[0], exact_scale(grid_h)[0]
    return (
        cast(forward * fold_w),
        cast(inverse * fold_w),
        cast(np.concatenate([cos_h, sin_h], axis=0) * fold_h),
        cast(np.stack([swap, swap.T])),
    )


def half_turn(x):
    parts = [pltpu.roll(part, PAIR, 1) for part in lane_groups(x)]
    return parts[0] if len(parts) == 1 else jnp.concatenate(parts, axis=1)


def lane_groups(x):
    return [x[:, i : i + LANES] for i in range(0, x.shape[1], LANES)]


def low_lanes(shape):
    return lax.broadcasted_iota(jnp.int32, shape, len(shape) - 1) % LANES < PAIR


def scaled(x, factor):
    return x if factor == 1.0 else x * factor


def swap_halves(a, b):
    low = low_lanes(a.shape)
    return jnp.where(low, a, half_turn(b)), jnp.where(low, half_turn(a), b)


def mixing_kernel(
    n_row,
    n_col,
    scale_w,
    scale_h,
    patches_hbm,
    gain_hbm,
    w_first_hbm,
    w_second_hbm,
    depth_hbm,
    forward_hbm,
    inverse_hbm,
    height_hbm,
    swap_hbm,
    out_hbm,
    patches,
    gain,
    w_first,
    w_second,
    depth,
    forward_ref,
    inverse_ref,
    height_ref,
    swap_ref,
    send1,
    recv1,
    turned,
    send2,
    recv2,
    send3,
    recv3,
    send4,
    recv4,
    conv,
    rim_send,
    rim_recv,
    rim,
    s1,
    r1,
    s2,
    r2,
    s3,
    r3,
    s4,
    r4,
    sh,
    rh,
    fetch_sem,
    patch_sem,
    out_sem,
):
    f32, bf16 = jnp.float32, jnp.bfloat16
    row, col = lax.axis_index("row"), lax.axis_index("col")
    rows_dev, cols_dev, chans = patches.shape
    pairs = rows_dev // 2
    per_col = pairs // COL_CHUNKS
    zc = COL_CHUNKS
    grid_w = cols_dev * n_col
    half = grid_w // 2
    kl = half // n_row
    per_k = kl // 2 // KGROUPS
    turns = [pl.ds(q * TURN, TURN) for q in range(half // TURN)]
    owners = [pl.ds(q * TURN // kl, TURN // kl) for q in range(half // TURN)]
    groups = chans // LANES

    def col_peer(d):
        return lax.rem(col + d, n_col)

    def row_peer(d):
        return lax.rem(row + d, n_row)

    def to_col(d):
        return {"col": col_peer(d)}

    def to_row(d):
        return {"row": row_peer(d)}

    def dot(a, b):
        return jnp.dot(a, b, preferred_element_type=f32)

    barrier = pltpu.get_barrier_semaphore()
    for d in range(1, n_col):
        pl.semaphore_signal(barrier, inc=1, device_id=to_col(d), device_id_type=pl.DeviceIdType.MESH)
    for d in range(1, n_row):
        pl.semaphore_signal(barrier, inc=1, device_id=to_row(d), device_id_type=pl.DeviceIdType.MESH)

    def chunk_rows(ch, side):
        return pl.ds(side * pairs + ch * per_col, per_col)

    def fetch_patches(ch, side):
        rows = chunk_rows(ch, side)
        return pltpu.make_async_copy(patches_hbm.at[rows], patches.at[rows], patch_sem.at[ch, side])

    def leave(ch, side):
        rows = chunk_rows(ch, side)
        return pltpu.make_async_copy(patches.at[rows], out_hbm.at[rows], out_sem.at[ch, side])

    operands = (
        (gain_hbm, gain),
        (forward_hbm, forward_ref),
        (swap_hbm, swap_ref),
        (w_first_hbm, w_first),
        (w_second_hbm, w_second),
        (depth_hbm, depth),
        (height_hbm, height_ref),
        (inverse_hbm, inverse_ref),
    )
    fetches = [
        pltpu.make_async_copy(src, dst, fetch_sem.at[i]) for i, (src, dst) in enumerate(operands)
    ]
    for side in range(2):
        fetch_patches(0, side).start()
    fetches[0].start()
    for ch in range(1, COL_CHUNKS):
        for side in range(2):
            fetch_patches(ch, side).start()
    for fetch in fetches[1:]:
        fetch.start()
    fetches[0].wait()

    def copy1(ch, d):
        return pltpu.make_async_remote_copy(
            src_ref=send1.at[ch, col_peer(d)],
            dst_ref=recv1.at[ch, col],
            send_sem=s1.at[ch, d - 1],
            recv_sem=r1.at[ch, d - 1],
            device_id=to_col(d),
            device_id_type=pl.DeviceIdType.MESH,
        )

    def copy2(z, g, d):
        ks = pl.ds(g * per_k, per_k)
        return pltpu.make_async_remote_copy(
            src_ref=send2.at[z, row_peer(d), ks],
            dst_ref=recv2.at[z, row, ks],
            send_sem=s2.at[z, g, d - 1],
            recv_sem=r2.at[z, g, d - 1],
            device_id=to_row(d),
            device_id_type=pl.DeviceIdType.MESH,
        )

    def copy3(z, g, d):
        ks = pl.ds(g * per_k, per_k)
        return pltpu.make_async_remote_copy(
            src_ref=send3.at[z, row_peer(d), ks],
            dst_ref=recv3.at[z, row, ks],
            send_sem=s3.at[z, g, d - 1],
            recv_sem=r3.at[z, g, d - 1],
            device_id=to_row(d),
            device_id_type=pl.DeviceIdType.MESH,
        )

    def copy4(ch, d):
        return pltpu.make_async_remote_copy(
            src_ref=send4.at[ch, col_peer(d)],
            dst_ref=recv4.at[ch, col],
            send_sem=s4.at[ch, d - 1],
            recv_sem=r4.at[ch, d - 1],
            device_id=to_col(d),
            device_id_type=pl.DeviceIdType.MESH,
        )

    def copy_rim(side):
        return pltpu.make_async_remote_copy(
            src_ref=rim_send.at[side],
            dst_ref=rim_recv.at[side],
            send_sem=sh.at[side],
            recv_sem=rh.at[side],
            device_id=to_row(1 if side == 0 else n_row - 1),
            device_id_type=pl.DeviceIdType.MESH,
        )

    def normed_row(h):
        x = patches[h].astype(f32)
        mean = jnp.mean(x, axis=-1, keepdims=True)
        centred = x - mean
        var = jnp.mean(centred * centred, axis=-1, keepdims=True)
        return centred * lax.rsqrt(var + 1e-05) * gain[...]

    for ch in range(COL_CHUNKS):
        for side in range(2):
            fetch_patches(ch, side).wait()

        def norm_pair(i, carry, ch=ch):
            hp = ch * per_col + i
            lower, upper = normed_row(hp), normed_row(hp + pairs)
            for j in range(groups):
                lanes = slice(j * LANES, (j + 1) * LANES)
                even, odd = swap_halves(lower[:, lanes], upper[:, lanes])
                send1[ch, 2 * j, i] = even.astype(bf16)
                send1[ch, 2 * j + 1, i] = odd.astype(bf16)
            return carry

        lax.fori_loop(0, per_col, norm_pair, 0)
        if ch == 0:
            pl.semaphore_wait(barrier, n_col + n_row - 2)
        for d in range(1, n_col):
            copy1(ch, d).start()
        recv1[ch, col] = send1[ch, col]

    def line(ch, i):
        return recv1[ch, :, i].reshape(grid_w, LANES)

    for fetch in fetches[1:]:
        fetch.wait()
    for z in range(zc):
        for d in range(1, n_col):
            copy1(z, d).wait_recv()
        x = jnp.concatenate([line(z, i) for i in range(per_col)], axis=1)
        y = scaled(dot(forward_ref[...], x), scale_w)
        lower, upper = swap_halves(y[:half], y[half:])
        for i in range(per_col):
            turned[i] = lane_groups(lower)[i].astype(bf16)
            turned[per_col + i] = lane_groups(upper)[i].astype(bf16)
        tiles = [turned[:, ks, :].reshape(TURN * SLOTS, LANES) for ks in turns]
        swapped = dot(swap_ref[0], jnp.concatenate(tiles, axis=1)).astype(bf16)
        for own, part in zip(owners, lane_groups(swapped)):
            send2[z, own] = part.reshape(TURN // kl, kl // 2, TILE, LANES)
        for g in range(KGROUPS):
            for d in range(1, n_row):
                copy2(z, g, d).start()
        recv2[z, row] = send2[z, row]

    first = line(0, 0).astype(f32)
    final = line(COL_CHUNKS - 1, per_col - 1).astype(f32)
    rim_send[0] = swap_halves(final[:half], final[half:])[1].astype(bf16)
    rim_send[1] = swap_halves(first[:half], first[half:])[0].astype(bf16)
    for side in range(2):
        copy_rim(side).start()

    def complex_weight(ref):
        re, im = ref[0, col].astype(f32), ref[1, col].astype(f32)
        one = jnp.concatenate(
            [jnp.concatenate([re, im], axis=1), jnp.concatenate([-im, re], axis=1)], axis=0
        ).astype(bf16)
        none = jnp.zeros_like(one)
        return jnp.concatenate(
            [jnp.concatenate([one, none], axis=1), jnp.concatenate([none, one], axis=1)], axis=0
        )

    weight_a, weight_b = complex_weight(w_first), complex_weight(w_second)

    lane_group = pl.multiple_of((col // 2) * LANES, LANES)
    taps = []
    for i in range(3):
        own = depth[i, :, pl.ds(lane_group, LANES)]
        low = low_lanes(own.shape)
        other = half_turn(own)
        taps.append(
            jnp.where((col % 2) == 0, jnp.where(low, own, other), jnp.where(low, other, own))
        )
    for side in range(2):
        copy_rim(side).wait_recv()
    before = rim_recv[0].astype(f32)
    after = rim_recv[1].astype(f32)
    before = jnp.concatenate([before, half_turn(before)], axis=0)
    after = jnp.concatenate([half_turn(after), after], axis=0)
    low = low_lanes(before.shape)
    rim[0] = jnp.where(low, before, half_turn(final)).astype(bf16)
    rim[1] = jnp.where(low, half_turn(first), after).astype(bf16)

    def conv_pair(hp, above, here, below):
        total = None
        for j in range(3):
            part = None
            for i, rows in enumerate((above, here, below)):
                term = rows * taps[i][j : j + 1]
                part = term if part is None else part + term
            if j == 0:
                part = pltpu.roll(part, 1, 0)
            if j == 2:
                part = pltpu.roll(part, grid_w - 1, 0)
            total = part if total is None else total + part
        conv[hp] = total

    def at(hp):
        return line(hp // per_col, hp % per_col).astype(f32)

    conv_pair(0, rim[0].astype(f32), at(0), at(1))

    def conv_inner(hp, carry):
        conv_pair(hp, at(hp - 1), at(hp), at(hp + 1))
        return carry

    lax.fori_loop(1, pairs - 1, conv_inner, 0)
    conv_pair(pairs - 1, at(pairs - 2), at(pairs - 1), rim[1].astype(f32))

    grid_h = rows_dev * n_row
    sign = jnp.where(low_lanes((1, 2 * LANES)), 1.0, -1.0)

    def height(u):
        both = dot(height_ref[...], u)
        return both[:grid_h], half_turn(both[grid_h:]) * sign

    def filter_pair(k):
        tile = recv2[:, :, k].astype(f32).reshape(zc * n_row, TILE, LANES)
        u = jnp.concatenate(
            [
                tile[:, i : i + SLOTS].reshape(grid_h, LANES).astype(bf16)
                for i in range(0, TILE, SLOTS)
            ],
            axis=1,
        )
        a, b = height(u)
        zed = scaled(a + b, scale_h).astype(bf16)
        hidden = jnp.tanh(dot(zed, weight_a)).astype(bf16)
        s = dot(hidden, weight_b)
        s = (s - jnp.clip(s, -0.25, 0.25)).astype(bf16)
        a, b = height(s)
        v = lane_groups(scaled(a - b, scale_h))
        v = jnp.concatenate([part.reshape(zc * n_row, SLOTS, LANES) for part in v], axis=1)
        send3[:, :, k] = v.astype(bf16).reshape(zc, n_row, TILE, LANES)

    def filter_modes(step, carry):
        for i in range(BATCH):
            filter_pair(step * BATCH + i)
        return carry

    for g in range(KGROUPS):
        for z in range(zc):
            for d in range(1, n_row):
                copy2(z, g, d).wait_recv()
        lax.fori_loop(g * per_k // BATCH, (g + 1) * per_k // BATCH, filter_modes, 0)
        for d in range(1, n_row):
            copy3(0, g, d).start()
    for z in range(1, zc):
        for g in range(KGROUPS):
            for d in range(1, n_row):
                copy3(z, g, d).start()
    for z in range(zc):
        recv3[z, row] = send3[z, row]

    for z in range(zc):
        for g in range(KGROUPS):
            for d in range(1, n_row):
                copy3(z, g, d).wait_recv()

        tiles = [recv3[z, own].reshape(TURN * SLOTS, LANES) for own in owners]
        swapped = dot(swap_ref[1], jnp.concatenate(tiles, axis=1)).astype(bf16)
        for ks, part in zip(turns, lane_groups(swapped)):
            turned[:, ks, :] = part.reshape(SLOTS, TURN, LANES)
        columns = []
        for i in range(per_col):
            re, im = swap_halves(turned[i].astype(f32), turned[per_col + i].astype(f32))
            columns.append(jnp.concatenate([re.astype(bf16), im.astype(bf16)], axis=0))
        cells = scaled(dot(inverse_ref[...], jnp.concatenate(columns, axis=1)), scale_w)
        for i, part in enumerate(lane_groups(cells)):
            part = (part + conv[z * per_col + i]).astype(bf16)
            send4[z, :, i] = part.reshape(n_col, cols_dev, LANES)
        for d in range(1, n_col):
            copy4(z, d).start()
        recv4[z, col] = send4[z, col]

    for ch in range(COL_CHUNKS):
        for d in range(1, n_col):
            copy4(ch, d).wait_recv()

        def finish_pair(i, carry, ch=ch):
            hp = ch * per_col + i
            for j in range(groups):
                lanes = slice(j * LANES, (j + 1) * LANES)
                lower, upper = swap_halves(
                    recv4[ch, 2 * j, i].astype(f32), recv4[ch, 2 * j + 1, i].astype(f32)
                )
                patches[hp, :, lanes] = (patches[hp, :, lanes].astype(f32) + lower).astype(bf16)
                patches[hp + pairs, :, lanes] = (
                    patches[hp + pairs, :, lanes].astype(f32) + upper
                ).astype(bf16)
            return carry

        lax.fori_loop(0, per_col, finish_pair, 0)
        for side in range(2):
            leave(ch, side).start()

    for ch in range(COL_CHUNKS):
        for d in range(1, n_col):
            copy1(ch, d).wait_send()
            copy4(ch, d).wait_send()
    for z in range(zc):
        for g in range(KGROUPS):
            for d in range(1, n_row):
                copy2(z, g, d).wait_send()
                copy3(z, g, d).wait_send()
    for side in range(2):
        copy_rim(side).wait_send()
    for ch in range(COL_CHUNKS):
        for side in range(2):
            leave(ch, side).wait()


def fused(patches, norm_gain, w_first, w_second, depth_kernel):
    n_row = lax.axis_size("row")
    n_col = lax.axis_size("col")
    rows_dev, cols_dev, chans = patches.shape
    grid_h, grid_w = rows_dev * n_row, cols_dev * n_col
    pairs, zc = rows_dev // 2, COL_CHUNKS
    per_col = pairs // COL_CHUNKS
    half = grid_w // 2
    kl = half // n_row
    tables = host_tables(grid_h, grid_w, n_row, rows_dev)
    bf16, f32 = jnp.bfloat16, jnp.float32
    anywhere = pl.BlockSpec(memory_space=pltpu.HBM)
    col_buffer = pltpu.VMEM((COL_CHUNKS, n_col, per_col, cols_dev, LANES), bf16)
    row_buffer = pltpu.VMEM((zc, n_row, kl // 2, TILE, LANES), bf16)
    col_sems = pltpu.SemaphoreType.DMA((COL_CHUNKS, n_col - 1))
    row_sems = pltpu.SemaphoreType.DMA((zc, KGROUPS, n_row - 1))
    rim_sems = pltpu.SemaphoreType.DMA((2,))
    operands = (
        patches,
        norm_gain.reshape(1, chans),
        w_first,
        w_second,
        depth_kernel,
        *[jnp.asarray(t) for t in tables],
    )
    return pl.pallas_call(
        functools.partial(
            mixing_kernel, n_row, n_col, exact_scale(grid_w)[1], exact_scale(grid_h)[1]
        ),
        out_shape=jax.ShapeDtypeStruct(patches.shape, bf16),
        in_specs=[anywhere] * 9,
        out_specs=anywhere,
        scratch_shapes=[
            *[pltpu.VMEM(v.shape, v.dtype) for v in operands],
            col_buffer,
            col_buffer,
            pltpu.VMEM((SLOTS, half, LANES), bf16),
            row_buffer,
            row_buffer,
            row_buffer,
            row_buffer,
            col_buffer,
            col_buffer,
            pltpu.VMEM((pairs, grid_w, LANES), f32),
            pltpu.VMEM((2, half, LANES), bf16),
            pltpu.VMEM((2, half, LANES), bf16),
            pltpu.VMEM((2, grid_w, LANES), bf16),
            col_sems,
            col_sems,
            row_sems,
            row_sems,
            row_sems,
            row_sems,
            col_sems,
            col_sems,
            rim_sems,
            rim_sems,
            pltpu.SemaphoreType.DMA((8,)),
            pltpu.SemaphoreType.DMA((COL_CHUNKS, 2)),
            pltpu.SemaphoreType.DMA((COL_CHUNKS, 2)),
        ],
        compiler_params=pltpu.CompilerParams(
            collective_id=0, has_side_effects=True, vmem_limit_bytes=62 * 1024 * 1024
        ),
        cost_estimate=pl.CostEstimate(flops=2_000_000_000, bytes_accessed=3_000_000, transcendentals=600_000),
    )(*operands)


def fits(patches, w_first):
    n_row, n_col = lax.axis_size("row"), lax.axis_size("col")
    rows_dev, cols_dev, chans = patches.shape
    blocks, width = w_first.shape[1:3]
    half = cols_dev * n_col // 2
    return (
        blocks == n_col
        and width == PAIR
        and chans % LANES == 0
        and rows_dev == COL_CHUNKS * SLOTS
        and cols_dev % TILE == 0
        and half == n_row * TILE
        and half % TURN == 0
    )


def local(patches, norm_gain, w_first, w_second, depth_kernel):
    plan = fused if fits(patches, w_first) else general
    return plan(patches, norm_gain, w_first, w_second, depth_kernel)


def solution(mesh):
    return jax.shard_map(
        local,
        mesh=mesh,
        in_specs=(P("row", "col", None), P(), P(), P(), P()),
        out_specs=P("row", "col", None),
        check_vma=False,
    )
```

```python
import functools
import math

import jax
import jax.numpy as jnp
import ml_dtypes
import numpy as np
from jax import lax
from jax.experimental import pallas as pl
from jax.experimental.pallas import tpu as pltpu
from jax.sharding import PartitionSpec as P


def with_halo(shard, sides, width):
    for axis, dim in sides:
        devices, length = (lax.axis_size(axis), shard.shape[dim])
        up = [(i, (i + 1) % devices) for i in range(devices)]
        down = [(j, i) for i, j in up]
        last = lax.slice_in_dim(shard, length - width, length, axis=dim)
        leading = lax.slice_in_dim(shard, 0, width, axis=dim)
        before = lax.ppermute(last, axis, up)
        after = lax.ppermute(leading, axis, down)
        shard = jnp.concatenate([before, shard, after], axis=dim)
    return shard


def phase_table(first_idx, second_idx, length):
    product = first_idx[:, None] * second_idx[None, :] % length
    phase = product.astype(jnp.float32) * (2.0 * math.pi / length)
    return (jnp.cos(phase).astype(jnp.bfloat16), jnp.sin(phase).astype(jnp.bfloat16))


def shrink(values):
    level = 0.25
    return jnp.where(
        values > level, values - level, jnp.where(values < -level, values + level, 0.0 * values)
    )


def block_product(left, weight):
    return jnp.einsum("qmbc,bcd->qmbd", left, weight, preferred_element_type=jnp.float32)


def general(patches, norm_gain, w_first, w_second, depth_kernel):
    n_row = lax.axis_size("row")
    n_col = lax.axis_size("col")
    rows_dev, cols_dev, chans = patches.shape
    patch_grid_height = rows_dev * n_row
    grid_w = cols_dev * n_col
    half = grid_w // 2
    blocks = w_first.shape[1]
    width = w_first.shape[2]
    width_factors = 1.0 / math.sqrt(grid_w)
    height_factors = 1.0 / math.sqrt(patch_grid_height)
    xf = patches.astype(jnp.float32)
    mean = jnp.mean(xf, axis=-1, keepdims=True)
    var = jnp.mean((xf - mean) ** 2, axis=-1, keepdims=True)
    normed = ((xf - mean) * lax.rsqrt(var + 1e-05) * norm_gain).astype(jnp.bfloat16)
    padded = with_halo(normed, (("row", 0), ("col", 1)), 1)
    conv = jnp.zeros((rows_dev, cols_dev, chans), jnp.float32)
    for i in range(3):
        for j in range(3):
            conv = conv + padded[i : i + rows_dev, j : j + cols_dev] * depth_kernel[i, j]
    strips = lax.all_to_all(normed, "col", split_axis=0, concat_axis=1, tiled=True)
    cos_w, sin_w = phase_table(
        jnp.arange(grid_w, dtype=jnp.int32), jnp.arange(half, dtype=jnp.int32), grid_w
    )
    forward_w = jnp.concatenate([cos_w, -sin_w], axis=1)
    spectrum_values = jnp.einsum(
        "hwc,wk->hkc", strips, forward_w, preferred_element_type=jnp.float32
    )
    spectrum_values = (spectrum_values * width_factors).astype(jnp.bfloat16)
    wre = spectrum_values[:, :half]
    wim = spectrum_values[:, half:]
    positions = jnp.arange(patch_grid_height, dtype=jnp.int32)
    across_re, across_im = (
        lax.all_to_all(wre, "col", split_axis=1, concat_axis=0, tiled=True),
        lax.all_to_all(wim, "col", split_axis=1, concat_axis=0, tiled=True),
    )
    full_re, full_im = (
        lax.all_to_all(across_re, "row", split_axis=1, concat_axis=0, tiled=True),
        lax.all_to_all(across_im, "row", split_axis=1, concat_axis=0, tiled=True),
    )
    cos_h, sin_h = phase_table(positions, positions, patch_grid_height)
    big_table = jnp.concatenate(
        [jnp.concatenate([cos_h, sin_h], axis=1), jnp.concatenate([-sin_h, cos_h], axis=1)], axis=0
    )
    stacked = jnp.concatenate([full_re, full_im], axis=0)
    spectrum = jnp.einsum("qp,pmc->qmc", big_table, stacked, preferred_element_type=jnp.float32)
    spectrum = (spectrum * height_factors).astype(jnp.bfloat16)
    modes = spectrum.shape[1]
    zre = spectrum[:patch_grid_height].reshape(patch_grid_height, modes, blocks, width)
    zim = spectrum[patch_grid_height:].reshape(patch_grid_height, modes, blocks, width)
    hre = jnp.tanh(block_product(zre, w_first[0]) - block_product(zim, w_first[1])).astype(
        jnp.bfloat16
    )
    him = jnp.tanh(block_product(zre, w_first[1]) + block_product(zim, w_first[0])).astype(
        jnp.bfloat16
    )
    spectrum_real = shrink(
        block_product(hre, w_second[0]) - block_product(him, w_second[1])
    ).astype(jnp.bfloat16)
    spectrum_imaginary = shrink(
        block_product(hre, w_second[1]) + block_product(him, w_second[0])
    ).astype(jnp.bfloat16)
    filtered = jnp.concatenate(
        [
            spectrum_real.reshape(patch_grid_height, modes, chans),
            spectrum_imaginary.reshape(patch_grid_height, modes, chans),
        ],
        axis=0,
    )
    inverse_transform = jnp.einsum(
        "qp,qmc->pmc", big_table, filtered, preferred_element_type=jnp.float32
    )
    inverse_transform = (inverse_transform * height_factors).astype(jnp.bfloat16)
    value_real = inverse_transform[:patch_grid_height]
    value_imaginary = inverse_transform[patch_grid_height:]
    part_re, part_im = (
        lax.all_to_all(value_real, "row", split_axis=0, concat_axis=1, tiled=True),
        lax.all_to_all(value_imaginary, "row", split_axis=0, concat_axis=1, tiled=True),
    )
    line_re, line_im = (
        lax.all_to_all(part_re, "col", split_axis=0, concat_axis=1, tiled=True),
        lax.all_to_all(part_im, "col", split_axis=0, concat_axis=1, tiled=True),
    )
    filter_coefficient = jnp.where(jnp.arange(half) == 0, 1.0, 2.0).astype(jnp.float32)
    inverse_w = jnp.concatenate(
        [
            (cos_w.astype(jnp.float32) * filter_coefficient).T,
            -(sin_w.astype(jnp.float32) * filter_coefficient).T,
        ],
        axis=0,
    ).astype(jnp.bfloat16)
    lines = jnp.concatenate([line_re, line_im], axis=1)
    spectral = jnp.einsum("hkc,kw->hwc", lines, inverse_w, preferred_element_type=jnp.float32)
    spectral = (spectral * width_factors).astype(jnp.bfloat16)
    home = lax.all_to_all(spectral, "col", split_axis=1, concat_axis=0, tiled=True)
    return (xf + home.astype(jnp.float32) + conv).astype(jnp.bfloat16)


LANES = 128
PAIR = 64
TILE = 16
SLOTS = 8
TURN = 32
COL_CHUNKS = 4
KGROUPS = 2
BATCH = 2


def row_order(n_row, rows_dev):
    pairs = rows_dev // 2
    zc = rows_dev // SLOTS
    per = pairs // zc
    order = []
    for z in range(zc):
        for s in range(n_row):
            for slot in range(SLOTS):
                order.append(s * rows_dev + (slot // per) * pairs + z * per + slot % per)
    return np.array(order)


def exact_scale(length):
    scale = 1.0 / math.sqrt(length)
    return (scale, 1.0) if math.frexp(scale)[0] == 0.5 else (1.0, scale)


def host_tables(grid_h, grid_w, n_row, rows_dev):
    half = grid_w // 2

    def table(a, b, n):
        phase = (np.outer(a, b) % n).astype(np.float32) * np.float32(2.0 * math.pi / n)
        bf16 = ml_dtypes.bfloat16
        cos, sin = (np.cos(phase).astype(bf16), np.sin(phase).astype(bf16))
        return cos.astype(np.float32), sin.astype(np.float32)

    cos_w, sin_w = table(np.arange(half), np.arange(grid_w), grid_w)
    weight = np.where(np.arange(half) == 0, 1.0, 2.0).astype(np.float32)[:, None]
    forward = np.concatenate([cos_w, -sin_w], axis=0)
    inverse = np.concatenate([cos_w * weight, -sin_w * weight], axis=0).T
    order = row_order(n_row, rows_dev)
    cos_h, sin_h = table(order, order, grid_h)
    swap = np.zeros((TURN, SLOTS, SLOTS, TURN), np.float32)
    for a in range(TURN):
        for b in range(SLOTS):
            swap[a, b, b, a] = 1.0
    swap = swap.reshape(TURN * SLOTS, TURN * SLOTS)
    cast = lambda v: v.astype(ml_dtypes.bfloat16)
    fold_w, fold_h = exact_scale(grid_w)[0], exact_scale(grid_h)[0]
    return (
        cast(forward * fold_w),
        cast(inverse * fold_w),
        cast(np.concatenate([cos_h, sin_h], axis=0) * fold_h),
        cast(np.stack([swap, swap.T])),
    )


def half_turn(x):
    parts = [pltpu.roll(part, PAIR, 1) for part in lane_groups(x)]
    return parts[0] if len(parts) == 1 else jnp.concatenate(parts, axis=1)


def lane_groups(x):
    return [x[:, i : i + LANES] for i in range(0, x.shape[1], LANES)]


def low_lanes(shape):
    return lax.broadcasted_iota(jnp.int32, shape, len(shape) - 1) % LANES < PAIR


def scaled(x, factor):
    return x if factor == 1.0 else x * factor


def swap_halves(a, b):
    low = low_lanes(a.shape)
    return jnp.where(low, a, half_turn(b)), jnp.where(low, half_turn(a), b)


def mixing_kernel(
    n_row,
    n_col,
    scale_w,
    scale_h,
    patches_hbm,
    gain_hbm,
    w_first_hbm,
    w_second_hbm,
    depth_hbm,
    forward_hbm,
    inverse_hbm,
    height_hbm,
    swap_hbm,
    out_hbm,
    patches,
    gain,
    w_first,
    w_second,
    depth,
    forward_ref,
    inverse_ref,
    height_ref,
    swap_ref,
    send1,
    recv1,
    turned,
    send2,
    recv2,
    send3,
    recv3,
    send4,
    recv4,
    conv,
    rim_send,
    rim_recv,
    rim,
    s1,
    r1,
    s2,
    r2,
    s3,
    r3,
    s4,
    r4,
    sh,
    rh,
    fetch_sem,
    patch_sem,
    out_sem,
):
    f32, bf16 = jnp.float32, jnp.bfloat16
    row, col = lax.axis_index("row"), lax.axis_index("col")
    rows_dev, cols_dev, chans = patches.shape
    pairs = rows_dev // 2
    per_col = pairs // COL_CHUNKS
    zc = COL_CHUNKS
    grid_w = cols_dev * n_col
    half = grid_w // 2
    kl = half // n_row
    per_k = kl // 2 // KGROUPS
    turns = [pl.ds(q * TURN, TURN) for q in range(half // TURN)]
    owners = [pl.ds(q * TURN // kl, TURN // kl) for q in range(half // TURN)]
    groups = chans // LANES

    def col_peer(d):
        return lax.rem(col + d, n_col)

    def row_peer(d):
        bits, peer, weight = d, 0, 1
        while weight < n_row:
            own = lax.rem(row // weight, 2)
            peer = peer + weight * (1 - own if bits % 2 else own)
            bits, weight = bits // 2, 2 * weight
        return peer

    near = list(range(1, n_row // 2))
    row_order_of = []
    for d in range(n_row // 2, n_row):
        row_order_of.append(d)
        if near:
            row_order_of.append(near.pop(0))

    def to_col(d):
        return {"col": col_peer(d)}

    def to_row(d):
        return {"row": row_peer(d)}

    def dot(a, b):
        return jnp.dot(a, b, preferred_element_type=f32)

    barrier = pltpu.get_barrier_semaphore()
    for d in range(1, n_col):
        pl.semaphore_signal(barrier, inc=1, device_id=to_col(d), device_id_type=pl.DeviceIdType.MESH)
    for d in range(1, n_row):
        pl.semaphore_signal(barrier, inc=1, device_id=to_row(d), device_id_type=pl.DeviceIdType.MESH)

    def chunk_rows(ch, side):
        return pl.ds(side * pairs + ch * per_col, per_col)

    def fetch_patches(ch, side):
        rows = chunk_rows(ch, side)
        return pltpu.make_async_copy(patches_hbm.at[rows], patches.at[rows], patch_sem.at[ch, side])

    def leave(ch, side):
        rows = chunk_rows(ch, side)
        return pltpu.make_async_copy(patches.at[rows], out_hbm.at[rows], out_sem.at[ch, side])

    operands = (
        (gain_hbm, gain),
        (forward_hbm, forward_ref),
        (swap_hbm, swap_ref),
        (w_first_hbm, w_first),
        (w_second_hbm, w_second),
        (depth_hbm, depth),
        (height_hbm, height_ref),
        (inverse_hbm, inverse_ref),
    )
    fetches = [
        pltpu.make_async_copy(src, dst, fetch_sem.at[i]) for i, (src, dst) in enumerate(operands)
    ]
    for side in range(2):
        fetch_patches(0, side).start()
    fetches[0].start()
    for ch in range(1, COL_CHUNKS):
        for side in range(2):
            fetch_patches(ch, side).start()
    for fetch in fetches[1:]:
        fetch.start()
    fetches[0].wait()

    def copy1(ch, d):
        return pltpu.make_async_remote_copy(
            src_ref=send1.at[ch, col_peer(d)],
            dst_ref=recv1.at[ch, col],
            send_sem=s1.at[ch, d - 1],
            recv_sem=r1.at[ch, d - 1],
            device_id=to_col(d),
            device_id_type=pl.DeviceIdType.MESH,
        )

    def copy2(z, g, d):
        ks = pl.ds(g * per_k, per_k)
        return pltpu.make_async_remote_copy(
            src_ref=send2.at[z, row_peer(d), ks],
            dst_ref=recv2.at[z, row, ks],
            send_sem=s2.at[z, g, d - 1],
            recv_sem=r2.at[z, g, d - 1],
            device_id=to_row(d),
            device_id_type=pl.DeviceIdType.MESH,
        )

    def copy3(z, g, d):
        ks = pl.ds(g * per_k, per_k)
        return pltpu.make_async_remote_copy(
            src_ref=send3.at[z, row_peer(d), ks],
            dst_ref=recv3.at[z, row, ks],
            send_sem=s3.at[z, g, d - 1],
            recv_sem=r3.at[z, g, d - 1],
            device_id=to_row(d),
            device_id_type=pl.DeviceIdType.MESH,
        )

    def copy4(ch, d):
        return pltpu.make_async_remote_copy(
            src_ref=send4.at[ch, col_peer(d)],
            dst_ref=recv4.at[ch, col],
            send_sem=s4.at[ch, d - 1],
            recv_sem=r4.at[ch, d - 1],
            device_id=to_col(d),
            device_id_type=pl.DeviceIdType.MESH,
        )

    def copy_rim(side):
        return pltpu.make_async_remote_copy(
            src_ref=rim_send.at[side],
            dst_ref=rim_recv.at[side],
            send_sem=sh.at[side],
            recv_sem=rh.at[side],
            device_id={"row": lax.rem(row + (1 if side == 0 else n_row - 1), n_row)},
            device_id_type=pl.DeviceIdType.MESH,
        )

    def normed_row(h):
        x = patches[h].astype(f32)
        mean = jnp.mean(x, axis=-1, keepdims=True)
        centred = x - mean
        var = jnp.mean(centred * centred, axis=-1, keepdims=True)
        return centred * lax.rsqrt(var + 1e-05) * gain[...]

    for ch in range(COL_CHUNKS):
        for side in range(2):
            fetch_patches(ch, side).wait()

        def norm_pair(i, carry, ch=ch):
            hp = ch * per_col + i
            lower, upper = normed_row(hp), normed_row(hp + pairs)
            for j in range(groups):
                lanes = slice(j * LANES, (j + 1) * LANES)
                even, odd = swap_halves(lower[:, lanes], upper[:, lanes])
                send1[ch, 2 * j, i] = even.astype(bf16)
                send1[ch, 2 * j + 1, i] = odd.astype(bf16)
            return carry

        lax.fori_loop(0, per_col, norm_pair, 0)
        if ch == 0:
            pl.semaphore_wait(barrier, n_col + n_row - 2)
        for d in range(1, n_col):
            copy1(ch, d).start()
        recv1[ch, col] = send1[ch, col]

    def line(ch, i):
        return recv1[ch, :, i].reshape(grid_w, LANES)

    for fetch in fetches[1:]:
        fetch.wait()
    for z in range(zc):
        for d in range(1, n_col):
            copy1(z, d).wait_recv()
        x = jnp.concatenate([line(z, i) for i in range(per_col)], axis=1)
        y = scaled(dot(forward_ref[...], x), scale_w)
        lower, upper = swap_halves(y[:half], y[half:])
        for i in range(per_col):
            turned[i] = lane_groups(lower)[i].astype(bf16)
            turned[per_col + i] = lane_groups(upper)[i].astype(bf16)
        tiles = [turned[:, ks, :].reshape(TURN * SLOTS, LANES) for ks in turns]
        swapped = dot(swap_ref[0], jnp.concatenate(tiles, axis=1)).astype(bf16)
        for own, part in zip(owners, lane_groups(swapped)):
            send2[z, own] = part.reshape(TURN // kl, kl // 2, TILE, LANES)
        for g in range(KGROUPS):
            for d in row_order_of:
                copy2(z, g, d).start()
        recv2[z, row] = send2[z, row]

    first = line(0, 0).astype(f32)
    final = line(COL_CHUNKS - 1, per_col - 1).astype(f32)
    rim_send[0] = swap_halves(final[:half], final[half:])[1].astype(bf16)
    rim_send[1] = swap_halves(first[:half], first[half:])[0].astype(bf16)
    for side in range(2):
        copy_rim(side).start()

    def complex_weight(ref):
        re, im = ref[0, col].astype(f32), ref[1, col].astype(f32)
        one = jnp.concatenate(
            [jnp.concatenate([re, im], axis=1), jnp.concatenate([-im, re], axis=1)], axis=0
        ).astype(bf16)
        none = jnp.zeros_like(one)
        return jnp.concatenate(
            [jnp.concatenate([one, none], axis=1), jnp.concatenate([none, one], axis=1)], axis=0
        )

    weight_a, weight_b = complex_weight(w_first), complex_weight(w_second)

    lane_group = pl.multiple_of((col // 2) * LANES, LANES)
    taps = []
    for i in range(3):
        own = depth[i, :, pl.ds(lane_group, LANES)]
        low = low_lanes(own.shape)
        other = half_turn(own)
        taps.append(
            jnp.where((col % 2) == 0, jnp.where(low, own, other), jnp.where(low, other, own))
        )
    def conv_pair(hp, above, here, below):
        total = None
        for j in range(3):
            part = None
            for i, rows in enumerate((above, here, below)):
                term = rows * taps[i][j : j + 1]
                part = term if part is None else part + term
            if j == 0:
                part = pltpu.roll(part, 1, 0)
            if j == 2:
                part = pltpu.roll(part, grid_w - 1, 0)
            total = part if total is None else total + part
        conv[hp] = total

    def at(hp):
        return line(hp // per_col, hp % per_col).astype(f32)

    def conv_inner(hp, carry):
        conv_pair(hp, at(hp - 1), at(hp), at(hp + 1))
        return carry

    lax.fori_loop(1, pairs - 1, conv_inner, 0)

    grid_h = rows_dev * n_row
    sign = jnp.where(low_lanes((1, 2 * LANES)), 1.0, -1.0)

    def height(u):
        both = dot(height_ref[...], u)
        return both[:grid_h], half_turn(both[grid_h:]) * sign

    def filter_pair(k):
        tile = recv2[:, :, k].astype(f32).reshape(zc * n_row, TILE, LANES)
        u = jnp.concatenate(
            [
                tile[:, i : i + SLOTS].reshape(grid_h, LANES).astype(bf16)
                for i in range(0, TILE, SLOTS)
            ],
            axis=1,
        )
        a, b = height(u)
        zed = scaled(a + b, scale_h).astype(bf16)
        hidden = jnp.tanh(dot(zed, weight_a)).astype(bf16)
        s = dot(hidden, weight_b)
        s = (s - jnp.clip(s, -0.25, 0.25)).astype(bf16)
        a, b = height(s)
        v = lane_groups(scaled(a - b, scale_h))
        v = jnp.concatenate([part.reshape(zc * n_row, SLOTS, LANES) for part in v], axis=1)
        send3[:, :, k] = v.astype(bf16).reshape(zc, n_row, TILE, LANES)

    def filter_modes(step, carry):
        for i in range(BATCH):
            filter_pair(step * BATCH + i)
        return carry

    for g in range(KGROUPS):
        for z in range(zc):
            for d in range(1, n_row):
                copy2(z, g, d).wait_recv()
        lax.fori_loop(g * per_k // BATCH, (g + 1) * per_k // BATCH, filter_modes, 0)
        for d in row_order_of:
            copy3(0, g, d).start()
    for z in range(1, zc):
        for g in range(KGROUPS):
            for d in row_order_of:
                copy3(z, g, d).start()
    for z in range(zc):
        recv3[z, row] = send3[z, row]

    for side in range(2):
        copy_rim(side).wait_recv()
    before = rim_recv[0].astype(f32)
    after = rim_recv[1].astype(f32)
    before = jnp.concatenate([before, half_turn(before)], axis=0)
    after = jnp.concatenate([half_turn(after), after], axis=0)
    low = low_lanes(before.shape)
    rim[0] = jnp.where(low, before, half_turn(at(pairs - 1))).astype(bf16)
    rim[1] = jnp.where(low, half_turn(at(0)), after).astype(bf16)

    conv_pair(0, rim[0].astype(f32), at(0), at(1))
    conv_pair(pairs - 1, at(pairs - 2), at(pairs - 1), rim[1].astype(f32))

    for z in range(zc):
        for g in range(KGROUPS):
            for d in range(1, n_row):
                copy3(z, g, d).wait_recv()

        tiles = [recv3[z, own].reshape(TURN * SLOTS, LANES) for own in owners]
        swapped = dot(swap_ref[1], jnp.concatenate(tiles, axis=1)).astype(bf16)
        for ks, part in zip(turns, lane_groups(swapped)):
            turned[:, ks, :] = part.reshape(SLOTS, TURN, LANES)
        columns = []
        for i in range(per_col):
            re, im = swap_halves(turned[i].astype(f32), turned[per_col + i].astype(f32))
            columns.append(jnp.concatenate([re.astype(bf16), im.astype(bf16)], axis=0))
        cells = scaled(dot(inverse_ref[...], jnp.concatenate(columns, axis=1)), scale_w)
        for i, part in enumerate(lane_groups(cells)):
            part = (part + conv[z * per_col + i]).astype(bf16)
            send4[z, :, i] = part.reshape(n_col, cols_dev, LANES)
        for d in range(1, n_col):
            copy4(z, d).start()
        recv4[z, col] = send4[z, col]

    for ch in range(COL_CHUNKS):
        for d in range(1, n_col):
            copy4(ch, d).wait_recv()

        def finish_pair(i, carry, ch=ch):
            hp = ch * per_col + i
            for j in range(groups):
                lanes = slice(j * LANES, (j + 1) * LANES)
                lower, upper = swap_halves(
                    recv4[ch, 2 * j, i].astype(f32), recv4[ch, 2 * j + 1, i].astype(f32)
                )
                patches[hp, :, lanes] = lower.astype(bf16)
                patches[hp + pairs, :, lanes] = upper.astype(bf16)
            return carry

        lax.fori_loop(0, per_col, finish_pair, 0)
        for side in range(2):
            leave(ch, side).start()

    for ch in range(COL_CHUNKS):
        for d in range(1, n_col):
            copy1(ch, d).wait_send()
            copy4(ch, d).wait_send()
    for z in range(zc):
        for g in range(KGROUPS):
            for d in range(1, n_row):
                copy2(z, g, d).wait_send()
                copy3(z, g, d).wait_send()
    for side in range(2):
        copy_rim(side).wait_send()
    for ch in range(COL_CHUNKS):
        for side in range(2):
            leave(ch, side).wait()


def fused(patches, norm_gain, w_first, w_second, depth_kernel):
    n_row = lax.axis_size("row")
    n_col = lax.axis_size("col")
    rows_dev, cols_dev, chans = patches.shape
    grid_h, grid_w = rows_dev * n_row, cols_dev * n_col
    pairs, zc = rows_dev // 2, COL_CHUNKS
    per_col = pairs // COL_CHUNKS
    half = grid_w // 2
    kl = half // n_row
    tables = host_tables(grid_h, grid_w, n_row, rows_dev)
    bf16, f32 = jnp.bfloat16, jnp.float32
    anywhere = pl.BlockSpec(memory_space=pltpu.HBM)
    col_buffer = pltpu.VMEM((COL_CHUNKS, n_col, per_col, cols_dev, LANES), bf16)
    row_buffer = pltpu.VMEM((zc, n_row, kl // 2, TILE, LANES), bf16)
    col_sems = pltpu.SemaphoreType.DMA((COL_CHUNKS, n_col - 1))
    row_sems = pltpu.SemaphoreType.DMA((zc, KGROUPS, n_row - 1))
    rim_sems = pltpu.SemaphoreType.DMA((2,))
    operands = (
        patches,
        norm_gain.reshape(1, chans),
        w_first,
        w_second,
        depth_kernel,
        *[jnp.asarray(t) for t in tables],
    )
    branches = pl.pallas_call(
        functools.partial(
            mixing_kernel, n_row, n_col, exact_scale(grid_w)[1], exact_scale(grid_h)[1]
        ),
        out_shape=jax.ShapeDtypeStruct(patches.shape, bf16),
        in_specs=[anywhere] * 9,
        out_specs=anywhere,
        scratch_shapes=[
            *[pltpu.VMEM(v.shape, v.dtype) for v in operands],
            col_buffer,
            col_buffer,
            pltpu.VMEM((SLOTS, half, LANES), bf16),
            row_buffer,
            row_buffer,
            row_buffer,
            row_buffer,
            col_buffer,
            col_buffer,
            pltpu.VMEM((pairs, grid_w, LANES), f32),
            pltpu.VMEM((2, half, LANES), bf16),
            pltpu.VMEM((2, half, LANES), bf16),
            pltpu.VMEM((2, grid_w, LANES), bf16),
            col_sems,
            col_sems,
            row_sems,
            row_sems,
            row_sems,
            row_sems,
            col_sems,
            col_sems,
            rim_sems,
            rim_sems,
            pltpu.SemaphoreType.DMA((8,)),
            pltpu.SemaphoreType.DMA((COL_CHUNKS, 2)),
            pltpu.SemaphoreType.DMA((COL_CHUNKS, 2)),
        ],
        compiler_params=pltpu.CompilerParams(
            collective_id=0, has_side_effects=True, vmem_limit_bytes=62 * 1024 * 1024
        ),
        cost_estimate=pl.CostEstimate(flops=2_000_000_000, bytes_accessed=3_000_000, transcendentals=600_000),
    )(*operands)
    return (patches.astype(f32) + branches.astype(f32)).astype(bf16)


def fits(patches, w_first):
    n_row, n_col = lax.axis_size("row"), lax.axis_size("col")
    rows_dev, cols_dev, chans = patches.shape
    blocks, width = w_first.shape[1:3]
    half = cols_dev * n_col // 2
    return (
        blocks == n_col
        and width == PAIR
        and chans % LANES == 0
        and rows_dev == COL_CHUNKS * SLOTS
        and cols_dev % TILE == 0
        and half == n_row * TILE
        and half % TURN == 0
        and n_row & (n_row - 1) == 0
    )


def local(patches, norm_gain, w_first, w_second, depth_kernel):
    plan = fused if fits(patches, w_first) else general
    return plan(patches, norm_gain, w_first, w_second, depth_kernel)


def solution(mesh):
    return jax.shard_map(
        local,
        mesh=mesh,
        in_specs=(P("row", "col", None), P(), P(), P(), P()),
        out_specs=P("row", "col", None),
        check_vma=False,
    )
```

```python
import functools
import math

import jax
import jax.numpy as jnp
import ml_dtypes
import numpy as np
from jax import lax
from jax.experimental import pallas as pl
from jax.experimental.pallas import tpu as pltpu
from jax.sharding import PartitionSpec as P


def with_halo(shard, sides, width):
    for axis, dim in sides:
        devices, length = (lax.axis_size(axis), shard.shape[dim])
        up = [(i, (i + 1) % devices) for i in range(devices)]
        down = [(j, i) for i, j in up]
        last = lax.slice_in_dim(shard, length - width, length, axis=dim)
        leading = lax.slice_in_dim(shard, 0, width, axis=dim)
        before = lax.ppermute(last, axis, up)
        after = lax.ppermute(leading, axis, down)
        shard = jnp.concatenate([before, shard, after], axis=dim)
    return shard


def phase_table(first_idx, second_idx, length):
    product = first_idx[:, None] * second_idx[None, :] % length
    phase = product.astype(jnp.float32) * (2.0 * math.pi / length)
    return (jnp.cos(phase).astype(jnp.bfloat16), jnp.sin(phase).astype(jnp.bfloat16))


def shrink(values):
    level = 0.25
    return jnp.where(
        values > level, values - level, jnp.where(values < -level, values + level, 0.0 * values)
    )


def block_product(left, weight):
    return jnp.einsum("qmbc,bcd->qmbd", left, weight, preferred_element_type=jnp.float32)


def general(patches, norm_gain, w_first, w_second, depth_kernel):
    n_row = lax.axis_size("row")
    n_col = lax.axis_size("col")
    rows_dev, cols_dev, chans = patches.shape
    patch_grid_height = rows_dev * n_row
    grid_w = cols_dev * n_col
    half = grid_w // 2
    blocks = w_first.shape[1]
    width = w_first.shape[2]
    width_factors = 1.0 / math.sqrt(grid_w)
    height_factors = 1.0 / math.sqrt(patch_grid_height)
    xf = patches.astype(jnp.float32)
    mean = jnp.mean(xf, axis=-1, keepdims=True)
    var = jnp.mean((xf - mean) ** 2, axis=-1, keepdims=True)
    normed = ((xf - mean) * lax.rsqrt(var + 1e-05) * norm_gain).astype(jnp.bfloat16)
    padded = with_halo(normed, (("row", 0), ("col", 1)), 1)
    conv = jnp.zeros((rows_dev, cols_dev, chans), jnp.float32)
    for i in range(3):
        for j in range(3):
            conv = conv + padded[i : i + rows_dev, j : j + cols_dev] * depth_kernel[i, j]
    strips = lax.all_to_all(normed, "col", split_axis=0, concat_axis=1, tiled=True)
    cos_w, sin_w = phase_table(
        jnp.arange(grid_w, dtype=jnp.int32), jnp.arange(half, dtype=jnp.int32), grid_w
    )
    forward_w = jnp.concatenate([cos_w, -sin_w], axis=1)
    spectrum_values = jnp.einsum(
        "hwc,wk->hkc", strips, forward_w, preferred_element_type=jnp.float32
    )
    spectrum_values = (spectrum_values * width_factors).astype(jnp.bfloat16)
    wre = spectrum_values[:, :half]
    wim = spectrum_values[:, half:]
    positions = jnp.arange(patch_grid_height, dtype=jnp.int32)
    across_re, across_im = (
        lax.all_to_all(wre, "col", split_axis=1, concat_axis=0, tiled=True),
        lax.all_to_all(wim, "col", split_axis=1, concat_axis=0, tiled=True),
    )
    full_re, full_im = (
        lax.all_to_all(across_re, "row", split_axis=1, concat_axis=0, tiled=True),
        lax.all_to_all(across_im, "row", split_axis=1, concat_axis=0, tiled=True),
    )
    cos_h, sin_h = phase_table(positions, positions, patch_grid_height)
    big_table = jnp.concatenate(
        [jnp.concatenate([cos_h, sin_h], axis=1), jnp.concatenate([-sin_h, cos_h], axis=1)], axis=0
    )
    stacked = jnp.concatenate([full_re, full_im], axis=0)
    spectrum = jnp.einsum("qp,pmc->qmc", big_table, stacked, preferred_element_type=jnp.float32)
    spectrum = (spectrum * height_factors).astype(jnp.bfloat16)
    modes = spectrum.shape[1]
    zre = spectrum[:patch_grid_height].reshape(patch_grid_height, modes, blocks, width)
    zim = spectrum[patch_grid_height:].reshape(patch_grid_height, modes, blocks, width)
    hre = jnp.tanh(block_product(zre, w_first[0]) - block_product(zim, w_first[1])).astype(
        jnp.bfloat16
    )
    him = jnp.tanh(block_product(zre, w_first[1]) + block_product(zim, w_first[0])).astype(
        jnp.bfloat16
    )
    spectrum_real = shrink(
        block_product(hre, w_second[0]) - block_product(him, w_second[1])
    ).astype(jnp.bfloat16)
    spectrum_imaginary = shrink(
        block_product(hre, w_second[1]) + block_product(him, w_second[0])
    ).astype(jnp.bfloat16)
    filtered = jnp.concatenate(
        [
            spectrum_real.reshape(patch_grid_height, modes, chans),
            spectrum_imaginary.reshape(patch_grid_height, modes, chans),
        ],
        axis=0,
    )
    inverse_transform = jnp.einsum(
        "qp,qmc->pmc", big_table, filtered, preferred_element_type=jnp.float32
    )
    inverse_transform = (inverse_transform * height_factors).astype(jnp.bfloat16)
    value_real = inverse_transform[:patch_grid_height]
    value_imaginary = inverse_transform[patch_grid_height:]
    part_re, part_im = (
        lax.all_to_all(value_real, "row", split_axis=0, concat_axis=1, tiled=True),
        lax.all_to_all(value_imaginary, "row", split_axis=0, concat_axis=1, tiled=True),
    )
    line_re, line_im = (
        lax.all_to_all(part_re, "col", split_axis=0, concat_axis=1, tiled=True),
        lax.all_to_all(part_im, "col", split_axis=0, concat_axis=1, tiled=True),
    )
    filter_coefficient = jnp.where(jnp.arange(half) == 0, 1.0, 2.0).astype(jnp.float32)
    inverse_w = jnp.concatenate(
        [
            (cos_w.astype(jnp.float32) * filter_coefficient).T,
            -(sin_w.astype(jnp.float32) * filter_coefficient).T,
        ],
        axis=0,
    ).astype(jnp.bfloat16)
    lines = jnp.concatenate([line_re, line_im], axis=1)
    spectral = jnp.einsum("hkc,kw->hwc", lines, inverse_w, preferred_element_type=jnp.float32)
    spectral = (spectral * width_factors).astype(jnp.bfloat16)
    home = lax.all_to_all(spectral, "col", split_axis=1, concat_axis=0, tiled=True)
    return (xf + home.astype(jnp.float32) + conv).astype(jnp.bfloat16)


LANES = 128
PAIR = 64
TILE = 16
SLOTS = 8
TURN = 32
COL_CHUNKS = 4
KGROUPS = 2
BATCH = 2


def row_order(n_row, rows_dev):
    pairs = rows_dev // 2
    zc = rows_dev // SLOTS
    per = pairs // zc
    order = []
    for z in range(zc):
        for s in range(n_row):
            for slot in range(SLOTS):
                order.append(s * rows_dev + (slot // per) * pairs + z * per + slot % per)
    return np.array(order)


def exact_scale(length):
    scale = 1.0 / math.sqrt(length)
    return (scale, 1.0) if math.frexp(scale)[0] == 0.5 else (1.0, scale)


def host_tables(grid_h, grid_w, n_row, rows_dev):
    half = grid_w // 2

    def table(a, b, n):
        phase = (np.outer(a, b) % n).astype(np.float32) * np.float32(2.0 * math.pi / n)
        bf16 = ml_dtypes.bfloat16
        cos, sin = (np.cos(phase).astype(bf16), np.sin(phase).astype(bf16))
        return cos.astype(np.float32), sin.astype(np.float32)

    cos_w, sin_w = table(np.arange(half), np.arange(grid_w), grid_w)
    weight = np.where(np.arange(half) == 0, 1.0, 2.0).astype(np.float32)[:, None]
    forward = np.concatenate([cos_w, -sin_w], axis=0)
    inverse = np.concatenate([cos_w * weight, -sin_w * weight], axis=0).T
    order = row_order(n_row, rows_dev)
    cos_h, sin_h = table(order, order, grid_h)
    swap = np.zeros((TURN, SLOTS, SLOTS, TURN), np.float32)
    for a in range(TURN):
        for b in range(SLOTS):
            swap[a, b, b, a] = 1.0
    swap = swap.reshape(TURN * SLOTS, TURN * SLOTS)
    cast = lambda v: v.astype(ml_dtypes.bfloat16)
    fold_w, fold_h = exact_scale(grid_w)[0], exact_scale(grid_h)[0]
    return (
        cast(forward * fold_w),
        cast(inverse * fold_w),
        cast(np.concatenate([cos_h, sin_h], axis=0) * fold_h),
        cast(np.stack([swap, swap.T])),
    )


def half_turn(x):
    parts = [pltpu.roll(part, PAIR, 1) for part in lane_groups(x)]
    return parts[0] if len(parts) == 1 else jnp.concatenate(parts, axis=1)


def lane_groups(x):
    return [x[:, i : i + LANES] for i in range(0, x.shape[1], LANES)]


def low_lanes(shape):
    return lax.broadcasted_iota(jnp.int32, shape, len(shape) - 1) % LANES < PAIR


def scaled(x, factor):
    return x if factor == 1.0 else x * factor


def swap_halves(a, b):
    low = low_lanes(a.shape)
    return jnp.where(low, a, half_turn(b)), jnp.where(low, half_turn(a), b)


def mixing_kernel(
    n_row,
    n_col,
    scale_w,
    scale_h,
    patches_hbm,
    gain_hbm,
    w_first_hbm,
    w_second_hbm,
    depth_hbm,
    forward_hbm,
    inverse_hbm,
    height_hbm,
    swap_hbm,
    out_hbm,
    patches,
    gain,
    w_first,
    w_second,
    depth,
    forward_ref,
    inverse_ref,
    height_ref,
    swap_ref,
    send1,
    recv1,
    turned,
    send2,
    recv2,
    send3,
    recv3,
    send4,
    recv4,
    conv,
    rim_send,
    rim_recv,
    rim,
    s1,
    r1,
    s2,
    r2,
    s3,
    r3,
    s4,
    r4,
    sh,
    rh,
    fetch_sem,
    patch_sem,
    out_sem,
):
    f32, bf16 = jnp.float32, jnp.bfloat16
    row, col = lax.axis_index("row"), lax.axis_index("col")
    rows_dev, cols_dev, chans = patches.shape
    pairs = rows_dev // 2
    per_col = pairs // COL_CHUNKS
    zc = COL_CHUNKS
    grid_w = cols_dev * n_col
    half = grid_w // 2
    kl = half // n_row
    per_k = kl // 2 // KGROUPS
    turns = [pl.ds(q * TURN, TURN) for q in range(half // TURN)]
    owners = [pl.ds(q * TURN // kl, TURN // kl) for q in range(half // TURN)]
    groups = chans // LANES

    def col_peer(d):
        return lax.rem(col + d, n_col)

    def row_peer(d):
        bits, peer, weight = d, 0, 1
        while weight < n_row:
            own = lax.rem(row // weight, 2)
            peer = peer + weight * (1 - own if bits % 2 else own)
            bits, weight = bits // 2, 2 * weight
        return peer

    near = list(range(1, n_row // 2))
    row_order_of = []
    for d in range(n_row // 2, n_row):
        row_order_of.append(d)
        if near:
            row_order_of.append(near.pop(0))

    def to_col(d):
        return {"col": col_peer(d)}

    def to_row(d):
        return {"row": row_peer(d)}

    def dot(a, b):
        return jnp.dot(a, b, preferred_element_type=f32)

    barrier = pltpu.get_barrier_semaphore()
    for d in range(1, n_col):
        pl.semaphore_signal(barrier, inc=1, device_id=to_col(d), device_id_type=pl.DeviceIdType.MESH)
    for d in range(1, n_row):
        pl.semaphore_signal(barrier, inc=1, device_id=to_row(d), device_id_type=pl.DeviceIdType.MESH)

    def chunk_rows(ch, side):
        return pl.ds(side * pairs + ch * per_col, per_col)

    def fetch_patches(ch, side):
        rows = chunk_rows(ch, side)
        return pltpu.make_async_copy(patches_hbm.at[rows], patches.at[rows], patch_sem.at[ch, side])

    def leave(ch, side):
        rows = chunk_rows(ch, side)
        return pltpu.make_async_copy(patches.at[rows], out_hbm.at[rows], out_sem.at[ch, side])

    operands = (
        (gain_hbm, gain),
        (forward_hbm, forward_ref),
        (swap_hbm, swap_ref),
        (w_first_hbm, w_first),
        (w_second_hbm, w_second),
        (depth_hbm, depth),
        (height_hbm, height_ref),
        (inverse_hbm, inverse_ref),
    )
    fetches = [
        pltpu.make_async_copy(src, dst, fetch_sem.at[i]) for i, (src, dst) in enumerate(operands)
    ]
    for side in range(2):
        fetch_patches(0, side).start()
    fetches[0].start()
    for ch in range(1, COL_CHUNKS):
        for side in range(2):
            fetch_patches(ch, side).start()
    for fetch in fetches[1:]:
        fetch.start()
    fetches[0].wait()

    def copy1(ch, d):
        return pltpu.make_async_remote_copy(
            src_ref=send1.at[ch, col_peer(d)],
            dst_ref=recv1.at[ch, col],
            send_sem=s1.at[ch, d - 1],
            recv_sem=r1.at[ch, d - 1],
            device_id=to_col(d),
            device_id_type=pl.DeviceIdType.MESH,
        )

    def copy2(z, g, d):
        ks = pl.ds(g * per_k, per_k)
        return pltpu.make_async_remote_copy(
            src_ref=send2.at[z, row_peer(d), ks],
            dst_ref=recv2.at[z, row, ks],
            send_sem=s2.at[z, g, d - 1],
            recv_sem=r2.at[z, g, d - 1],
            device_id=to_row(d),
            device_id_type=pl.DeviceIdType.MESH,
        )

    def copy3(z, g, d):
        ks = pl.ds(g * per_k, per_k)
        return pltpu.make_async_remote_copy(
            src_ref=send3.at[z, row_peer(d), ks],
            dst_ref=recv3.at[z, row, ks],
            send_sem=s3.at[z, g, d - 1],
            recv_sem=r3.at[z, g, d - 1],
            device_id=to_row(d),
            device_id_type=pl.DeviceIdType.MESH,
        )

    def copy4(ch, d):
        return pltpu.make_async_remote_copy(
            src_ref=send4.at[ch, col_peer(d)],
            dst_ref=recv4.at[ch, col],
            send_sem=s4.at[ch, d - 1],
            recv_sem=r4.at[ch, d - 1],
            device_id=to_col(d),
            device_id_type=pl.DeviceIdType.MESH,
        )

    def copy_rim(side):
        return pltpu.make_async_remote_copy(
            src_ref=rim_send.at[side],
            dst_ref=rim_recv.at[side],
            send_sem=sh.at[side],
            recv_sem=rh.at[side],
            device_id={"row": lax.rem(row + (1 if side == 0 else n_row - 1), n_row)},
            device_id_type=pl.DeviceIdType.MESH,
        )

    def normed_row(h):
        x = patches[h].astype(f32)
        mean = jnp.mean(x, axis=-1, keepdims=True)
        centred = x - mean
        var = jnp.mean(centred * centred, axis=-1, keepdims=True)
        return centred * lax.rsqrt(var + 1e-05) * gain[...]

    def norm_chunk(ch):
        for side in range(2):
            fetch_patches(ch, side).wait()

        def norm_pair(i, carry):
            hp = ch * per_col + i
            lower, upper = normed_row(hp), normed_row(hp + pairs)
            for j in range(groups):
                lanes = slice(j * LANES, (j + 1) * LANES)
                even, odd = swap_halves(lower[:, lanes], upper[:, lanes])
                send1[ch, 2 * j, i] = even.astype(bf16)
                send1[ch, 2 * j + 1, i] = odd.astype(bf16)
            return carry

        lax.fori_loop(0, per_col, norm_pair, 0, unroll=2)
        if ch == 0:
            pl.semaphore_wait(barrier, n_col + n_row - 2)
        for d in range(1, n_col):
            copy1(ch, d).start()
        recv1[ch, col] = send1[ch, col]

    norm_chunk(0)
    norm_chunk(1)

    def line(ch, i):
        return recv1[ch, :, i].reshape(grid_w, LANES)

    for fetch in fetches[1:]:
        fetch.wait()
    for z in range(zc):
        for d in range(1, n_col):
            copy1(z, d).wait_recv()
        x = jnp.concatenate([line(z, i) for i in range(per_col)], axis=1)
        y = scaled(dot(forward_ref[...], x), scale_w)
        lower, upper = swap_halves(y[:half], y[half:])
        for i in range(per_col):
            turned[i] = lane_groups(lower)[i].astype(bf16)
            turned[per_col + i] = lane_groups(upper)[i].astype(bf16)
        tiles = [turned[:, ks, :].reshape(TURN * SLOTS, LANES) for ks in turns]
        swapped = dot(swap_ref[0], jnp.concatenate(tiles, axis=1)).astype(bf16)
        for own, part in zip(owners, lane_groups(swapped)):
            send2[z, own] = part.reshape(TURN // kl, kl // 2, TILE, LANES)
        for g in range(KGROUPS):
            for d in row_order_of:
                copy2(z, g, d).start()
        recv2[z, row] = send2[z, row]
        if z + 2 < COL_CHUNKS:
            norm_chunk(z + 2)

    first = line(0, 0).astype(f32)
    final = line(COL_CHUNKS - 1, per_col - 1).astype(f32)
    rim_send[0] = swap_halves(final[:half], final[half:])[1].astype(bf16)
    rim_send[1] = swap_halves(first[:half], first[half:])[0].astype(bf16)
    for side in range(2):
        copy_rim(side).start()

    def complex_weight(ref):
        re, im = ref[0, col].astype(f32), ref[1, col].astype(f32)
        one = jnp.concatenate(
            [jnp.concatenate([re, im], axis=1), jnp.concatenate([-im, re], axis=1)], axis=0
        ).astype(bf16)
        none = jnp.zeros_like(one)
        return jnp.concatenate(
            [jnp.concatenate([one, none], axis=1), jnp.concatenate([none, one], axis=1)], axis=0
        )

    weight_a, weight_b = complex_weight(w_first), complex_weight(w_second)

    lane_group = pl.multiple_of((col // 2) * LANES, LANES)
    taps = []
    for i in range(3):
        own = depth[i, :, pl.ds(lane_group, LANES)]
        low = low_lanes(own.shape)
        other = half_turn(own)
        taps.append(
            jnp.where((col % 2) == 0, jnp.where(low, own, other), jnp.where(low, other, own))
        )
    def conv_pair(hp, above, here, below):
        total = None
        for j in range(3):
            part = None
            for i, rows in enumerate((above, here, below)):
                term = rows * taps[i][j : j + 1]
                part = term if part is None else part + term
            if j == 0:
                part = pltpu.roll(part, 1, 0)
            if j == 2:
                part = pltpu.roll(part, grid_w - 1, 0)
            total = part if total is None else total + part
        conv[hp] = total

    def at(hp):
        return line(hp // per_col, hp % per_col).astype(f32)

    def conv_inner(hp, carry):
        conv_pair(hp, at(hp - 1), at(hp), at(hp + 1))
        return carry

    lax.fori_loop(1, pairs - 1, conv_inner, 0)

    grid_h = rows_dev * n_row
    sign = jnp.where(low_lanes((1, 2 * LANES)), 1.0, -1.0)

    def height(u):
        both = dot(height_ref[...], u)
        return both[:grid_h], half_turn(both[grid_h:]) * sign

    def filter_pair(k):
        tile = recv2[:, :, k].astype(f32).reshape(zc * n_row, TILE, LANES)
        u = jnp.concatenate(
            [
                tile[:, i : i + SLOTS].reshape(grid_h, LANES).astype(bf16)
                for i in range(0, TILE, SLOTS)
            ],
            axis=1,
        )
        a, b = height(u)
        zed = scaled(a + b, scale_h).astype(bf16)
        hidden = jnp.tanh(dot(zed, weight_a)).astype(bf16)
        s = dot(hidden, weight_b)
        s = (s - jnp.clip(s, -0.25, 0.25)).astype(bf16)
        a, b = height(s)
        v = lane_groups(scaled(a - b, scale_h))
        v = jnp.concatenate([part.reshape(zc * n_row, SLOTS, LANES) for part in v], axis=1)
        send3[:, :, k] = v.astype(bf16).reshape(zc, n_row, TILE, LANES)

    def filter_modes(step, carry):
        for i in range(BATCH):
            filter_pair(step * BATCH + i)
        return carry

    for g in range(KGROUPS):
        for z in range(zc):
            for d in range(1, n_row):
                copy2(z, g, d).wait_recv()
        lax.fori_loop(g * per_k // BATCH, (g + 1) * per_k // BATCH, filter_modes, 0)
        for d in row_order_of:
            copy3(0, g, d).start()
    for z in range(1, zc):
        for g in range(KGROUPS):
            for d in row_order_of:
                copy3(z, g, d).start()
    for z in range(zc):
        recv3[z, row] = send3[z, row]

    for side in range(2):
        copy_rim(side).wait_recv()
    before = rim_recv[0].astype(f32)
    after = rim_recv[1].astype(f32)
    before = jnp.concatenate([before, half_turn(before)], axis=0)
    after = jnp.concatenate([half_turn(after), after], axis=0)
    low = low_lanes(before.shape)
    rim[0] = jnp.where(low, before, half_turn(at(pairs - 1))).astype(bf16)
    rim[1] = jnp.where(low, half_turn(at(0)), after).astype(bf16)

    conv_pair(0, rim[0].astype(f32), at(0), at(1))
    conv_pair(pairs - 1, at(pairs - 2), at(pairs - 1), rim[1].astype(f32))

    def finish(ch):
        for d in range(1, n_col):
            copy4(ch, d).wait_recv()

        def finish_pair(i, carry):
            hp = ch * per_col + i
            for j in range(groups):
                lanes = slice(j * LANES, (j + 1) * LANES)
                lower, upper = swap_halves(
                    recv4[ch, 2 * j, i].astype(f32), recv4[ch, 2 * j + 1, i].astype(f32)
                )
                patches[hp, :, lanes] = (patches[hp, :, lanes].astype(f32) + lower).astype(bf16)
                patches[hp + pairs, :, lanes] = (
                    patches[hp + pairs, :, lanes].astype(f32) + upper
                ).astype(bf16)
            return carry

        lax.fori_loop(0, per_col, finish_pair, 0, unroll=2)
        for side in range(2):
            leave(ch, side).start()

    for z in range(zc):
        for g in range(KGROUPS):
            for d in range(1, n_row):
                copy3(z, g, d).wait_recv()

        tiles = [recv3[z, own].reshape(TURN * SLOTS, LANES) for own in owners]
        swapped = dot(swap_ref[1], jnp.concatenate(tiles, axis=1)).astype(bf16)
        for ks, part in zip(turns, lane_groups(swapped)):
            turned[:, ks, :] = part.reshape(SLOTS, TURN, LANES)
        columns = []
        for i in range(per_col):
            re, im = swap_halves(turned[i].astype(f32), turned[per_col + i].astype(f32))
            columns.append(jnp.concatenate([re.astype(bf16), im.astype(bf16)], axis=0))
        cells = scaled(dot(inverse_ref[...], jnp.concatenate(columns, axis=1)), scale_w)
        for i, part in enumerate(lane_groups(cells)):
            part = (part + conv[z * per_col + i]).astype(bf16)
            send4[z, :, i] = part.reshape(n_col, cols_dev, LANES)
        for d in range(1, n_col):
            copy4(z, d).start()
        recv4[z, col] = send4[z, col]
        if z > 0:
            finish(z - 1)

    finish(zc - 1)

    for ch in range(COL_CHUNKS):
        for d in range(1, n_col):
            copy1(ch, d).wait_send()
            copy4(ch, d).wait_send()
    for z in range(zc):
        for g in range(KGROUPS):
            for d in range(1, n_row):
                copy2(z, g, d).wait_send()
                copy3(z, g, d).wait_send()
    for side in range(2):
        copy_rim(side).wait_send()
    for ch in range(COL_CHUNKS):
        for side in range(2):
            leave(ch, side).wait()


def fused(patches, norm_gain, w_first, w_second, depth_kernel):
    n_row = lax.axis_size("row")
    n_col = lax.axis_size("col")
    rows_dev, cols_dev, chans = patches.shape
    grid_h, grid_w = rows_dev * n_row, cols_dev * n_col
    pairs, zc = rows_dev // 2, COL_CHUNKS
    per_col = pairs // COL_CHUNKS
    half = grid_w // 2
    kl = half // n_row
    tables = host_tables(grid_h, grid_w, n_row, rows_dev)
    bf16, f32 = jnp.bfloat16, jnp.float32
    anywhere = pl.BlockSpec(memory_space=pltpu.HBM)
    col_buffer = pltpu.VMEM((COL_CHUNKS, n_col, per_col, cols_dev, LANES), bf16)
    row_buffer = pltpu.VMEM((zc, n_row, kl // 2, TILE, LANES), bf16)
    col_sems = pltpu.SemaphoreType.DMA((COL_CHUNKS, n_col - 1))
    row_sems = pltpu.SemaphoreType.DMA((zc, KGROUPS, n_row - 1))
    rim_sems = pltpu.SemaphoreType.DMA((2,))
    operands = (
        patches,
        norm_gain.reshape(1, chans),
        w_first,
        w_second,
        depth_kernel,
        *[jnp.asarray(t) for t in tables],
    )
    return pl.pallas_call(
        functools.partial(
            mixing_kernel, n_row, n_col, exact_scale(grid_w)[1], exact_scale(grid_h)[1]
        ),
        out_shape=jax.ShapeDtypeStruct(patches.shape, bf16),
        in_specs=[anywhere] * 9,
        out_specs=anywhere,
        scratch_shapes=[
            *[pltpu.VMEM(v.shape, v.dtype) for v in operands],
            col_buffer,
            col_buffer,
            pltpu.VMEM((SLOTS, half, LANES), bf16),
            row_buffer,
            row_buffer,
            row_buffer,
            row_buffer,
            col_buffer,
            col_buffer,
            pltpu.VMEM((pairs, grid_w, LANES), f32),
            pltpu.VMEM((2, half, LANES), bf16),
            pltpu.VMEM((2, half, LANES), bf16),
            pltpu.VMEM((2, grid_w, LANES), bf16),
            col_sems,
            col_sems,
            row_sems,
            row_sems,
            row_sems,
            row_sems,
            col_sems,
            col_sems,
            rim_sems,
            rim_sems,
            pltpu.SemaphoreType.DMA((8,)),
            pltpu.SemaphoreType.DMA((COL_CHUNKS, 2)),
            pltpu.SemaphoreType.DMA((COL_CHUNKS, 2)),
        ],
        compiler_params=pltpu.CompilerParams(
            collective_id=0, has_side_effects=True, vmem_limit_bytes=62 * 1024 * 1024
        ),
        cost_estimate=pl.CostEstimate(flops=2_000_000_000, bytes_accessed=3_000_000, transcendentals=600_000),
    )(*operands)


def fits(patches, w_first):
    n_row, n_col = lax.axis_size("row"), lax.axis_size("col")
    rows_dev, cols_dev, chans = patches.shape
    blocks, width = w_first.shape[1:3]
    half = cols_dev * n_col // 2
    return (
        blocks == n_col
        and width == PAIR
        and chans % LANES == 0
        and rows_dev == COL_CHUNKS * SLOTS
        and cols_dev % TILE == 0
        and half == n_row * TILE
        and half % TURN == 0
        and n_row & (n_row - 1) == 0
    )


def local(patches, norm_gain, w_first, w_second, depth_kernel):
    plan = fused if fits(patches, w_first) else general
    return plan(patches, norm_gain, w_first, w_second, depth_kernel)


def solution(mesh):
    return jax.shard_map(
        local,
        mesh=mesh,
        in_specs=(P("row", "col", None), P(), P(), P(), P()),
        out_specs=P("row", "col", None),
        check_vma=False,
    )
```

```python
import functools
import math

import jax
import jax.numpy as jnp
import ml_dtypes
import numpy as np
from jax import lax
from jax.experimental import pallas as pl
from jax.experimental.pallas import tpu as pltpu
from jax.sharding import PartitionSpec as P


def with_halo(shard, sides, width):
    for axis, dim in sides:
        devices, length = (lax.axis_size(axis), shard.shape[dim])
        up = [(i, (i + 1) % devices) for i in range(devices)]
        down = [(j, i) for i, j in up]
        last = lax.slice_in_dim(shard, length - width, length, axis=dim)
        leading = lax.slice_in_dim(shard, 0, width, axis=dim)
        before = lax.ppermute(last, axis, up)
        after = lax.ppermute(leading, axis, down)
        shard = jnp.concatenate([before, shard, after], axis=dim)
    return shard


def phase_table(first_idx, second_idx, length):
    product = first_idx[:, None] * second_idx[None, :] % length
    phase = product.astype(jnp.float32) * (2.0 * math.pi / length)
    return (jnp.cos(phase).astype(jnp.bfloat16), jnp.sin(phase).astype(jnp.bfloat16))


def shrink(values):
    level = 0.25
    return jnp.where(
        values > level, values - level, jnp.where(values < -level, values + level, 0.0 * values)
    )


def block_product(left, weight):
    return jnp.einsum("qmbc,bcd->qmbd", left, weight, preferred_element_type=jnp.float32)


def general(patches, norm_gain, w_first, w_second, depth_kernel):
    n_row = lax.axis_size("row")
    n_col = lax.axis_size("col")
    rows_dev, cols_dev, chans = patches.shape
    patch_grid_height = rows_dev * n_row
    grid_w = cols_dev * n_col
    half = grid_w // 2
    blocks = w_first.shape[1]
    width = w_first.shape[2]
    width_factors = 1.0 / math.sqrt(grid_w)
    height_factors = 1.0 / math.sqrt(patch_grid_height)
    xf = patches.astype(jnp.float32)
    mean = jnp.mean(xf, axis=-1, keepdims=True)
    var = jnp.mean((xf - mean) ** 2, axis=-1, keepdims=True)
    normed = ((xf - mean) * lax.rsqrt(var + 1e-05) * norm_gain).astype(jnp.bfloat16)
    padded = with_halo(normed, (("row", 0), ("col", 1)), 1)
    conv = jnp.zeros((rows_dev, cols_dev, chans), jnp.float32)
    for i in range(3):
        for j in range(3):
            conv = conv + padded[i : i + rows_dev, j : j + cols_dev] * depth_kernel[i, j]
    strips = lax.all_to_all(normed, "col", split_axis=0, concat_axis=1, tiled=True)
    cos_w, sin_w = phase_table(
        jnp.arange(grid_w, dtype=jnp.int32), jnp.arange(half, dtype=jnp.int32), grid_w
    )
    forward_w = jnp.concatenate([cos_w, -sin_w], axis=1)
    spectrum_values = jnp.einsum(
        "hwc,wk->hkc", strips, forward_w, preferred_element_type=jnp.float32
    )
    spectrum_values = (spectrum_values * width_factors).astype(jnp.bfloat16)
    wre = spectrum_values[:, :half]
    wim = spectrum_values[:, half:]
    positions = jnp.arange(patch_grid_height, dtype=jnp.int32)
    across_re, across_im = (
        lax.all_to_all(wre, "col", split_axis=1, concat_axis=0, tiled=True),
        lax.all_to_all(wim, "col", split_axis=1, concat_axis=0, tiled=True),
    )
    full_re, full_im = (
        lax.all_to_all(across_re, "row", split_axis=1, concat_axis=0, tiled=True),
        lax.all_to_all(across_im, "row", split_axis=1, concat_axis=0, tiled=True),
    )
    cos_h, sin_h = phase_table(positions, positions, patch_grid_height)
    big_table = jnp.concatenate(
        [jnp.concatenate([cos_h, sin_h], axis=1), jnp.concatenate([-sin_h, cos_h], axis=1)], axis=0
    )
    stacked = jnp.concatenate([full_re, full_im], axis=0)
    spectrum = jnp.einsum("qp,pmc->qmc", big_table, stacked, preferred_element_type=jnp.float32)
    spectrum = (spectrum * height_factors).astype(jnp.bfloat16)
    modes = spectrum.shape[1]
    zre = spectrum[:patch_grid_height].reshape(patch_grid_height, modes, blocks, width)
    zim = spectrum[patch_grid_height:].reshape(patch_grid_height, modes, blocks, width)
    hre = jnp.tanh(block_product(zre, w_first[0]) - block_product(zim, w_first[1])).astype(
        jnp.bfloat16
    )
    him = jnp.tanh(block_product(zre, w_first[1]) + block_product(zim, w_first[0])).astype(
        jnp.bfloat16
    )
    spectrum_real = shrink(
        block_product(hre, w_second[0]) - block_product(him, w_second[1])
    ).astype(jnp.bfloat16)
    spectrum_imaginary = shrink(
        block_product(hre, w_second[1]) + block_product(him, w_second[0])
    ).astype(jnp.bfloat16)
    filtered = jnp.concatenate(
        [
            spectrum_real.reshape(patch_grid_height, modes, chans),
            spectrum_imaginary.reshape(patch_grid_height, modes, chans),
        ],
        axis=0,
    )
    inverse_transform = jnp.einsum(
        "qp,qmc->pmc", big_table, filtered, preferred_element_type=jnp.float32
    )
    inverse_transform = (inverse_transform * height_factors).astype(jnp.bfloat16)
    value_real = inverse_transform[:patch_grid_height]
    value_imaginary = inverse_transform[patch_grid_height:]
    part_re, part_im = (
        lax.all_to_all(value_real, "row", split_axis=0, concat_axis=1, tiled=True),
        lax.all_to_all(value_imaginary, "row", split_axis=0, concat_axis=1, tiled=True),
    )
    line_re, line_im = (
        lax.all_to_all(part_re, "col", split_axis=0, concat_axis=1, tiled=True),
        lax.all_to_all(part_im, "col", split_axis=0, concat_axis=1, tiled=True),
    )
    filter_coefficient = jnp.where(jnp.arange(half) == 0, 1.0, 2.0).astype(jnp.float32)
    inverse_w = jnp.concatenate(
        [
            (cos_w.astype(jnp.float32) * filter_coefficient).T,
            -(sin_w.astype(jnp.float32) * filter_coefficient).T,
        ],
        axis=0,
    ).astype(jnp.bfloat16)
    lines = jnp.concatenate([line_re, line_im], axis=1)
    spectral = jnp.einsum("hkc,kw->hwc", lines, inverse_w, preferred_element_type=jnp.float32)
    spectral = (spectral * width_factors).astype(jnp.bfloat16)
    home = lax.all_to_all(spectral, "col", split_axis=1, concat_axis=0, tiled=True)
    return (xf + home.astype(jnp.float32) + conv).astype(jnp.bfloat16)


LANES = 128
PAIR = 64
TILE = 16
SLOTS = 8
TURN = 32
COL_CHUNKS = 4
KGROUPS = 4
BATCH = 2


def row_order(n_row, rows_dev):
    pairs = rows_dev // 2
    zc = rows_dev // SLOTS
    per = pairs // zc
    order = []
    for z in range(zc):
        for s in range(n_row):
            for slot in range(SLOTS):
                order.append(s * rows_dev + (slot // per) * pairs + z * per + slot % per)
    return np.array(order)


def exact_scale(length):
    scale = 1.0 / math.sqrt(length)
    return (scale, 1.0) if math.frexp(scale)[0] == 0.5 else (1.0, scale)


def host_tables(grid_h, grid_w, n_row, rows_dev):
    half = grid_w // 2

    def table(a, b, n):
        phase = (np.outer(a, b) % n).astype(np.float32) * np.float32(2.0 * math.pi / n)
        bf16 = ml_dtypes.bfloat16
        cos, sin = (np.cos(phase).astype(bf16), np.sin(phase).astype(bf16))
        return cos.astype(np.float32), sin.astype(np.float32)

    cos_w, sin_w = table(np.arange(half), np.arange(grid_w), grid_w)
    weight = np.where(np.arange(half) == 0, 1.0, 2.0).astype(np.float32)[:, None]
    forward = np.concatenate([cos_w, -sin_w], axis=0)
    inverse = np.concatenate([cos_w * weight, -sin_w * weight], axis=0).T
    order = row_order(n_row, rows_dev)
    cos_h, sin_h = table(order, order, grid_h)
    swap = np.zeros((TURN, SLOTS, SLOTS, TURN), np.float32)
    for a in range(TURN):
        for b in range(SLOTS):
            swap[a, b, b, a] = 1.0
    swap = swap.reshape(TURN * SLOTS, TURN * SLOTS)
    cast = lambda v: v.astype(ml_dtypes.bfloat16)
    fold_w, fold_h = exact_scale(grid_w)[0], exact_scale(grid_h)[0]
    return (
        cast(forward * fold_w),
        cast(inverse * fold_w),
        cast(np.concatenate([cos_h, sin_h], axis=0) * fold_h),
        cast(np.stack([swap, swap.T])),
    )


def half_turn(x):
    parts = [pltpu.roll(part, PAIR, 1) for part in lane_groups(x)]
    return parts[0] if len(parts) == 1 else jnp.concatenate(parts, axis=1)


def lane_groups(x):
    return [x[:, i : i + LANES] for i in range(0, x.shape[1], LANES)]


def low_lanes(shape):
    return lax.broadcasted_iota(jnp.int32, shape, len(shape) - 1) % LANES < PAIR


def scaled(x, factor):
    return x if factor == 1.0 else x * factor


def swap_halves(a, b):
    low = low_lanes(a.shape)
    return jnp.where(low, a, half_turn(b)), jnp.where(low, half_turn(a), b)


def mixing_kernel(
    n_row,
    n_col,
    scale_w,
    scale_h,
    patches_hbm,
    gain_hbm,
    w_first_hbm,
    w_second_hbm,
    depth_hbm,
    forward_hbm,
    inverse_hbm,
    height_hbm,
    swap_hbm,
    out_hbm,
    patches,
    gain,
    w_first,
    w_second,
    depth,
    forward_ref,
    inverse_ref,
    height_ref,
    swap_ref,
    send1,
    recv1,
    turned,
    send2,
    recv2,
    send3,
    recv3,
    send4,
    recv4,
    conv,
    rim_send,
    rim_recv,
    rim,
    s1,
    r1,
    s2,
    r2,
    s3,
    r3,
    s4,
    r4,
    sh,
    rh,
    fetch_sem,
    patch_sem,
    out_sem,
):
    f32, bf16 = jnp.float32, jnp.bfloat16
    row, col = lax.axis_index("row"), lax.axis_index("col")
    rows_dev, cols_dev, chans = patches.shape
    pairs = rows_dev // 2
    per_col = pairs // COL_CHUNKS
    zc = COL_CHUNKS
    grid_w = cols_dev * n_col
    half = grid_w // 2
    kl = half // n_row
    per_k = kl // 2 // KGROUPS
    turns = [pl.ds(q * TURN, TURN) for q in range(half // TURN)]
    owners = [pl.ds(q * TURN // kl, TURN // kl) for q in range(half // TURN)]
    groups = chans // LANES

    def col_peer(d):
        return lax.rem(col + d, n_col)

    def row_peer(d):
        bits, peer, weight = d, 0, 1
        while weight < n_row:
            own = lax.rem(row // weight, 2)
            peer = peer + weight * (1 - own if bits % 2 else own)
            bits, weight = bits // 2, 2 * weight
        return peer

    near = list(range(1, n_row // 2))
    row_order_of = []
    for d in range(n_row // 2, n_row):
        row_order_of.append(d)
        if near:
            row_order_of.append(near.pop(0))

    def to_col(d):
        return {"col": col_peer(d)}

    def to_row(d):
        return {"row": row_peer(d)}

    def dot(a, b):
        return jnp.dot(a, b, preferred_element_type=f32)

    barrier = pltpu.get_barrier_semaphore()
    for d in range(1, n_col):
        pl.semaphore_signal(barrier, inc=1, device_id=to_col(d), device_id_type=pl.DeviceIdType.MESH)
    for d in range(1, n_row):
        pl.semaphore_signal(barrier, inc=1, device_id=to_row(d), device_id_type=pl.DeviceIdType.MESH)

    def chunk_rows(ch, side):
        return pl.ds(side * pairs + ch * per_col, per_col)

    def fetch_patches(ch, side):
        rows = chunk_rows(ch, side)
        return pltpu.make_async_copy(patches_hbm.at[rows], patches.at[rows], patch_sem.at[ch, side])

    def leave(ch, side):
        rows = chunk_rows(ch, side)
        return pltpu.make_async_copy(patches.at[rows], out_hbm.at[rows], out_sem.at[ch, side])

    operands = (
        (gain_hbm, gain),
        (forward_hbm, forward_ref),
        (swap_hbm, swap_ref),
        (w_first_hbm, w_first),
        (w_second_hbm, w_second),
        (depth_hbm, depth),
        (height_hbm, height_ref),
        (inverse_hbm, inverse_ref),
    )
    fetches = [
        pltpu.make_async_copy(src, dst, fetch_sem.at[i]) for i, (src, dst) in enumerate(operands)
    ]
    for side in range(2):
        fetch_patches(0, side).start()
    fetches[0].start()
    for ch in range(1, COL_CHUNKS):
        for side in range(2):
            fetch_patches(ch, side).start()
    for fetch in fetches[1:]:
        fetch.start()
    fetches[0].wait()

    def copy1(ch, d):
        return pltpu.make_async_remote_copy(
            src_ref=send1.at[ch, col_peer(d)],
            dst_ref=recv1.at[ch, col],
            send_sem=s1.at[ch, d - 1],
            recv_sem=r1.at[ch, d - 1],
            device_id=to_col(d),
            device_id_type=pl.DeviceIdType.MESH,
        )

    def part_of(g, in_parts):
        return pl.ds(g * per_k, per_k) if in_parts else pl.ds(0, kl // 2)

    parts2 = [KGROUPS if z == zc - 1 else 1 for z in range(zc)]
    parts3 = [KGROUPS if z == 0 else 1 for z in range(zc)]

    def copy2(z, g, d):
        ks = part_of(g, z == zc - 1)
        return pltpu.make_async_remote_copy(
            src_ref=send2.at[z, row_peer(d), ks],
            dst_ref=recv2.at[z, row, ks],
            send_sem=s2.at[z, g, d - 1],
            recv_sem=r2.at[z, g, d - 1],
            device_id=to_row(d),
            device_id_type=pl.DeviceIdType.MESH,
        )

    def copy3(z, g, d):
        ks = part_of(g, z == 0)
        return pltpu.make_async_remote_copy(
            src_ref=send3.at[z, row_peer(d), ks],
            dst_ref=recv3.at[z, row, ks],
            send_sem=s3.at[z, g, d - 1],
            recv_sem=r3.at[z, g, d - 1],
            device_id=to_row(d),
            device_id_type=pl.DeviceIdType.MESH,
        )

    def copy4(ch, d):
        return pltpu.make_async_remote_copy(
            src_ref=send4.at[ch, col_peer(d)],
            dst_ref=recv4.at[ch, col],
            send_sem=s4.at[ch, d - 1],
            recv_sem=r4.at[ch, d - 1],
            device_id=to_col(d),
            device_id_type=pl.DeviceIdType.MESH,
        )

    def copy_rim(side):
        return pltpu.make_async_remote_copy(
            src_ref=rim_send.at[side],
            dst_ref=rim_recv.at[side],
            send_sem=sh.at[side],
            recv_sem=rh.at[side],
            device_id={"row": lax.rem(row + (1 if side == 0 else n_row - 1), n_row)},
            device_id_type=pl.DeviceIdType.MESH,
        )

    def normed_row(h):
        x = patches[h].astype(f32)
        mean = jnp.mean(x, axis=-1, keepdims=True)
        centred = x - mean
        var = jnp.mean(centred * centred, axis=-1, keepdims=True)
        return centred * lax.rsqrt(var + 1e-05) * gain[...]

    def norm_chunk(ch):
        for side in range(2):
            fetch_patches(ch, side).wait()

        def norm_pair(i, carry):
            hp = ch * per_col + i
            lower, upper = normed_row(hp), normed_row(hp + pairs)
            for j in range(groups):
                lanes = slice(j * LANES, (j + 1) * LANES)
                even, odd = swap_halves(lower[:, lanes], upper[:, lanes])
                send1[ch, 2 * j, i] = even.astype(bf16)
                send1[ch, 2 * j + 1, i] = odd.astype(bf16)
            return carry

        lax.fori_loop(0, per_col, norm_pair, 0, unroll=2)
        if ch == 0:
            pl.semaphore_wait(barrier, n_col + n_row - 2)
        for d in range(1, n_col):
            copy1(ch, d).start()
        recv1[ch, col] = send1[ch, col]

    norm_chunk(0)
    norm_chunk(1)

    def line(ch, i):
        return recv1[ch, :, i].reshape(grid_w, LANES)

    for fetch in fetches[1:]:
        fetch.wait()
    for z in range(zc):
        for d in range(1, n_col):
            copy1(z, d).wait_recv()
        x = jnp.concatenate([line(z, i) for i in range(per_col)], axis=1)
        y = scaled(dot(forward_ref[...], x), scale_w)
        lower, upper = swap_halves(y[:half], y[half:])
        for i in range(per_col):
            turned[i] = lane_groups(lower)[i].astype(bf16)
            turned[per_col + i] = lane_groups(upper)[i].astype(bf16)
        tiles = [turned[:, ks, :].reshape(TURN * SLOTS, LANES) for ks in turns]
        swapped = dot(swap_ref[0], jnp.concatenate(tiles, axis=1)).astype(bf16)
        for own, part in zip(owners, lane_groups(swapped)):
            send2[z, own] = part.reshape(TURN // kl, kl // 2, TILE, LANES)
        for g in range(parts2[z]):
            for d in row_order_of:
                copy2(z, g, d).start()
        recv2[z, row] = send2[z, row]
        if z + 2 < COL_CHUNKS:
            norm_chunk(z + 2)

    first = line(0, 0).astype(f32)
    final = line(COL_CHUNKS - 1, per_col - 1).astype(f32)
    rim_send[0] = swap_halves(final[:half], final[half:])[1].astype(bf16)
    rim_send[1] = swap_halves(first[:half], first[half:])[0].astype(bf16)
    for side in range(2):
        copy_rim(side).start()

    def complex_weight(ref):
        re, im = ref[0, col].astype(f32), ref[1, col].astype(f32)
        one = jnp.concatenate(
            [jnp.concatenate([re, im], axis=1), jnp.concatenate([-im, re], axis=1)], axis=0
        ).astype(bf16)
        none = jnp.zeros_like(one)
        return jnp.concatenate(
            [jnp.concatenate([one, none], axis=1), jnp.concatenate([none, one], axis=1)], axis=0
        )

    weight_a, weight_b = complex_weight(w_first), complex_weight(w_second)

    lane_group = pl.multiple_of((col // 2) * LANES, LANES)
    taps = []
    for i in range(3):
        own = depth[i, :, pl.ds(lane_group, LANES)]
        low = low_lanes(own.shape)
        other = half_turn(own)
        taps.append(
            jnp.where((col % 2) == 0, jnp.where(low, own, other), jnp.where(low, other, own))
        )
    def conv_pair(hp, above, here, below):
        total = None
        for j in range(3):
            part = None
            for i, rows in enumerate((above, here, below)):
                term = rows * taps[i][j : j + 1]
                part = term if part is None else part + term
            if j == 0:
                part = pltpu.roll(part, 1, 0)
            if j == 2:
                part = pltpu.roll(part, grid_w - 1, 0)
            total = part if total is None else total + part
        conv[hp] = total

    def at(hp):
        return line(hp // per_col, hp % per_col).astype(f32)

    def conv_inner(hp, carry):
        conv_pair(hp, at(hp - 1), at(hp), at(hp + 1))
        return carry

    lax.fori_loop(1, pairs - 1, conv_inner, 0)

    grid_h = rows_dev * n_row
    sign = jnp.where(low_lanes((1, 2 * LANES)), 1.0, -1.0)

    def height(u):
        both = dot(height_ref[...], u)
        return both[:grid_h], half_turn(both[grid_h:]) * sign

    def filter_pair(k):
        tile = recv2[:, :, k].astype(f32).reshape(zc * n_row, TILE, LANES)
        u = jnp.concatenate(
            [
                tile[:, i : i + SLOTS].reshape(grid_h, LANES).astype(bf16)
                for i in range(0, TILE, SLOTS)
            ],
            axis=1,
        )
        a, b = height(u)
        zed = scaled(a + b, scale_h).astype(bf16)
        hidden = jnp.tanh(dot(zed, weight_a)).astype(bf16)
        s = dot(hidden, weight_b)
        s = (s - jnp.clip(s, -0.25, 0.25)).astype(bf16)
        a, b = height(s)
        v = lane_groups(scaled(a - b, scale_h))
        v = jnp.concatenate([part.reshape(zc * n_row, SLOTS, LANES) for part in v], axis=1)
        send3[:, :, k] = v.astype(bf16).reshape(zc, n_row, TILE, LANES)

    def filter_modes(step, carry):
        for i in range(BATCH):
            filter_pair(step * BATCH + i)
        return carry

    for g in range(KGROUPS):
        for z in range(zc):
            for d in range(1, n_row) if g < parts2[z] else ():
                copy2(z, g, d).wait_recv()
        lax.fori_loop(g * per_k // BATCH, (g + 1) * per_k // BATCH, filter_modes, 0)
        for d in row_order_of:
            copy3(0, g, d).start()
    for z in range(1, zc):
        for d in row_order_of:
            copy3(z, 0, d).start()
    for z in range(zc):
        recv3[z, row] = send3[z, row]

    for side in range(2):
        copy_rim(side).wait_recv()
    before = rim_recv[0].astype(f32)
    after = rim_recv[1].astype(f32)
    before = jnp.concatenate([before, half_turn(before)], axis=0)
    after = jnp.concatenate([half_turn(after), after], axis=0)
    low = low_lanes(before.shape)
    rim[0] = jnp.where(low, before, half_turn(at(pairs - 1))).astype(bf16)
    rim[1] = jnp.where(low, half_turn(at(0)), after).astype(bf16)

    conv_pair(0, rim[0].astype(f32), at(0), at(1))
    conv_pair(pairs - 1, at(pairs - 2), at(pairs - 1), rim[1].astype(f32))

    def finish(ch):
        for d in range(1, n_col):
            copy4(ch, d).wait_recv()

        def finish_pair(i, carry):
            hp = ch * per_col + i
            for j in range(groups):
                lanes = slice(j * LANES, (j + 1) * LANES)
                lower, upper = swap_halves(
                    recv4[ch, 2 * j, i].astype(f32), recv4[ch, 2 * j + 1, i].astype(f32)
                )
                patches[hp, :, lanes] = (patches[hp, :, lanes].astype(f32) + lower).astype(bf16)
                patches[hp + pairs, :, lanes] = (
                    patches[hp + pairs, :, lanes].astype(f32) + upper
                ).astype(bf16)
            return carry

        lax.fori_loop(0, per_col, finish_pair, 0, unroll=2)
        for side in range(2):
            leave(ch, side).start()

    for z in range(zc):
        for g in range(parts3[z]):
            for d in range(1, n_row):
                copy3(z, g, d).wait_recv()

        tiles = [recv3[z, own].reshape(TURN * SLOTS, LANES) for own in owners]
        swapped = dot(swap_ref[1], jnp.concatenate(tiles, axis=1)).astype(bf16)
        for ks, part in zip(turns, lane_groups(swapped)):
            turned[:, ks, :] = part.reshape(SLOTS, TURN, LANES)
        columns = []
        for i in range(per_col):
            re, im = swap_halves(turned[i].astype(f32), turned[per_col + i].astype(f32))
            columns.append(jnp.concatenate([re.astype(bf16), im.astype(bf16)], axis=0))
        cells = scaled(dot(inverse_ref[...], jnp.concatenate(columns, axis=1)), scale_w)
        for i, part in enumerate(lane_groups(cells)):
            part = (part + conv[z * per_col + i]).astype(bf16)
            send4[z, :, i] = part.reshape(n_col, cols_dev, LANES)
        for d in range(1, n_col):
            copy4(z, d).start()
        recv4[z, col] = send4[z, col]
        if z > 0:
            finish(z - 1)

    finish(zc - 1)

    for ch in range(COL_CHUNKS):
        for d in range(1, n_col):
            copy1(ch, d).wait_send()
            copy4(ch, d).wait_send()
    for z in range(zc):
        for d in range(1, n_row):
            for g in range(parts2[z]):
                copy2(z, g, d).wait_send()
            for g in range(parts3[z]):
                copy3(z, g, d).wait_send()
    for side in range(2):
        copy_rim(side).wait_send()
    for ch in range(COL_CHUNKS):
        for side in range(2):
            leave(ch, side).wait()


def fused(patches, norm_gain, w_first, w_second, depth_kernel):
    n_row = lax.axis_size("row")
    n_col = lax.axis_size("col")
    rows_dev, cols_dev, chans = patches.shape
    grid_h, grid_w = rows_dev * n_row, cols_dev * n_col
    pairs, zc = rows_dev // 2, COL_CHUNKS
    per_col = pairs // COL_CHUNKS
    half = grid_w // 2
    kl = half // n_row
    tables = host_tables(grid_h, grid_w, n_row, rows_dev)
    bf16, f32 = jnp.bfloat16, jnp.float32
    anywhere = pl.BlockSpec(memory_space=pltpu.HBM)
    col_buffer = pltpu.VMEM((COL_CHUNKS, n_col, per_col, cols_dev, LANES), bf16)
    row_buffer = pltpu.VMEM((zc, n_row, kl // 2, TILE, LANES), bf16)
    col_sems = pltpu.SemaphoreType.DMA((COL_CHUNKS, n_col - 1))
    row_sems = pltpu.SemaphoreType.DMA((zc, KGROUPS, n_row - 1))
    rim_sems = pltpu.SemaphoreType.DMA((2,))
    operands = (
        patches,
        norm_gain.reshape(1, chans),
        w_first,
        w_second,
        depth_kernel,
        *[jnp.asarray(t) for t in tables],
    )
    return pl.pallas_call(
        functools.partial(
            mixing_kernel, n_row, n_col, exact_scale(grid_w)[1], exact_scale(grid_h)[1]
        ),
        out_shape=jax.ShapeDtypeStruct(patches.shape, bf16),
        in_specs=[anywhere] * 9,
        out_specs=anywhere,
        scratch_shapes=[
            *[pltpu.VMEM(v.shape, v.dtype) for v in operands],
            col_buffer,
            col_buffer,
            pltpu.VMEM((SLOTS, half, LANES), bf16),
            row_buffer,
            row_buffer,
            row_buffer,
            row_buffer,
            col_buffer,
            col_buffer,
            pltpu.VMEM((pairs, grid_w, LANES), f32),
            pltpu.VMEM((2, half, LANES), bf16),
            pltpu.VMEM((2, half, LANES), bf16),
            pltpu.VMEM((2, grid_w, LANES), bf16),
            col_sems,
            col_sems,
            row_sems,
            row_sems,
            row_sems,
            row_sems,
            col_sems,
            col_sems,
            rim_sems,
            rim_sems,
            pltpu.SemaphoreType.DMA((8,)),
            pltpu.SemaphoreType.DMA((COL_CHUNKS, 2)),
            pltpu.SemaphoreType.DMA((COL_CHUNKS, 2)),
        ],
        compiler_params=pltpu.CompilerParams(
            collective_id=0, has_side_effects=True, vmem_limit_bytes=62 * 1024 * 1024
        ),
        cost_estimate=pl.CostEstimate(flops=2_000_000_000, bytes_accessed=3_000_000, transcendentals=600_000),
    )(*operands)


def fits(patches, w_first):
    n_row, n_col = lax.axis_size("row"), lax.axis_size("col")
    rows_dev, cols_dev, chans = patches.shape
    blocks, width = w_first.shape[1:3]
    half = cols_dev * n_col // 2
    return (
        blocks == n_col
        and width == PAIR
        and chans % LANES == 0
        and rows_dev == COL_CHUNKS * SLOTS
        and cols_dev % TILE == 0
        and half == n_row * TILE
        and half % TURN == 0
        and n_row & (n_row - 1) == 0
    )


def local(patches, norm_gain, w_first, w_second, depth_kernel):
    plan = fused if fits(patches, w_first) else general
    return plan(patches, norm_gain, w_first, w_second, depth_kernel)


def solution(mesh):
    return jax.shard_map(
        local,
        mesh=mesh,
        in_specs=(P("row", "col", None), P(), P(), P(), P()),
        out_specs=P("row", "col", None),
        check_vma=False,
    )
```

```python
import functools
import math

import jax
import jax.numpy as jnp
import ml_dtypes
import numpy as np
from jax import lax
from jax.experimental import pallas as pl
from jax.experimental.pallas import tpu as pltpu
from jax.sharding import PartitionSpec as P


def with_halo(shard, sides, width):
    for axis, dim in sides:
        devices, length = (lax.axis_size(axis), shard.shape[dim])
        up = [(i, (i + 1) % devices) for i in range(devices)]
        down = [(j, i) for i, j in up]
        last = lax.slice_in_dim(shard, length - width, length, axis=dim)
        leading = lax.slice_in_dim(shard, 0, width, axis=dim)
        before = lax.ppermute(last, axis, up)
        after = lax.ppermute(leading, axis, down)
        shard = jnp.concatenate([before, shard, after], axis=dim)
    return shard


def phase_table(first_idx, second_idx, length):
    product = first_idx[:, None] * second_idx[None, :] % length
    phase = product.astype(jnp.float32) * (2.0 * math.pi / length)
    return (jnp.cos(phase).astype(jnp.bfloat16), jnp.sin(phase).astype(jnp.bfloat16))


def shrink(values):
    level = 0.25
    return jnp.where(
        values > level, values - level, jnp.where(values < -level, values + level, 0.0 * values)
    )


def block_product(left, weight):
    return jnp.einsum("qmbc,bcd->qmbd", left, weight, preferred_element_type=jnp.float32)


def general(patches, norm_gain, w_first, w_second, depth_kernel):
    n_row = lax.axis_size("row")
    n_col = lax.axis_size("col")
    rows_dev, cols_dev, chans = patches.shape
    patch_grid_height = rows_dev * n_row
    grid_w = cols_dev * n_col
    half = grid_w // 2
    blocks = w_first.shape[1]
    width = w_first.shape[2]
    width_factors = 1.0 / math.sqrt(grid_w)
    height_factors = 1.0 / math.sqrt(patch_grid_height)
    xf = patches.astype(jnp.float32)
    mean = jnp.mean(xf, axis=-1, keepdims=True)
    var = jnp.mean((xf - mean) ** 2, axis=-1, keepdims=True)
    normed = ((xf - mean) * lax.rsqrt(var + 1e-05) * norm_gain).astype(jnp.bfloat16)
    padded = with_halo(normed, (("row", 0), ("col", 1)), 1)
    conv = jnp.zeros((rows_dev, cols_dev, chans), jnp.float32)
    for i in range(3):
        for j in range(3):
            conv = conv + padded[i : i + rows_dev, j : j + cols_dev] * depth_kernel[i, j]
    strips = lax.all_to_all(normed, "col", split_axis=0, concat_axis=1, tiled=True)
    cos_w, sin_w = phase_table(
        jnp.arange(grid_w, dtype=jnp.int32), jnp.arange(half, dtype=jnp.int32), grid_w
    )
    forward_w = jnp.concatenate([cos_w, -sin_w], axis=1)
    spectrum_values = jnp.einsum(
        "hwc,wk->hkc", strips, forward_w, preferred_element_type=jnp.float32
    )
    spectrum_values = (spectrum_values * width_factors).astype(jnp.bfloat16)
    wre = spectrum_values[:, :half]
    wim = spectrum_values[:, half:]
    positions = jnp.arange(patch_grid_height, dtype=jnp.int32)
    across_re, across_im = (
        lax.all_to_all(wre, "col", split_axis=1, concat_axis=0, tiled=True),
        lax.all_to_all(wim, "col", split_axis=1, concat_axis=0, tiled=True),
    )
    full_re, full_im = (
        lax.all_to_all(across_re, "row", split_axis=1, concat_axis=0, tiled=True),
        lax.all_to_all(across_im, "row", split_axis=1, concat_axis=0, tiled=True),
    )
    cos_h, sin_h = phase_table(positions, positions, patch_grid_height)
    big_table = jnp.concatenate(
        [jnp.concatenate([cos_h, sin_h], axis=1), jnp.concatenate([-sin_h, cos_h], axis=1)], axis=0
    )
    stacked = jnp.concatenate([full_re, full_im], axis=0)
    spectrum = jnp.einsum("qp,pmc->qmc", big_table, stacked, preferred_element_type=jnp.float32)
    spectrum = (spectrum * height_factors).astype(jnp.bfloat16)
    modes = spectrum.shape[1]
    zre = spectrum[:patch_grid_height].reshape(patch_grid_height, modes, blocks, width)
    zim = spectrum[patch_grid_height:].reshape(patch_grid_height, modes, blocks, width)
    hre = jnp.tanh(block_product(zre, w_first[0]) - block_product(zim, w_first[1])).astype(
        jnp.bfloat16
    )
    him = jnp.tanh(block_product(zre, w_first[1]) + block_product(zim, w_first[0])).astype(
        jnp.bfloat16
    )
    spectrum_real = shrink(
        block_product(hre, w_second[0]) - block_product(him, w_second[1])
    ).astype(jnp.bfloat16)
    spectrum_imaginary = shrink(
        block_product(hre, w_second[1]) + block_product(him, w_second[0])
    ).astype(jnp.bfloat16)
    filtered = jnp.concatenate(
        [
            spectrum_real.reshape(patch_grid_height, modes, chans),
            spectrum_imaginary.reshape(patch_grid_height, modes, chans),
        ],
        axis=0,
    )
    inverse_transform = jnp.einsum(
        "qp,qmc->pmc", big_table, filtered, preferred_element_type=jnp.float32
    )
    inverse_transform = (inverse_transform * height_factors).astype(jnp.bfloat16)
    value_real = inverse_transform[:patch_grid_height]
    value_imaginary = inverse_transform[patch_grid_height:]
    part_re, part_im = (
        lax.all_to_all(value_real, "row", split_axis=0, concat_axis=1, tiled=True),
        lax.all_to_all(value_imaginary, "row", split_axis=0, concat_axis=1, tiled=True),
    )
    line_re, line_im = (
        lax.all_to_all(part_re, "col", split_axis=0, concat_axis=1, tiled=True),
        lax.all_to_all(part_im, "col", split_axis=0, concat_axis=1, tiled=True),
    )
    filter_coefficient = jnp.where(jnp.arange(half) == 0, 1.0, 2.0).astype(jnp.float32)
    inverse_w = jnp.concatenate(
        [
            (cos_w.astype(jnp.float32) * filter_coefficient).T,
            -(sin_w.astype(jnp.float32) * filter_coefficient).T,
        ],
        axis=0,
    ).astype(jnp.bfloat16)
    lines = jnp.concatenate([line_re, line_im], axis=1)
    spectral = jnp.einsum("hkc,kw->hwc", lines, inverse_w, preferred_element_type=jnp.float32)
    spectral = (spectral * width_factors).astype(jnp.bfloat16)
    home = lax.all_to_all(spectral, "col", split_axis=1, concat_axis=0, tiled=True)
    return (xf + home.astype(jnp.float32) + conv).astype(jnp.bfloat16)


LANES = 128
PAIR = 64
TILE = 16
SLOTS = 8
TURN = 32
COL_CHUNKS = 4
KGROUPS = 4
BATCH = 2


def row_order(n_row, rows_dev):
    pairs = rows_dev // 2
    zc = rows_dev // SLOTS
    per = pairs // zc
    order = []
    for z in range(zc):
        for s in range(n_row):
            for slot in range(SLOTS):
                order.append(s * rows_dev + (slot // per) * pairs + z * per + slot % per)
    return np.array(order)


def exact_scale(length):
    scale = 1.0 / math.sqrt(length)
    return (scale, 1.0) if math.frexp(scale)[0] == 0.5 else (1.0, scale)


def host_tables(grid_h, grid_w, n_row, rows_dev):
    half = grid_w // 2

    def table(a, b, n):
        phase = (np.outer(a, b) % n).astype(np.float32) * np.float32(2.0 * math.pi / n)
        bf16 = ml_dtypes.bfloat16
        cos, sin = (np.cos(phase).astype(bf16), np.sin(phase).astype(bf16))
        return cos.astype(np.float32), sin.astype(np.float32)

    cos_w, sin_w = table(np.arange(half), np.arange(grid_w), grid_w)
    weight = np.where(np.arange(half) == 0, 1.0, 2.0).astype(np.float32)[:, None]
    forward = np.concatenate([cos_w, -sin_w], axis=0)
    inverse = np.concatenate([cos_w * weight, -sin_w * weight], axis=0).T
    order = row_order(n_row, rows_dev)
    cos_h, sin_h = table(order, order, grid_h)
    swap = np.zeros((TURN, SLOTS, SLOTS, TURN), np.float32)
    for a in range(TURN):
        for b in range(SLOTS):
            swap[a, b, b, a] = 1.0
    swap = swap.reshape(TURN * SLOTS, TURN * SLOTS)
    cast = lambda v: v.astype(ml_dtypes.bfloat16)
    fold_w, fold_h = exact_scale(grid_w)[0], exact_scale(grid_h)[0]
    return (
        cast(forward * fold_w),
        cast(inverse * fold_w),
        cast(np.concatenate([cos_h, sin_h], axis=0) * fold_h),
        cast(np.stack([swap, swap.T])),
    )


def half_turn(x):
    parts = [pltpu.roll(part, PAIR, 1) for part in lane_groups(x)]
    return parts[0] if len(parts) == 1 else jnp.concatenate(parts, axis=1)


def lane_groups(x):
    return [x[:, i : i + LANES] for i in range(0, x.shape[1], LANES)]


def low_lanes(shape):
    return lax.broadcasted_iota(jnp.int32, shape, len(shape) - 1) % LANES < PAIR


def scaled(x, factor):
    return x if factor == 1.0 else x * factor


def swap_halves(a, b):
    low = low_lanes(a.shape)
    return jnp.where(low, a, half_turn(b)), jnp.where(low, half_turn(a), b)


def mixing_kernel(
    n_row,
    n_col,
    scale_w,
    scale_h,
    patches_hbm,
    gain_hbm,
    w_first_hbm,
    w_second_hbm,
    depth_hbm,
    forward_hbm,
    inverse_hbm,
    height_hbm,
    swap_hbm,
    out_hbm,
    patches,
    gain,
    w_first,
    w_second,
    depth,
    forward_ref,
    inverse_ref,
    height_ref,
    swap_ref,
    send1,
    recv1,
    turned,
    send2,
    recv2,
    send3,
    recv3,
    send4,
    recv4,
    conv,
    rim_send,
    rim_recv,
    rim,
    s1,
    r1,
    s2,
    r2,
    s3,
    r3,
    s4,
    r4,
    sh,
    rh,
    fetch_sem,
    patch_sem,
    out_sem,
):
    f32, bf16 = jnp.float32, jnp.bfloat16
    row, col = lax.axis_index("row"), lax.axis_index("col")
    rows_dev, cols_dev, chans = patches.shape
    pairs = rows_dev // 2
    per_col = pairs // COL_CHUNKS
    zc = COL_CHUNKS
    grid_w = cols_dev * n_col
    half = grid_w // 2
    kl = half // n_row
    per_k = kl // 2 // KGROUPS
    turns = [pl.ds(q * TURN, TURN) for q in range(half // TURN)]
    owners = [pl.ds(q * TURN // kl, TURN // kl) for q in range(half // TURN)]
    groups = chans // LANES

    def col_peer(d):
        return lax.rem(col + d, n_col)

    def row_peer(d):
        bits, peer, weight = d, 0, 1
        while weight < n_row:
            own = lax.rem(row // weight, 2)
            peer = peer + weight * (1 - own if bits % 2 else own)
            bits, weight = bits // 2, 2 * weight
        return peer

    near = list(range(1, n_row // 2))
    row_order_of = []
    for d in range(n_row // 2, n_row):
        row_order_of.append(d)
        if near:
            row_order_of.append(near.pop(0))

    def to_col(d):
        return {"col": col_peer(d)}

    def to_row(d):
        return {"row": row_peer(d)}

    def dot(a, b):
        return jnp.dot(a, b, preferred_element_type=f32)

    barrier = pltpu.get_barrier_semaphore()
    for d in range(1, n_col):
        pl.semaphore_signal(barrier, inc=1, device_id=to_col(d), device_id_type=pl.DeviceIdType.MESH)
    for d in range(1, n_row):
        pl.semaphore_signal(barrier, inc=1, device_id=to_row(d), device_id_type=pl.DeviceIdType.MESH)

    def chunk_rows(ch, side):
        return pl.ds(side * pairs + ch * per_col, per_col)

    def fetch_patches(ch, side):
        rows = chunk_rows(ch, side)
        return pltpu.make_async_copy(patches_hbm.at[rows], patches.at[rows], patch_sem.at[ch, side])

    def leave(ch):
        return pltpu.make_async_copy(recv4.at[ch], out_hbm.at[ch], out_sem.at[ch])

    operands = (
        (gain_hbm, gain),
        (forward_hbm, forward_ref),
        (swap_hbm, swap_ref),
        (w_first_hbm, w_first),
        (w_second_hbm, w_second),
        (depth_hbm, depth),
        (height_hbm, height_ref),
        (inverse_hbm, inverse_ref),
    )
    fetches = [
        pltpu.make_async_copy(src, dst, fetch_sem.at[i]) for i, (src, dst) in enumerate(operands)
    ]
    for side in range(2):
        fetch_patches(0, side).start()
    fetches[0].start()
    for ch in range(1, COL_CHUNKS):
        for side in range(2):
            fetch_patches(ch, side).start()
    for fetch in fetches[1:]:
        fetch.start()
    fetches[0].wait()

    def copy1(ch, d):
        return pltpu.make_async_remote_copy(
            src_ref=send1.at[ch, col_peer(d)],
            dst_ref=recv1.at[ch, col],
            send_sem=s1.at[ch, d - 1],
            recv_sem=r1.at[ch, d - 1],
            device_id=to_col(d),
            device_id_type=pl.DeviceIdType.MESH,
        )

    def part_of(g, in_parts):
        return pl.ds(g * per_k, per_k) if in_parts else pl.ds(0, kl // 2)

    parts2 = [KGROUPS if z == zc - 1 else 1 for z in range(zc)]
    parts3 = [KGROUPS if z == 0 else 1 for z in range(zc)]

    def copy2(z, g, d):
        ks = part_of(g, z == zc - 1)
        return pltpu.make_async_remote_copy(
            src_ref=send2.at[z, row_peer(d), ks],
            dst_ref=recv2.at[z, row, ks],
            send_sem=s2.at[z, g, d - 1],
            recv_sem=r2.at[z, g, d - 1],
            device_id=to_row(d),
            device_id_type=pl.DeviceIdType.MESH,
        )

    def copy3(z, g, d):
        ks = part_of(g, z == 0)
        return pltpu.make_async_remote_copy(
            src_ref=send3.at[z, row_peer(d), ks],
            dst_ref=recv3.at[z, row, ks],
            send_sem=s3.at[z, g, d - 1],
            recv_sem=r3.at[z, g, d - 1],
            device_id=to_row(d),
            device_id_type=pl.DeviceIdType.MESH,
        )

    def copy4(ch, d):
        return pltpu.make_async_remote_copy(
            src_ref=send4.at[ch, col_peer(d)],
            dst_ref=recv4.at[ch, col],
            send_sem=s4.at[ch, d - 1],
            recv_sem=r4.at[ch, d - 1],
            device_id=to_col(d),
            device_id_type=pl.DeviceIdType.MESH,
        )

    def copy_rim(side):
        return pltpu.make_async_remote_copy(
            src_ref=rim_send.at[side],
            dst_ref=rim_recv.at[side],
            send_sem=sh.at[side],
            recv_sem=rh.at[side],
            device_id={"row": lax.rem(row + (1 if side == 0 else n_row - 1), n_row)},
            device_id_type=pl.DeviceIdType.MESH,
        )

    def normed_row(h):
        x = patches[h].astype(f32)
        mean = jnp.mean(x, axis=-1, keepdims=True)
        centred = x - mean
        var = jnp.mean(centred * centred, axis=-1, keepdims=True)
        return centred * lax.rsqrt(var + 1e-05) * gain[...]

    def norm_chunk(ch):
        for side in range(2):
            fetch_patches(ch, side).wait()

        def norm_pair(i, carry):
            hp = ch * per_col + i
            lower, upper = normed_row(hp), normed_row(hp + pairs)
            for j in range(groups):
                lanes = slice(j * LANES, (j + 1) * LANES)
                even, odd = swap_halves(lower[:, lanes], upper[:, lanes])
                send1[ch, 2 * j, i] = even.astype(bf16)
                send1[ch, 2 * j + 1, i] = odd.astype(bf16)
            return carry

        lax.fori_loop(0, per_col, norm_pair, 0, unroll=2)
        if ch == 0:
            pl.semaphore_wait(barrier, n_col + n_row - 2)
        for d in range(1, n_col):
            copy1(ch, d).start()
        recv1[ch, col] = send1[ch, col]

    norm_chunk(0)
    norm_chunk(1)

    def line(ch, i):
        return recv1[ch, :, i].reshape(grid_w, LANES)

    for fetch in fetches[1:]:
        fetch.wait()
    for z in range(zc):
        for d in range(1, n_col):
            copy1(z, d).wait_recv()
        x = jnp.concatenate([line(z, i) for i in range(per_col)], axis=1)
        y = scaled(dot(forward_ref[...], x), scale_w)
        lower, upper = swap_halves(y[:half], y[half:])
        for i in range(per_col):
            turned[i] = lane_groups(lower)[i].astype(bf16)
            turned[per_col + i] = lane_groups(upper)[i].astype(bf16)
        tiles = [turned[:, ks, :].reshape(TURN * SLOTS, LANES) for ks in turns]
        swapped = dot(swap_ref[0], jnp.concatenate(tiles, axis=1)).astype(bf16)
        for own, part in zip(owners, lane_groups(swapped)):
            send2[z, own] = part.reshape(TURN // kl, kl // 2, TILE, LANES)
        for g in range(parts2[z]):
            for d in row_order_of:
                copy2(z, g, d).start()
        recv2[z, row] = send2[z, row]
        if z + 2 < COL_CHUNKS:
            norm_chunk(z + 2)

    first = line(0, 0).astype(f32)
    final = line(COL_CHUNKS - 1, per_col - 1).astype(f32)
    rim_send[0] = swap_halves(final[:half], final[half:])[1].astype(bf16)
    rim_send[1] = swap_halves(first[:half], first[half:])[0].astype(bf16)
    for side in range(2):
        copy_rim(side).start()

    def complex_weight(ref):
        re, im = ref[0, col].astype(f32), ref[1, col].astype(f32)
        one = jnp.concatenate(
            [jnp.concatenate([re, im], axis=1), jnp.concatenate([-im, re], axis=1)], axis=0
        ).astype(bf16)
        none = jnp.zeros_like(one)
        return jnp.concatenate(
            [jnp.concatenate([one, none], axis=1), jnp.concatenate([none, one], axis=1)], axis=0
        )

    weight_a, weight_b = complex_weight(w_first), complex_weight(w_second)

    lane_group = pl.multiple_of((col // 2) * LANES, LANES)
    taps = []
    for i in range(3):
        own = depth[i, :, pl.ds(lane_group, LANES)]
        low = low_lanes(own.shape)
        other = half_turn(own)
        taps.append(
            jnp.where((col % 2) == 0, jnp.where(low, own, other), jnp.where(low, other, own))
        )
    def conv_pair(hp, above, here, below):
        total = None
        for j in range(3):
            part = None
            for i, rows in enumerate((above, here, below)):
                term = rows * taps[i][j : j + 1]
                part = term if part is None else part + term
            if j == 0:
                part = pltpu.roll(part, 1, 0)
            if j == 2:
                part = pltpu.roll(part, grid_w - 1, 0)
            total = part if total is None else total + part
        conv[hp] = total

    def at(hp):
        return line(hp // per_col, hp % per_col).astype(f32)

    def conv_inner(hp, carry):
        conv_pair(hp, at(hp - 1), at(hp), at(hp + 1))
        return carry

    lax.fori_loop(1, pairs - 1, conv_inner, 0)

    grid_h = rows_dev * n_row
    sign = jnp.where(low_lanes((1, 2 * LANES)), 1.0, -1.0)

    def height(u):
        both = dot(height_ref[...], u)
        return both[:grid_h], half_turn(both[grid_h:]) * sign

    def filter_pair(k):
        tile = recv2[:, :, k].astype(f32).reshape(zc * n_row, TILE, LANES)
        u = jnp.concatenate(
            [
                tile[:, i : i + SLOTS].reshape(grid_h, LANES).astype(bf16)
                for i in range(0, TILE, SLOTS)
            ],
            axis=1,
        )
        a, b = height(u)
        zed = scaled(a + b, scale_h).astype(bf16)
        hidden = jnp.tanh(dot(zed, weight_a)).astype(bf16)
        s = dot(hidden, weight_b)
        s = (s - jnp.clip(s, -0.25, 0.25)).astype(bf16)
        a, b = height(s)
        v = lane_groups(scaled(a - b, scale_h))
        v = jnp.concatenate([part.reshape(zc * n_row, SLOTS, LANES) for part in v], axis=1)
        send3[:, :, k] = v.astype(bf16).reshape(zc, n_row, TILE, LANES)

    def filter_modes(step, carry):
        for i in range(BATCH):
            filter_pair(step * BATCH + i)
        return carry

    for g in range(KGROUPS):
        for z in range(zc):
            for d in range(1, n_row) if g < parts2[z] else ():
                copy2(z, g, d).wait_recv()
        lax.fori_loop(g * per_k // BATCH, (g + 1) * per_k // BATCH, filter_modes, 0)
        for d in row_order_of:
            copy3(0, g, d).start()
    for z in range(1, zc):
        for d in row_order_of:
            copy3(z, 0, d).start()
    for z in range(zc):
        recv3[z, row] = send3[z, row]

    for side in range(2):
        copy_rim(side).wait_recv()
    before = rim_recv[0].astype(f32)
    after = rim_recv[1].astype(f32)
    before = jnp.concatenate([before, half_turn(before)], axis=0)
    after = jnp.concatenate([half_turn(after), after], axis=0)
    low = low_lanes(before.shape)
    rim[0] = jnp.where(low, before, half_turn(at(pairs - 1))).astype(bf16)
    rim[1] = jnp.where(low, half_turn(at(0)), after).astype(bf16)

    conv_pair(0, rim[0].astype(f32), at(0), at(1))
    conv_pair(pairs - 1, at(pairs - 2), at(pairs - 1), rim[1].astype(f32))

    def finish(ch):
        for d in range(1, n_col):
            copy4(ch, d).wait_recv()

        leave(ch).start()

    for z in range(zc):
        for g in range(parts3[z]):
            for d in range(1, n_row):
                copy3(z, g, d).wait_recv()

        tiles = [recv3[z, own].reshape(TURN * SLOTS, LANES) for own in owners]
        swapped = dot(swap_ref[1], jnp.concatenate(tiles, axis=1)).astype(bf16)
        for ks, part in zip(turns, lane_groups(swapped)):
            turned[:, ks, :] = part.reshape(SLOTS, TURN, LANES)
        columns = []
        for i in range(per_col):
            re, im = swap_halves(turned[i].astype(f32), turned[per_col + i].astype(f32))
            columns.append(jnp.concatenate([re.astype(bf16), im.astype(bf16)], axis=0))
        cells = scaled(dot(inverse_ref[...], jnp.concatenate(columns, axis=1)), scale_w)
        for i, part in enumerate(lane_groups(cells)):
            part = (part + conv[z * per_col + i]).astype(bf16)
            send4[z, :, i] = part.reshape(n_col, cols_dev, LANES)
        for d in range(1, n_col):
            copy4(z, d).start()
        recv4[z, col] = send4[z, col]
        if z > 0:
            finish(z - 1)

    finish(zc - 1)

    for ch in range(COL_CHUNKS):
        for d in range(1, n_col):
            copy1(ch, d).wait_send()
            copy4(ch, d).wait_send()
    for z in range(zc):
        for d in range(1, n_row):
            for g in range(parts2[z]):
                copy2(z, g, d).wait_send()
            for g in range(parts3[z]):
                copy3(z, g, d).wait_send()
    for side in range(2):
        copy_rim(side).wait_send()
    for ch in range(COL_CHUNKS):
        leave(ch).wait()


def finish_kernel(patches, branches, out):
    f32 = jnp.float32
    for i in range(patches.shape[1]):
        for j in range(patches.shape[3] // LANES):
            lanes = slice(j * LANES, (j + 1) * LANES)
            both = swap_halves(
                branches[0, 2 * j, i].astype(f32), branches[0, 2 * j + 1, i].astype(f32)
            )
            for side in range(2):
                total = patches[side, i, :, lanes].astype(f32) + both[side]
                out[side, i, :, lanes] = total.astype(out.dtype)


def fused(patches, norm_gain, w_first, w_second, depth_kernel):
    n_row = lax.axis_size("row")
    n_col = lax.axis_size("col")
    rows_dev, cols_dev, chans = patches.shape
    grid_h, grid_w = rows_dev * n_row, cols_dev * n_col
    pairs, zc = rows_dev // 2, COL_CHUNKS
    per_col = pairs // COL_CHUNKS
    half = grid_w // 2
    kl = half // n_row
    tables = host_tables(grid_h, grid_w, n_row, rows_dev)
    bf16, f32 = jnp.bfloat16, jnp.float32
    anywhere = pl.BlockSpec(memory_space=pltpu.HBM)
    col_buffer = pltpu.VMEM((COL_CHUNKS, n_col, per_col, cols_dev, LANES), bf16)
    row_buffer = pltpu.VMEM((zc, n_row, kl // 2, TILE, LANES), bf16)
    col_sems = pltpu.SemaphoreType.DMA((COL_CHUNKS, n_col - 1))
    row_sems = pltpu.SemaphoreType.DMA((zc, KGROUPS, n_row - 1))
    rim_sems = pltpu.SemaphoreType.DMA((2,))
    operands = (
        patches,
        norm_gain.reshape(1, chans),
        w_first,
        w_second,
        depth_kernel,
        *[jnp.asarray(t) for t in tables],
    )
    branches = pl.pallas_call(
        functools.partial(
            mixing_kernel, n_row, n_col, exact_scale(grid_w)[1], exact_scale(grid_h)[1]
        ),
        out_shape=jax.ShapeDtypeStruct((COL_CHUNKS, n_col, per_col, cols_dev, LANES), bf16),
        in_specs=[anywhere] * 9,
        out_specs=anywhere,
        scratch_shapes=[
            *[pltpu.VMEM(v.shape, v.dtype) for v in operands],
            col_buffer,
            col_buffer,
            pltpu.VMEM((SLOTS, half, LANES), bf16),
            row_buffer,
            row_buffer,
            row_buffer,
            row_buffer,
            col_buffer,
            col_buffer,
            pltpu.VMEM((pairs, grid_w, LANES), f32),
            pltpu.VMEM((2, half, LANES), bf16),
            pltpu.VMEM((2, half, LANES), bf16),
            pltpu.VMEM((2, grid_w, LANES), bf16),
            col_sems,
            col_sems,
            row_sems,
            row_sems,
            row_sems,
            row_sems,
            col_sems,
            col_sems,
            rim_sems,
            rim_sems,
            pltpu.SemaphoreType.DMA((8,)),
            pltpu.SemaphoreType.DMA((COL_CHUNKS, 2)),
            pltpu.SemaphoreType.DMA((COL_CHUNKS,)),
        ],
        compiler_params=pltpu.CompilerParams(
            collective_id=0, has_side_effects=True, vmem_limit_bytes=62 * 1024 * 1024
        ),
        cost_estimate=pl.CostEstimate(flops=2_000_000_000, bytes_accessed=3_000_000, transcendentals=600_000),
    )(*operands)
    cells = pl.BlockSpec((2, per_col, cols_dev, chans), lambda ch: (0, ch, 0, 0))
    sides = (2, pairs, cols_dev, chans)
    mixed = pl.pallas_call(
        finish_kernel,
        grid=(COL_CHUNKS,),
        out_shape=jax.ShapeDtypeStruct(sides, bf16),
        in_specs=[
            cells,
            pl.BlockSpec((1, n_col, per_col, cols_dev, LANES), lambda ch: (ch, 0, 0, 0, 0)),
        ],
        out_specs=cells,
    )(patches.reshape(sides), branches)
    return mixed.reshape(patches.shape)


def fits(patches, w_first):
    n_row, n_col = lax.axis_size("row"), lax.axis_size("col")
    rows_dev, cols_dev, chans = patches.shape
    blocks, width = w_first.shape[1:3]
    half = cols_dev * n_col // 2
    return (
        blocks == n_col
        and width == PAIR
        and chans % LANES == 0
        and rows_dev == COL_CHUNKS * SLOTS
        and cols_dev % TILE == 0
        and half == n_row * TILE
        and half % TURN == 0
        and n_row & (n_row - 1) == 0
    )


def local(patches, norm_gain, w_first, w_second, depth_kernel):
    plan = fused if fits(patches, w_first) else general
    return plan(patches, norm_gain, w_first, w_second, depth_kernel)


def solution(mesh):
    return jax.shard_map(
        local,
        mesh=mesh,
        in_specs=(P("row", "col", None), P(), P(), P(), P()),
        out_specs=P("row", "col", None),
        check_vma=False,
    )
```

```python
import functools
import math

import jax
import jax.numpy as jnp
import ml_dtypes
import numpy as np
from jax import lax
from jax.experimental import pallas as pl
from jax.experimental.pallas import tpu as pltpu
from jax.sharding import PartitionSpec as P


def with_halo(shard, sides, width):
    for axis, dim in sides:
        devices, length = (lax.axis_size(axis), shard.shape[dim])
        up = [(i, (i + 1) % devices) for i in range(devices)]
        down = [(j, i) for i, j in up]
        last = lax.slice_in_dim(shard, length - width, length, axis=dim)
        leading = lax.slice_in_dim(shard, 0, width, axis=dim)
        before = lax.ppermute(last, axis, up)
        after = lax.ppermute(leading, axis, down)
        shard = jnp.concatenate([before, shard, after], axis=dim)
    return shard


def phase_table(first_idx, second_idx, length):
    product = first_idx[:, None] * second_idx[None, :] % length
    phase = product.astype(jnp.float32) * (2.0 * math.pi / length)
    return (jnp.cos(phase).astype(jnp.bfloat16), jnp.sin(phase).astype(jnp.bfloat16))


def shrink(values):
    level = 0.25
    return jnp.where(
        values > level, values - level, jnp.where(values < -level, values + level, 0.0 * values)
    )


def block_product(left, weight):
    return jnp.einsum("qmbc,bcd->qmbd", left, weight, preferred_element_type=jnp.float32)


def general(patches, norm_gain, w_first, w_second, depth_kernel):
    n_row = lax.axis_size("row")
    n_col = lax.axis_size("col")
    rows_dev, cols_dev, chans = patches.shape
    patch_grid_height = rows_dev * n_row
    grid_w = cols_dev * n_col
    half = grid_w // 2
    blocks = w_first.shape[1]
    width = w_first.shape[2]
    width_factors = 1.0 / math.sqrt(grid_w)
    height_factors = 1.0 / math.sqrt(patch_grid_height)
    xf = patches.astype(jnp.float32)
    mean = jnp.mean(xf, axis=-1, keepdims=True)
    var = jnp.mean((xf - mean) ** 2, axis=-1, keepdims=True)
    normed = ((xf - mean) * lax.rsqrt(var + 1e-05) * norm_gain).astype(jnp.bfloat16)
    padded = with_halo(normed, (("row", 0), ("col", 1)), 1)
    conv = jnp.zeros((rows_dev, cols_dev, chans), jnp.float32)
    for i in range(3):
        for j in range(3):
            conv = conv + padded[i : i + rows_dev, j : j + cols_dev] * depth_kernel[i, j]
    strips = lax.all_to_all(normed, "col", split_axis=0, concat_axis=1, tiled=True)
    cos_w, sin_w = phase_table(
        jnp.arange(grid_w, dtype=jnp.int32), jnp.arange(half, dtype=jnp.int32), grid_w
    )
    forward_w = jnp.concatenate([cos_w, -sin_w], axis=1)
    spectrum_values = jnp.einsum(
        "hwc,wk->hkc", strips, forward_w, preferred_element_type=jnp.float32
    )
    spectrum_values = (spectrum_values * width_factors).astype(jnp.bfloat16)
    wre = spectrum_values[:, :half]
    wim = spectrum_values[:, half:]
    positions = jnp.arange(patch_grid_height, dtype=jnp.int32)
    across_re, across_im = (
        lax.all_to_all(wre, "col", split_axis=1, concat_axis=0, tiled=True),
        lax.all_to_all(wim, "col", split_axis=1, concat_axis=0, tiled=True),
    )
    full_re, full_im = (
        lax.all_to_all(across_re, "row", split_axis=1, concat_axis=0, tiled=True),
        lax.all_to_all(across_im, "row", split_axis=1, concat_axis=0, tiled=True),
    )
    cos_h, sin_h = phase_table(positions, positions, patch_grid_height)
    big_table = jnp.concatenate(
        [jnp.concatenate([cos_h, sin_h], axis=1), jnp.concatenate([-sin_h, cos_h], axis=1)], axis=0
    )
    stacked = jnp.concatenate([full_re, full_im], axis=0)
    spectrum = jnp.einsum("qp,pmc->qmc", big_table, stacked, preferred_element_type=jnp.float32)
    spectrum = (spectrum * height_factors).astype(jnp.bfloat16)
    modes = spectrum.shape[1]
    zre = spectrum[:patch_grid_height].reshape(patch_grid_height, modes, blocks, width)
    zim = spectrum[patch_grid_height:].reshape(patch_grid_height, modes, blocks, width)
    hre = jnp.tanh(block_product(zre, w_first[0]) - block_product(zim, w_first[1])).astype(
        jnp.bfloat16
    )
    him = jnp.tanh(block_product(zre, w_first[1]) + block_product(zim, w_first[0])).astype(
        jnp.bfloat16
    )
    spectrum_real = shrink(
        block_product(hre, w_second[0]) - block_product(him, w_second[1])
    ).astype(jnp.bfloat16)
    spectrum_imaginary = shrink(
        block_product(hre, w_second[1]) + block_product(him, w_second[0])
    ).astype(jnp.bfloat16)
    filtered = jnp.concatenate(
        [
            spectrum_real.reshape(patch_grid_height, modes, chans),
            spectrum_imaginary.reshape(patch_grid_height, modes, chans),
        ],
        axis=0,
    )
    inverse_transform = jnp.einsum(
        "qp,qmc->pmc", big_table, filtered, preferred_element_type=jnp.float32
    )
    inverse_transform = (inverse_transform * height_factors).astype(jnp.bfloat16)
    value_real = inverse_transform[:patch_grid_height]
    value_imaginary = inverse_transform[patch_grid_height:]
    part_re, part_im = (
        lax.all_to_all(value_real, "row", split_axis=0, concat_axis=1, tiled=True),
        lax.all_to_all(value_imaginary, "row", split_axis=0, concat_axis=1, tiled=True),
    )
    line_re, line_im = (
        lax.all_to_all(part_re, "col", split_axis=0, concat_axis=1, tiled=True),
        lax.all_to_all(part_im, "col", split_axis=0, concat_axis=1, tiled=True),
    )
    filter_coefficient = jnp.where(jnp.arange(half) == 0, 1.0, 2.0).astype(jnp.float32)
    inverse_w = jnp.concatenate(
        [
            (cos_w.astype(jnp.float32) * filter_coefficient).T,
            -(sin_w.astype(jnp.float32) * filter_coefficient).T,
        ],
        axis=0,
    ).astype(jnp.bfloat16)
    lines = jnp.concatenate([line_re, line_im], axis=1)
    spectral = jnp.einsum("hkc,kw->hwc", lines, inverse_w, preferred_element_type=jnp.float32)
    spectral = (spectral * width_factors).astype(jnp.bfloat16)
    home = lax.all_to_all(spectral, "col", split_axis=1, concat_axis=0, tiled=True)
    return (xf + home.astype(jnp.float32) + conv).astype(jnp.bfloat16)


LANES = 128
PAIR = 64
TILE = 16
SLOTS = 8
TURN = 32
COL_CHUNKS = 4
KGROUPS = 4
BATCH = 2


def row_order(n_row, rows_dev):
    pairs = rows_dev // 2
    zc = rows_dev // SLOTS
    per = pairs // zc
    order = []
    for z in range(zc):
        for s in range(n_row):
            for slot in range(SLOTS):
                order.append(s * rows_dev + (slot // per) * pairs + z * per + slot % per)
    return np.array(order)


def exact_scale(length):
    scale = 1.0 / math.sqrt(length)
    return (scale, 1.0) if math.frexp(scale)[0] == 0.5 else (1.0, scale)


def host_tables(grid_h, grid_w, n_row, rows_dev):
    half = grid_w // 2

    def table(a, b, n):
        phase = (np.outer(a, b) % n).astype(np.float32) * np.float32(2.0 * math.pi / n)
        bf16 = ml_dtypes.bfloat16
        cos, sin = (np.cos(phase).astype(bf16), np.sin(phase).astype(bf16))
        return cos.astype(np.float32), sin.astype(np.float32)

    cos_w, sin_w = table(np.arange(half), np.arange(grid_w), grid_w)
    weight = np.where(np.arange(half) == 0, 1.0, 2.0).astype(np.float32)[:, None]
    forward = np.concatenate([cos_w, -sin_w], axis=0)
    inverse = np.concatenate([cos_w * weight, -sin_w * weight], axis=0).T
    order = row_order(n_row, rows_dev)
    cos_h, sin_h = table(order, order, grid_h)
    swap = np.zeros((TURN, SLOTS, SLOTS, TURN), np.float32)
    for a in range(TURN):
        for b in range(SLOTS):
            swap[a, b, b, a] = 1.0
    swap = swap.reshape(TURN * SLOTS, TURN * SLOTS)
    cast = lambda v: v.astype(ml_dtypes.bfloat16)
    fold_w, fold_h = exact_scale(grid_w)[0], exact_scale(grid_h)[0]
    return (
        cast(forward * fold_w),
        cast(inverse * fold_w),
        cast(np.concatenate([cos_h, sin_h], axis=0) * fold_h),
        cast(np.stack([swap, swap.T])),
    )


def half_turn(x):
    parts = [pltpu.roll(part, PAIR, 1) for part in lane_groups(x)]
    return parts[0] if len(parts) == 1 else jnp.concatenate(parts, axis=1)


def lane_groups(x):
    return [x[:, i : i + LANES] for i in range(0, x.shape[1], LANES)]


def low_lanes(shape):
    return lax.broadcasted_iota(jnp.int32, shape, len(shape) - 1) % LANES < PAIR


def scaled(x, factor):
    return x if factor == 1.0 else x * factor


def swap_halves(a, b):
    low = low_lanes(a.shape)
    return jnp.where(low, a, half_turn(b)), jnp.where(low, half_turn(a), b)


def mixing_kernel(
    n_row,
    n_col,
    scale_w,
    scale_h,
    patches_hbm,
    gain_hbm,
    w_first_hbm,
    w_second_hbm,
    depth_hbm,
    forward_hbm,
    inverse_hbm,
    height_hbm,
    swap_hbm,
    out_hbm,
    patches,
    gain,
    w_first,
    w_second,
    depth,
    forward_ref,
    inverse_ref,
    height_ref,
    swap_ref,
    send1,
    recv1,
    turned,
    send2,
    recv2,
    send3,
    recv3,
    send4,
    recv4,
    conv,
    rim_send,
    rim_recv,
    rim,
    s1,
    r1,
    s2,
    r2,
    s3,
    r3,
    s4,
    r4,
    sh,
    rh,
    fetch_sem,
    patch_sem,
    out_sem,
):
    f32, bf16 = jnp.float32, jnp.bfloat16
    row, col = lax.axis_index("row"), lax.axis_index("col")
    rows_dev, cols_dev, chans = patches.shape
    pairs = rows_dev // 2
    per_col = pairs // COL_CHUNKS
    zc = COL_CHUNKS
    grid_w = cols_dev * n_col
    half = grid_w // 2
    kl = half // n_row
    per_k = kl // 2 // KGROUPS
    turns = [pl.ds(q * TURN, TURN) for q in range(half // TURN)]
    owners = [pl.ds(q * TURN // kl, TURN // kl) for q in range(half // TURN)]
    groups = chans // LANES

    def col_peer(d):
        return lax.rem(col + d, n_col)

    def row_peer(d):
        bits, peer, weight = d, 0, 1
        while weight < n_row:
            own = lax.rem(row // weight, 2)
            peer = peer + weight * (1 - own if bits % 2 else own)
            bits, weight = bits // 2, 2 * weight
        return peer

    row_order_of = list(range(n_row - 1, 0, -1))

    def to_col(d):
        return {"col": col_peer(d)}

    def to_row(d):
        return {"row": row_peer(d)}

    def dot(a, b):
        return jnp.dot(a, b, preferred_element_type=f32)

    barrier = pltpu.get_barrier_semaphore()
    for d in range(1, n_col):
        pl.semaphore_signal(barrier, inc=1, device_id=to_col(d), device_id_type=pl.DeviceIdType.MESH)
    for d in range(1, n_row):
        pl.semaphore_signal(barrier, inc=1, device_id=to_row(d), device_id_type=pl.DeviceIdType.MESH)

    def chunk_rows(ch, side):
        return pl.ds(side * pairs + ch * per_col, per_col)

    def fetch_patches(ch, side):
        rows = chunk_rows(ch, side)
        return pltpu.make_async_copy(patches_hbm.at[rows], patches.at[rows], patch_sem.at[ch, side])

    def leave(ch, side):
        rows = chunk_rows(ch, side)
        return pltpu.make_async_copy(patches.at[rows], out_hbm.at[rows], out_sem.at[ch, side])

    operands = (
        (gain_hbm, gain),
        (forward_hbm, forward_ref),
        (swap_hbm, swap_ref),
        (w_first_hbm, w_first),
        (w_second_hbm, w_second),
        (depth_hbm, depth),
        (height_hbm, height_ref),
        (inverse_hbm, inverse_ref),
    )
    fetches = [
        pltpu.make_async_copy(src, dst, fetch_sem.at[i]) for i, (src, dst) in enumerate(operands)
    ]
    for side in range(2):
        fetch_patches(0, side).start()
    fetches[0].start()
    for ch in range(1, COL_CHUNKS):
        for side in range(2):
            fetch_patches(ch, side).start()
    for fetch in fetches[1:]:
        fetch.start()
    fetches[0].wait()

    def copy1(ch, d):
        return pltpu.make_async_remote_copy(
            src_ref=send1.at[ch, col_peer(d)],
            dst_ref=recv1.at[ch, col],
            send_sem=s1.at[ch, d - 1],
            recv_sem=r1.at[ch, d - 1],
            device_id=to_col(d),
            device_id_type=pl.DeviceIdType.MESH,
        )

    def part_of(g, in_parts):
        return pl.ds(g * per_k, per_k) if in_parts else pl.ds(0, kl // 2)

    parts2 = [KGROUPS if z == zc - 1 else 1 for z in range(zc)]
    parts3 = [KGROUPS if z == 0 else 1 for z in range(zc)]

    def copy2(z, g, d):
        ks = part_of(g, z == zc - 1)
        return pltpu.make_async_remote_copy(
            src_ref=send2.at[z, row_peer(d), ks],
            dst_ref=recv2.at[z, row, ks],
            send_sem=s2.at[z, g, d - 1],
            recv_sem=r2.at[z, g, d - 1],
            device_id=to_row(d),
            device_id_type=pl.DeviceIdType.MESH,
        )

    def copy3(z, g, d):
        ks = part_of(g, z == 0)
        return pltpu.make_async_remote_copy(
            src_ref=send3.at[z, row_peer(d), ks],
            dst_ref=recv3.at[z, row, ks],
            send_sem=s3.at[z, g, d - 1],
            recv_sem=r3.at[z, g, d - 1],
            device_id=to_row(d),
            device_id_type=pl.DeviceIdType.MESH,
        )

    def copy4(ch, d):
        return pltpu.make_async_remote_copy(
            src_ref=send4.at[ch, col_peer(d)],
            dst_ref=recv4.at[ch, col],
            send_sem=s4.at[ch, d - 1],
            recv_sem=r4.at[ch, d - 1],
            device_id=to_col(d),
            device_id_type=pl.DeviceIdType.MESH,
        )

    def copy_rim(side):
        return pltpu.make_async_remote_copy(
            src_ref=rim_send.at[side],
            dst_ref=rim_recv.at[side],
            send_sem=sh.at[side],
            recv_sem=rh.at[side],
            device_id={"row": lax.rem(row + (1 if side == 0 else n_row - 1), n_row)},
            device_id_type=pl.DeviceIdType.MESH,
        )

    def normed_row(h):
        x = patches[h].astype(f32)
        mean = jnp.mean(x, axis=-1, keepdims=True)
        centred = x - mean
        var = jnp.mean(centred * centred, axis=-1, keepdims=True)
        return centred * lax.rsqrt(var + 1e-05) * gain[...]

    def norm_chunk(ch):
        for side in range(2):
            fetch_patches(ch, side).wait()

        def norm_pair(i, carry):
            hp = ch * per_col + i
            lower, upper = normed_row(hp), normed_row(hp + pairs)
            for j in range(groups):
                lanes = slice(j * LANES, (j + 1) * LANES)
                even, odd = swap_halves(lower[:, lanes], upper[:, lanes])
                send1[ch, 2 * j, i] = even.astype(bf16)
                send1[ch, 2 * j + 1, i] = odd.astype(bf16)
            return carry

        lax.fori_loop(0, per_col, norm_pair, 0, unroll=2)
        if ch == 0:
            pl.semaphore_wait(barrier, n_col + n_row - 2)
        for d in range(1, n_col):
            copy1(ch, d).start()
        recv1[ch, col] = send1[ch, col]

    norm_chunk(0)
    norm_chunk(1)

    def line(ch, i):
        return recv1[ch, :, i].reshape(grid_w, LANES)

    for fetch in fetches[1:]:
        fetch.wait()
    for z in range(zc):
        for d in range(1, n_col):
            copy1(z, d).wait_recv()
        x = jnp.concatenate([line(z, i) for i in range(per_col)], axis=1)
        y = scaled(dot(forward_ref[...], x), scale_w)
        lower, upper = swap_halves(y[:half], y[half:])
        for i in range(per_col):
            turned[i] = lane_groups(lower)[i].astype(bf16)
            turned[per_col + i] = lane_groups(upper)[i].astype(bf16)
        tiles = [turned[:, ks, :].reshape(TURN * SLOTS, LANES) for ks in turns]
        swapped = dot(swap_ref[0], jnp.concatenate(tiles, axis=1)).astype(bf16)
        for own, part in zip(owners, lane_groups(swapped)):
            send2[z, own] = part.reshape(TURN // kl, kl // 2, TILE, LANES)
        for g in range(parts2[z]):
            for d in row_order_of:
                copy2(z, g, d).start()
        recv2[z, row] = send2[z, row]
        if z + 2 < COL_CHUNKS:
            norm_chunk(z + 2)

    first = line(0, 0).astype(f32)
    final = line(COL_CHUNKS - 1, per_col - 1).astype(f32)
    rim_send[0] = swap_halves(final[:half], final[half:])[1].astype(bf16)
    rim_send[1] = swap_halves(first[:half], first[half:])[0].astype(bf16)
    for side in range(2):
        copy_rim(side).start()

    def complex_weight(ref):
        re, im = ref[0, col].astype(f32), ref[1, col].astype(f32)
        one = jnp.concatenate(
            [jnp.concatenate([re, im], axis=1), jnp.concatenate([-im, re], axis=1)], axis=0
        ).astype(bf16)
        none = jnp.zeros_like(one)
        return jnp.concatenate(
            [jnp.concatenate([one, none], axis=1), jnp.concatenate([none, one], axis=1)], axis=0
        )

    weight_a, weight_b = complex_weight(w_first), complex_weight(w_second)

    lane_group = pl.multiple_of((col // 2) * LANES, LANES)
    taps = []
    for i in range(3):
        own = depth[i, :, pl.ds(lane_group, LANES)]
        low = low_lanes(own.shape)
        other = half_turn(own)
        taps.append(
            jnp.where((col % 2) == 0, jnp.where(low, own, other), jnp.where(low, other, own))
        )
    def conv_pair(hp, above, here, below):
        total = None
        for j in range(3):
            part = None
            for i, rows in enumerate((above, here, below)):
                term = rows * taps[i][j : j + 1]
                part = term if part is None else part + term
            if j == 0:
                part = pltpu.roll(part, 1, 0)
            if j == 2:
                part = pltpu.roll(part, grid_w - 1, 0)
            total = part if total is None else total + part
        conv[hp] = total

    def at(hp):
        return line(hp // per_col, hp % per_col).astype(f32)

    def conv_inner(hp, carry):
        conv_pair(hp, at(hp - 1), at(hp), at(hp + 1))
        return carry

    lax.fori_loop(1, pairs - 1, conv_inner, 0)

    grid_h = rows_dev * n_row
    sign = jnp.where(low_lanes((1, 2 * LANES)), 1.0, -1.0)

    def height(u):
        both = dot(height_ref[...], u)
        return both[:grid_h], half_turn(both[grid_h:]) * sign

    def filter_pair(k):
        tile = recv2[:, :, k].astype(f32).reshape(zc * n_row, TILE, LANES)
        u = jnp.concatenate(
            [
                tile[:, i : i + SLOTS].reshape(grid_h, LANES).astype(bf16)
                for i in range(0, TILE, SLOTS)
            ],
            axis=1,
        )
        a, b = height(u)
        zed = scaled(a + b, scale_h).astype(bf16)
        hidden = jnp.tanh(dot(zed, weight_a)).astype(bf16)
        s = dot(hidden, weight_b)
        s = (s - jnp.clip(s, -0.25, 0.25)).astype(bf16)
        a, b = height(s)
        v = lane_groups(scaled(a - b, scale_h))
        v = jnp.concatenate([part.reshape(zc * n_row, SLOTS, LANES) for part in v], axis=1)
        send3[:, :, k] = v.astype(bf16).reshape(zc, n_row, TILE, LANES)

    def filter_modes(step, carry):
        for i in range(BATCH):
            filter_pair(step * BATCH + i)
        return carry

    for g in range(KGROUPS):
        for z in range(zc):
            for d in range(1, n_row) if g < parts2[z] else ():
                copy2(z, g, d).wait_recv()
        lax.fori_loop(g * per_k // BATCH, (g + 1) * per_k // BATCH, filter_modes, 0)
        for d in row_order_of:
            copy3(0, g, d).start()
    for z in range(1, zc):
        for d in row_order_of:
            copy3(z, 0, d).start()
    for z in range(zc):
        recv3[z, row] = send3[z, row]

    for side in range(2):
        copy_rim(side).wait_recv()
    before = rim_recv[0].astype(f32)
    after = rim_recv[1].astype(f32)
    before = jnp.concatenate([before, half_turn(before)], axis=0)
    after = jnp.concatenate([half_turn(after), after], axis=0)
    low = low_lanes(before.shape)
    rim[0] = jnp.where(low, before, half_turn(at(pairs - 1))).astype(bf16)
    rim[1] = jnp.where(low, half_turn(at(0)), after).astype(bf16)

    conv_pair(0, rim[0].astype(f32), at(0), at(1))
    conv_pair(pairs - 1, at(pairs - 2), at(pairs - 1), rim[1].astype(f32))

    def finish(ch):
        for d in range(1, n_col):
            copy4(ch, d).wait_recv()

        def finish_pair(i, carry):
            hp = ch * per_col + i
            for j in range(groups):
                lanes = slice(j * LANES, (j + 1) * LANES)
                lower, upper = swap_halves(
                    recv4[ch, 2 * j, i].astype(f32), recv4[ch, 2 * j + 1, i].astype(f32)
                )
                patches[hp, :, lanes] = (patches[hp, :, lanes].astype(f32) + lower).astype(bf16)
                patches[hp + pairs, :, lanes] = (
                    patches[hp + pairs, :, lanes].astype(f32) + upper
                ).astype(bf16)
            return carry

        lax.fori_loop(0, per_col, finish_pair, 0, unroll=2)
        for side in range(2):
            leave(ch, side).start()

    for z in range(zc):
        for g in range(parts3[z]):
            for d in range(1, n_row):
                copy3(z, g, d).wait_recv()

        tiles = [recv3[z, own].reshape(TURN * SLOTS, LANES) for own in owners]
        swapped = dot(swap_ref[1], jnp.concatenate(tiles, axis=1)).astype(bf16)
        for ks, part in zip(turns, lane_groups(swapped)):
            turned[:, ks, :] = part.reshape(SLOTS, TURN, LANES)
        columns = []
        for i in range(per_col):
            re, im = swap_halves(turned[i].astype(f32), turned[per_col + i].astype(f32))
            columns.append(jnp.concatenate([re.astype(bf16), im.astype(bf16)], axis=0))
        cells = scaled(dot(inverse_ref[...], jnp.concatenate(columns, axis=1)), scale_w)
        for i, part in enumerate(lane_groups(cells)):
            part = (part + conv[z * per_col + i]).astype(bf16)
            send4[z, :, i] = part.reshape(n_col, cols_dev, LANES)
        for d in range(1, n_col):
            copy4(z, d).start()
        recv4[z, col] = send4[z, col]
        if z > 0:
            finish(z - 1)

    finish(zc - 1)

    for ch in range(COL_CHUNKS):
        for d in range(1, n_col):
            copy1(ch, d).wait_send()
            copy4(ch, d).wait_send()
    for z in range(zc):
        for d in range(1, n_row):
            for g in range(parts2[z]):
                copy2(z, g, d).wait_send()
            for g in range(parts3[z]):
                copy3(z, g, d).wait_send()
    for side in range(2):
        copy_rim(side).wait_send()
    for ch in range(COL_CHUNKS):
        for side in range(2):
            leave(ch, side).wait()


def fused(patches, norm_gain, w_first, w_second, depth_kernel):
    n_row = lax.axis_size("row")
    n_col = lax.axis_size("col")
    rows_dev, cols_dev, chans = patches.shape
    grid_h, grid_w = rows_dev * n_row, cols_dev * n_col
    pairs, zc = rows_dev // 2, COL_CHUNKS
    per_col = pairs // COL_CHUNKS
    half = grid_w // 2
    kl = half // n_row
    tables = host_tables(grid_h, grid_w, n_row, rows_dev)
    bf16, f32 = jnp.bfloat16, jnp.float32
    anywhere = pl.BlockSpec(memory_space=pltpu.HBM)
    col_buffer = pltpu.VMEM((COL_CHUNKS, n_col, per_col, cols_dev, LANES), bf16)
    row_buffer = pltpu.VMEM((zc, n_row, kl // 2, TILE, LANES), bf16)
    col_sems = pltpu.SemaphoreType.DMA((COL_CHUNKS, n_col - 1))
    row_sems = pltpu.SemaphoreType.DMA((zc, KGROUPS, n_row - 1))
    rim_sems = pltpu.SemaphoreType.DMA((2,))
    operands = (
        patches,
        norm_gain.reshape(1, chans),
        w_first,
        w_second,
        depth_kernel,
        *[jnp.asarray(t) for t in tables],
    )
    return pl.pallas_call(
        functools.partial(
            mixing_kernel, n_row, n_col, exact_scale(grid_w)[1], exact_scale(grid_h)[1]
        ),
        out_shape=jax.ShapeDtypeStruct(patches.shape, bf16),
        in_specs=[anywhere] * 9,
        out_specs=anywhere,
        scratch_shapes=[
            *[pltpu.VMEM(v.shape, v.dtype) for v in operands],
            col_buffer,
            col_buffer,
            pltpu.VMEM((SLOTS, half, LANES), bf16),
            row_buffer,
            row_buffer,
            row_buffer,
            row_buffer,
            col_buffer,
            col_buffer,
            pltpu.VMEM((pairs, grid_w, LANES), f32),
            pltpu.VMEM((2, half, LANES), bf16),
            pltpu.VMEM((2, half, LANES), bf16),
            pltpu.VMEM((2, grid_w, LANES), bf16),
            col_sems,
            col_sems,
            row_sems,
            row_sems,
            row_sems,
            row_sems,
            col_sems,
            col_sems,
            rim_sems,
            rim_sems,
            pltpu.SemaphoreType.DMA((8,)),
            pltpu.SemaphoreType.DMA((COL_CHUNKS, 2)),
            pltpu.SemaphoreType.DMA((COL_CHUNKS, 2)),
        ],
        compiler_params=pltpu.CompilerParams(
            collective_id=0, has_side_effects=True, vmem_limit_bytes=62 * 1024 * 1024
        ),
        cost_estimate=pl.CostEstimate(flops=2_000_000_000, bytes_accessed=3_000_000, transcendentals=600_000),
    )(*operands)


def fits(patches, w_first):
    n_row, n_col = lax.axis_size("row"), lax.axis_size("col")
    rows_dev, cols_dev, chans = patches.shape
    blocks, width = w_first.shape[1:3]
    half = cols_dev * n_col // 2
    return (
        blocks == n_col
        and width == PAIR
        and chans % LANES == 0
        and rows_dev == COL_CHUNKS * SLOTS
        and cols_dev % TILE == 0
        and half == n_row * TILE
        and half % TURN == 0
        and n_row & (n_row - 1) == 0
    )


def local(patches, norm_gain, w_first, w_second, depth_kernel):
    plan = fused if fits(patches, w_first) else general
    return plan(patches, norm_gain, w_first, w_second, depth_kernel)


def solution(mesh):
    return jax.shard_map(
        local,
        mesh=mesh,
        in_specs=(P("row", "col", None), P(), P(), P(), P()),
        out_specs=P("row", "col", None),
        check_vma=False,
    )
```
